32 devices in a mesh: gx: 4 (over y, x), gy: 2 (over core), gz: 4 (over z).
Axes of the slice: x: 2, y: 2, z: 4, core: 2. Of those that a mesh axis runs over, the one named last changes fastest.
Arguments:
- state: float32 [7, 4, 2, 32768], P(None, 'gx', 'gy', 'gz'), as said below
- tile_lists: int32 [4, 2, 256, 8], P('gx', 'gy', 'gz'), may hold values from 0 to 63
- tile_counts: int32 [4, 2, 256], P('gx', 'gy', 'gz'), may hold values from 1 to 8, as said below
- ghost_counts: int32 [4, 2, 4, 4], P('gx', 'gy', 'gz'), may hold values from 1 to 12
- cell_index: int32 [4, 2, 32768], P('gx', 'gy', 'gz'), may hold values from 0 to 4095, as said below
- fluid_vel: float32 [3, 4, 2, 4096], P(None, 'gx', 'gy', 'gz'), may hold values from -6 to 6
- fluid_frac: float32 [4, 2, 4096], P('gx', 'gy', 'gz'), may hold values from 0.4 to 0.9
Outputs:
- velocity_new: float32 [3, 4, 2, 32768], P(None, 'gx', 'gy', 'gz')
- fluid_new: float32 [3, 4, 2, 4096], P(None, 'gx', 'gy', 'gz')
The draws below stay inside these ranges and needn't reach their ends.
Inputs may be any that keep to these rules, and one draw needn't show every extreme that they name: `state`: rows 0 to 2 are positions within 0 to 1, rows 3 to 5 velocities, row 6 radii within 0.15 to 0.35. `tile_counts`: in every box the first tile's count is the largest of that box. `cell_index`: A particle of box z along z has its cell in that box's slab, cells z * 1024 to (z + 1) * 1024 - 1, or in the slab of a box beside it along z.
All inputs are finite; a program needn't handle non-finite values.
Results may differ from the reference program's by a relative error of at most 0.0003.
Values sent between devices are 32-bit elements; how exact they have to be, the bound alone decides.
No kernel may reach another device: no remote copies, remote signals or barrier semaphores. Data moves between devices by JAX's collectives and lax.ppermute only.
A program may use at most 64 MiB of HBM per device.

```python
import math
import jax
import jax.numpy as jnp
from jax import lax

TILE = 128
K = 8
NT = 64
FC_DEV = 1024
GB = 12
BOX_X = 4
BOX_Y = 2
BOX_Z = 4
TILES = 256
PARTS_SIZE = 32768
FLUID = 4096


def draw_state(key, part):
    key_pos = jax.random.fold_in(key, 101)
    key_vel = jax.random.fold_in(key, 102)
    key_rad = jax.random.fold_in(key, 103)
    positions = jax.random.uniform(key_pos, (3, BOX_X, BOX_Y, PARTS_SIZE), jnp.float32)
    velocity = jax.random.normal(key_vel, (3, BOX_X, BOX_Y, PARTS_SIZE), jnp.float32)
    radius = 0.15 * jnp.exp(jax.random.uniform(key_rad, (1, BOX_X, BOX_Y, PARTS_SIZE), jnp.float32) * math.log(0.35 / 0.15))
    return jnp.concatenate([positions, velocity, radius], axis=0).astype(jnp.float32)


def draw_tile_counts(key, part):
    key_level = jax.random.fold_in(key, 201)
    key_tiles = jax.random.fold_in(key, 202)
    level = jax.random.randint(key_level, (BOX_X, BOX_Y, BOX_Z, 1), 2, K + 1)
    level = level.at[0, 0, 0, 0].set(K)
    raw_draw = jax.random.randint(key_tiles, (BOX_X, BOX_Y, BOX_Z, NT), 0, 1048576)
    counts = 1 + raw_draw % level
    counts = counts.at[:, :, :, 0].set(level[:, :, :, 0])
    return counts.reshape(BOX_X, BOX_Y, BOX_Z * NT).astype(jnp.int32)


def draw_cell_index(key, part):
    key_side = jax.random.fold_in(key, 301)
    key_cell = jax.random.fold_in(key, 302)
    box_z = jnp.arange(PARTS_SIZE, dtype=jnp.int32) // (NT * TILE)
    roll = jax.random.randint(key_side, (BOX_X, BOX_Y, PARTS_SIZE), 0, 16)
    side = jnp.where(roll == 0, -1, jnp.where(roll == 1, 1, 0)).astype(jnp.int32)
    target = jnp.clip(box_z[None, None, :] + side, 0, BOX_Z - 1)
    offset = jax.random.randint(key_cell, (BOX_X, BOX_Y, PARTS_SIZE), 0, FC_DEV)
    return (target * FC_DEV + offset).astype(jnp.int32)


def plant(entries, rng, low, largest):
    extent = entries.shape
    place = [jax.random.randint(jax.random.fold_in(rng, axis), (), 0, extent[axis]) for axis in range(len(extent))]
    entries = entries.at[tuple(place)].set(low)
    longest = extent.index(max(extent))
    place[longest] = (place[longest] + 1) % extent[longest]
    return entries.at[tuple(place)].set(largest)


def block_scale(key, dims, cuts, low, largest):
    factor_of, own = 1.0, jax.random.fold_in(key, 6)
    for dim, blocks in cuts:
        draws = jnp.exp(jax.random.uniform(jax.random.fold_in(own, dim), (blocks,), jnp.float32, low / len(cuts), largest / len(cuts)))
        factor_of = factor_of * jnp.repeat(draws, dims[dim] // blocks).reshape([-1 if axis == dim else 1 for axis in range(len(dims))])
    return factor_of


def bell_draw(rng, extent, deviation, most, shards=(), kind=jnp.bfloat16):
    drawn = jax.random.normal(rng, extent, jnp.float32) * deviation
    if len(shards) > 0:
        drawn = block_scale(rng, extent, shards, -0.22, 0.18) * drawn
    return jnp.clip(drawn, min=-most, max=most).astype(kind)


def setup_inputs(seed: int = 0) -> dict:
    keys = jax.random.split(jax.random.key(seed), 8)
    state = draw_state(jax.random.fold_in(keys[7], 71), 0)
    tile_lists = plant(jax.random.randint(keys[1], (BOX_X, BOX_Y, TILES, K), 0, NT), jax.random.fold_in(keys[1], 1), 0, NT - 1).astype(jnp.int32)
    tile_counts = draw_tile_counts(jax.random.fold_in(keys[7], 71), 0)
    ghost_counts = plant(jax.random.randint(keys[3], (BOX_X, BOX_Y, BOX_Z, 4), 1, GB + 1), jax.random.fold_in(keys[3], 1), 1, GB).astype(jnp.int32)
    cell_index = draw_cell_index(jax.random.fold_in(keys[7], 71), 0)
    fluid_vel = bell_draw(keys[5], (3, BOX_X, BOX_Y, FLUID), 1.0, 6.0, ((1, 4), (2, 2), (3, 4)), jnp.float32)
    fluid_frac = jnp.clip(0.4 + 0.49999997 * jax.random.uniform(keys[6], (BOX_X, BOX_Y, FLUID), jnp.float32) ** block_scale(keys[6], (BOX_X, BOX_Y, FLUID), ((0, 4), (1, 2), (2, 4)), -0.2, 0.2), 0.4, 0.9)
    return dict(state=state, tile_lists=tile_lists, tile_counts=tile_counts, ghost_counts=ghost_counts, cell_index=cell_index, fluid_vel=fluid_vel, fluid_frac=fluid_frac)


stiffness = 5.0
damping = 2.0
time_step = 0.25
drag_coef = 64.0
fluid_density = 2.0
radius_ref = 0.25
highest = lax.Precision.HIGHEST


def pair_weight(near_tiles, far_tiles):
    offset = near_tiles[0][:, :, None] - far_tiles[0][:, None, :]
    distance = offset * offset
    for column in range(1, 3):
        offset = near_tiles[column][:, :, None] - far_tiles[column][:, None, :]
        distance = distance + offset * offset
    contact_reach = near_tiles[6][:, :, None] + far_tiles[6][:, None, :]
    return jnp.maximum(contact_reach * contact_reach - distance, 0.0) * near_tiles[7][:, :, None] * far_tiles[7][:, None, :]


def force_near(near_tiles, far_tiles, weight):
    totals = jnp.sum(weight, axis=2)
    weighted = jnp.einsum("tij,ctj->cti", weight, far_tiles[0:6], precision=highest)
    return stiffness * (near_tiles[0:3] * totals - weighted[0:3]) - damping * (near_tiles[3:6] * totals - weighted[3:6])


def face_block(tile_state, ghost_counts, face_index):
    border = tile_state[:, :, :, :, face_index * GB:(face_index + 1) * GB, :]
    living = (jnp.arange(GB, dtype=jnp.int32)[None, None, None, :] < ghost_counts[:, :, :, face_index:face_index + 1]).astype(jnp.float32)
    living = jnp.broadcast_to(living[None, :, :, :, :, None], (1,) + border.shape[1:])
    return jnp.concatenate([border, living], axis=0)


def shift_axis(blocked, along, upward):
    size_along = blocked.shape[along]
    zero_rim = jnp.zeros_like(lax.slice_in_dim(blocked, 0, 1, axis=along))
    if upward:
        return jnp.concatenate([zero_rim, lax.slice_in_dim(blocked, 0, size_along - 1, axis=along)], axis=along)
    return jnp.concatenate([lax.slice_in_dim(blocked, 1, size_along, axis=along), zero_rim], axis=along)


def box_forces(inputs):
    owned_tiles, tile_list, counts, face_tiles, ghosts = inputs

    def add_listed(listed, running):
        partner = jnp.take(owned_tiles, tile_list[:, listed], axis=1)
        weight = pair_weight(owned_tiles, partner)
        living = (listed < counts).astype(jnp.float32)
        return running + force_near(owned_tiles, partner, weight) * living[None, :, None]

    interior = lax.fori_loop(0, K, add_listed, jnp.zeros((3, NT, TILE), jnp.float32))
    across = force_near(face_tiles, ghosts, pair_weight(face_tiles, ghosts))
    return jnp.concatenate([interior[:, :4 * GB] + across, interior[:, 4 * GB:]], axis=1)


def reference(state, tile_lists, tile_counts, ghost_counts, cell_index, fluid_vel, fluid_frac):
    tile_state = state.reshape(7, BOX_X, BOX_Y, BOX_Z, NT, TILE)
    unit_rows = jnp.ones((1,) + tile_state.shape[1:], jnp.float32)
    owned_tiles = jnp.concatenate([tile_state, unit_rows], axis=0)
    face_list = [face_block(tile_state, ghost_counts, face_index) for face_index in range(4)]
    ghost_list = [shift_axis(face_list[1], 1, True), shift_axis(face_list[0], 1, False),
                  shift_axis(face_list[3], 2, True), shift_axis(face_list[2], 2, False)]
    face_tiles = jnp.concatenate(face_list, axis=4)
    ghosts = jnp.concatenate(ghost_list, axis=4)
    box_count = BOX_X * BOX_Y * BOX_Z

    def flatten_boxes(blocked):
        return jnp.moveaxis(blocked.reshape((blocked.shape[0], box_count) + blocked.shape[4:]), 1, 0)

    forces = lax.map(box_forces, (flatten_boxes(owned_tiles), tile_lists.reshape(box_count, NT, K),
                                  tile_counts.reshape(box_count, NT), flatten_boxes(face_tiles), flatten_boxes(ghosts)))
    columns = BOX_X * BOX_Y
    forces = jnp.moveaxis(forces, 0, 1).reshape(3, columns, PARTS_SIZE)
    velocity = state[3:6].reshape(3, columns, PARTS_SIZE)
    radius = state[6].reshape(1, columns, PARTS_SIZE)
    masses = (radius / radius_ref) ** 3
    drag_rate = drag_coef * radius * radius
    moved = velocity + time_step * forces / masses
    sources = jnp.concatenate([drag_rate * velocity, drag_rate], axis=0)
    cell_ids = cell_index.reshape(columns, PARTS_SIZE)

    def deposit(source, cell_row):
        return jax.ops.segment_sum(source.T, cell_row, num_segments=FLUID).T

    totals = jax.vmap(deposit, in_axes=(1, 0), out_axes=1)(sources, cell_ids)
    fraction = fluid_frac.reshape(1, columns, FLUID)
    previous = fluid_vel.reshape(3, columns, FLUID)
    fluid_new = (fluid_density * fraction * previous + time_step * totals[0:3]) / (fluid_density * fraction + time_step * totals[3:4])
    at_cell = jnp.take_along_axis(fluid_new, jnp.broadcast_to(cell_ids[None], (3, columns, PARTS_SIZE)), axis=2)
    coupling = time_step * drag_rate / masses
    velocity_new = (moved + coupling * at_cell) / (1.0 + coupling)
    return velocity_new.reshape(3, BOX_X, BOX_Y, PARTS_SIZE), fluid_new.reshape(3, BOX_X, BOX_Y, FLUID)
```

```python
import functools

import jax
import jax.numpy as jnp
from jax import lax
from jax.experimental import pallas as pl
from jax.experimental.pallas import tpu as pltpu
from jax.sharding import PartitionSpec as P

TILE = 128
K = 8
NT = 64
GB = 12
FACE = 16
LANES = 128

stiffness = 5.0
damping = 2.0
time_step = 0.25
drag_coef = 64.0
fluid_density = 2.0
radius_ref = 0.25
spring = stiffness / damping

f32 = jnp.float32
bf16 = jnp.bfloat16

NROW = 32
VROW = 16
GHOST = NT
NFAR = NT + 4 * FACE
DUMMY = NFAR
GROUP = 8
SLOTS = NT * 5 + GROUP


def parts_of(q):
    first = q.astype(bf16).astype(f32)
    rest = q - first
    second = rest.astype(bf16).astype(f32)
    return first, second, (rest - second).astype(bf16).astype(f32)


ORDER = ((0, 0), (0, 1), (0, 2), (1, 0), (1, 1), (2, 0))


def centred(position):
    return position - 0.5


def geometry(columns):
    x, y, z = (centred(columns[k]) for k in range(3))
    r = columns[6]
    return (x, y, z, r), r * r - (x * x + y * y + z * z)


def near_rows(columns):
    lengths, own = geometry(columns)
    one = jnp.ones_like(own)
    rows = []
    for q in lengths:
        cut = parts_of(q)
        rows += [2.0 * cut[j] for _, j in ORDER]
    return rows + [one] * 3 + list(parts_of(own))


def far_rows(columns):
    lengths, own = geometry(columns)
    one = jnp.ones_like(own)
    rows = []
    for q in lengths:
        cut = parts_of(q)
        rows += [cut[i] for i, _ in ORDER]
    return rows + list(parts_of(own)) + [one] * 3


def value_rows(columns, living):
    cuts = [parts_of((columns[3 + c] - spring * centred(columns[c]))) for c in range(3)]
    return [cuts[c][k] * living for k in range(3) for c in range(3)] + [living]


def deposit_kernel(
    state_ref, cell_ref, vel_ref, frac_ref, ghost_ref,
    up_ref, down_ref, far_up_ref, far_down_ref, own_ref, mine_ref,
    xup_ref, xdown_ref, yup_ref, ydown_ref, acc_ref,
):
    slab = vel_ref.shape[1]
    wide = 3 * slab
    first_row = (lax.axis_index("gz") - 1) * slab
    acc_ref[...] = jnp.zeros_like(acc_ref)
    sub = lax.broadcasted_iota(jnp.int32, (wide, LANES), 0)
    lane_of = lax.broadcasted_iota(jnp.int32, (LANES, LANES), 0)

    def add_group(group, carry):
        rows = pl.ds(pl.multiple_of(group * 8, 8), 8)
        r = state_ref[6, rows, :]
        rate = drag_coef * r * r
        sources = [rate * state_ref[3 + c, rows, :] for c in range(3)] + [rate]
        cut = [part for source in sources for part in parts_of(source)]
        cells = cell_ref[rows, :]
        high = lax.shift_right_logical(cells, 7) - first_row
        low = jnp.bitwise_and(cells, LANES - 1)
        left, right = [], []
        for t in range(8):
            mask = high[t : t + 1, :] == sub
            left.append(
                jnp.concatenate(
                    [jnp.where(mask, part[t : t + 1, :], 0.0) for part in cut], axis=0
                ).astype(bf16)
            )
            right.append(jnp.where(low[t : t + 1, :] == lane_of, 1.0, 0.0).astype(bf16))
        acc_ref[...] += lax.dot_general(
            jnp.concatenate(left, axis=1),
            jnp.concatenate(right, axis=1),
            (((1,), (1,)), ((), ())),
            preferred_element_type=f32,
        )
        return carry

    lax.fori_loop(0, NT // 8, add_group, 0)
    frac = fluid_density * frac_ref[...]
    for c in range(4):
        base = 3 * c * wide
        total = sum(acc_ref[pl.ds(base + k * wide, wide), :] for k in range(3)) * time_step
        below, here, above = (total[k * slab : (k + 1) * slab] for k in range(3))
        own = here + (frac * vel_ref[c] if c < 3 else frac)
        own_ref[c] = own
        mine_ref[c] = below
        mine_ref[4 + c] = above
        up_ref[c] = own
        up_ref[4 + c] = above
        down_ref[c] = own
        down_ref[4 + c] = below
        far_up_ref[c] = above
        far_down_ref[c] = below
    order = lax.broadcasted_iota(jnp.int32, (FACE, TILE), 0)
    for face, ref in enumerate((xdown_ref, xup_ref, ydown_ref, yup_ref)):
        for k in range(7):
            ref[k, 0:GB, :] = state_ref[k, face * GB : (face + 1) * GB, :]
            ref[k, GB:FACE, :] = jnp.zeros((FACE - GB, TILE), f32)
        ref[7] = jnp.where(order < ghost_ref[face], 1.0, 0.0)


def contact_kernel(
    state_ref, lists_ref, counts_ref, ghost_ref, xlow_ref, xhigh_ref, ylow_ref, yhigh_ref,
    out_ref, near_ref, near16_ref, far_ref, turned_ref, value_ref, value16_ref, acc_ref,
    at_near, at_first, at_second,
):
    columns = [state_ref[k] for k in range(7)]
    zero = jnp.zeros((NT, TILE), f32)
    one = jnp.ones((NT, TILE), f32)
    for k, row in enumerate(near_rows(columns) + [zero] * 2):
        near_ref[pl.ds(k, NT, stride=NROW), :] = row
    for k, row in enumerate(far_rows(columns) + [zero] * 2):
        far_ref[pl.ds(k, NT, stride=NROW), :] = row
    for k, row in enumerate(value_rows(columns, one) + [zero] * 6):
        value_ref[pl.ds(k, NT, stride=VROW), :] = row
    zero = jnp.zeros((FACE, TILE), f32)
    for face, ref in enumerate((xlow_ref, xhigh_ref, ylow_ref, yhigh_ref)):
        columns = [ref[k] for k in range(7)]
        first = GHOST + face * FACE
        for k, row in enumerate(far_rows(columns) + [zero] * 2):
            far_ref[pl.ds(first * NROW + k, FACE, stride=NROW), :] = row
        for k, row in enumerate(value_rows(columns, ref[7]) + [zero] * 6):
            value_ref[pl.ds(first * VROW + k, FACE, stride=VROW), :] = row
    value16_ref[pl.ds(DUMMY * VROW, VROW), :] = jnp.zeros((VROW, TILE), bf16)
    near16_ref[...] = jnp.zeros_like(near16_ref)
    acc_ref[...] = jnp.zeros_like(acc_ref)

    x, y = lax.axis_index("gx"), lax.axis_index("gy")
    beside = (x > 0, x < lax.axis_size("gx") - 1, y > 0, y < lax.axis_size("gy") - 1)
    living = [jnp.where(beside[face], ghost_ref[face], 0) for face in range(4)]

    def prepare(t, n):
        near16_ref[pl.ds(pl.multiple_of(t * 128 + 96, 32), NROW), :] = near_ref[
            pl.ds(pl.multiple_of(t * NROW, NROW), NROW), :
        ].astype(bf16)
        face = lax.div(t, GB)
        place = t - face * GB
        alive = jnp.where(
            face == 0, living[0],
            jnp.where(face == 1, living[1], jnp.where(face == 2, living[2], jnp.where(face == 3, living[3], 0))),
        )
        ghost = (place < alive).astype(jnp.int32)
        ghost_tile = GHOST + face * FACE + place
        count = counts_ref[t]
        for d in range(5):
            at_near[n + d] = t
            at_first[n + d] = jnp.where(2 * d < count, lists_ref[min(2 * d, K - 1), t], ghost_tile)
            at_second[n + d] = jnp.where(
                2 * d + 1 < count,
                lists_ref[min(2 * d + 1, K - 1), t],
                jnp.where(2 * d + 1 < count + ghost, ghost_tile, DUMMY),
            )
        return n + lax.shift_right_logical(count + ghost + 1, 1)

    steps = lax.fori_loop(0, NT, prepare, jnp.int32(0))
    for d in range(GROUP):
        at_near[steps + d] = NT
        at_first[steps + d] = 0
        at_second[steps + d] = DUMMY

    def turn(b, carry):
        rows = pl.ds(pl.multiple_of(b * 128, 128), 128)
        turned_ref[rows, :] = far_ref[rows, :].T.astype(bf16)
        rows = pl.ds(pl.multiple_of(b * 4 * VROW, 4 * VROW), 4 * VROW)
        value16_ref[rows, :] = value_ref[rows, :].astype(bf16)
        return carry

    lax.fori_loop(0, NFAR // 4, turn, 0)
    blank = jnp.zeros((128, TILE), bf16)

    def near_block(t, s):
        start = t * 128 + 96 - NROW * jnp.bitwise_and(s, 3)
        return near16_ref[pl.ds(pl.multiple_of(start, NROW), 128), :]

    def far_block(s):
        return turned_ref[pl.ds(pl.multiple_of(lax.shift_right_logical(s, 2) * 128, 128), 128), :]

    def value_block(s):
        return value16_ref[pl.ds(pl.multiple_of(s * VROW, VROW), VROW), :]

    def step(group, carry):
        sums = []
        for d in range(GROUP):
            at = group * GROUP + d
            t, a, b = at_near[at], at_first[at], at_second[at]
            near = jnp.minimum(t, NT - 1)
            far = jnp.minimum(b, NFAR - 1)
            right = jnp.concatenate(
                [
                    jnp.concatenate([near_block(near, a), blank], axis=1),
                    jnp.concatenate([blank, near_block(near, far)], axis=1),
                ],
                axis=0,
            )
            left = jnp.concatenate([far_block(a), far_block(far)], axis=1)
            weight = jnp.maximum(jnp.dot(left, right, preferred_element_type=f32), 0.0)
            coarse = weight.astype(bf16)
            fine = (weight - coarse.astype(f32)).astype(bf16)
            weights = jnp.concatenate(
                [
                    jnp.concatenate([coarse[:, :TILE], fine[:, :TILE]], axis=1),
                    jnp.concatenate([coarse[:, TILE:], fine[:, TILE:]], axis=1),
                ],
                axis=0,
            )
            values = jnp.concatenate([value_block(a), value_block(b)], axis=1)
            both = jnp.dot(values, weights, preferred_element_type=f32)
            sums.append((t, both[:, :TILE] + both[:, TILE:]))
        for t, total in sums:
            acc_ref[pl.ds(pl.multiple_of(t * VROW, VROW), VROW), :] += total
        return carry

    lax.fori_loop(0, lax.div(steps + (GROUP - 1), GROUP), step, 0)
    row = lambda k: acc_ref[pl.ds(k, NT, stride=VROW), :]
    total = row(9)
    for c in range(3):
        own = state_ref[3 + c] - spring * centred(state_ref[c])
        out_ref[c] = -damping * (own * total - (row(c) + row(3 + c) + row(6 + c)))


def update_kernel(
    state_ref, cell_ref, forces_ref, own_ref, mine_ref, below_ref, above_ref, far_below_ref, far_above_ref,
    new_ref, fluid_ref, table_ref,
):
    slab = own_ref.shape[1]
    wide = 3 * slab
    z, count = lax.axis_index("gz"), lax.axis_size("gz")
    first_row = (z - 1) * slab

    def inside(flag, value):
        return jnp.where(flag, value, 0.0)

    has_below, has_above = z >= 1, z <= count - 2
    has_far_below, has_far_above = z >= 2, z <= count - 3

    def solved(total):
        return [total[c] / total[3] for c in range(3)]

    here = solved([
        own_ref[c] + inside(has_below, below_ref[4 + c]) + inside(has_above, above_ref[4 + c]) for c in range(4)
    ])
    lower = solved([
        jnp.where(has_below, below_ref[c], 1.0) + mine_ref[c] + inside(has_far_below, far_below_ref[c]) for c in range(4)
    ])
    upper = solved([
        jnp.where(has_above, above_ref[c], 1.0) + mine_ref[4 + c] + inside(has_far_above, far_above_ref[c]) for c in range(4)
    ])
    for c in range(3):
        fluid_ref[c] = here[c]
        table_ref[pl.ds(c * wide, slab), :] = lower[c]
        table_ref[pl.ds(c * wide + slab, slab), :] = here[c]
        table_ref[pl.ds(c * wide + 2 * slab, slab), :] = upper[c]

    def update_group(group, carry):
        rows = pl.ds(pl.multiple_of(group * 8, 8), 8)
        cells = cell_ref[rows, :]
        high = lax.shift_right_logical(cells, 7) - first_row
        low = jnp.bitwise_and(cells, LANES - 1)
        at_cell = [jnp.zeros((8, LANES), f32)] * 3
        for h in range(wide):
            chosen = high == h
            for c in range(3):
                line = jnp.broadcast_to(table_ref[c * wide + h : c * wide + h + 1, :], (8, LANES))
                taken = jnp.take_along_axis(line, low, axis=1, mode="promise_in_bounds")
                at_cell[c] = jnp.where(chosen, taken, at_cell[c])
        r = state_ref[6, rows, :]
        ratio = r / radius_ref
        masses = ratio * ratio * ratio
        rate = drag_coef * r * r
        coupling = time_step * rate / masses
        for c in range(3):
            moved = state_ref[3 + c, rows, :] + time_step * forces_ref[c, rows, :] / masses
            new_ref[c, rows, :] = (moved + coupling * at_cell[c]) / (1.0 + coupling)
        return carry

    lax.fori_loop(0, NT // 8, update_group, 0)


def shifted(value, axis, steps):
    count = lax.axis_size(axis)
    return lax.ppermute(value, axis, [(i, (i + steps) % count) for i in range(count)])


vmem = pl.BlockSpec(memory_space=pltpu.VMEM)
smem = pl.BlockSpec(memory_space=pltpu.SMEM)
roomy = pltpu.CompilerParams(vmem_limit_bytes=40 * 2**20)


def body(state, tile_lists, tile_counts, ghost_counts, cell_index, fluid_vel, fluid_frac):
    particles = state.shape[3]
    cell_count = fluid_vel.shape[3]
    slab = cell_count // LANES
    tiles = state.reshape(7, NT, TILE)
    cells = cell_index.reshape(NT, TILE)
    lists = tile_lists.reshape(NT, K).T
    counts = tile_counts.reshape(NT)
    ghosts = ghost_counts.reshape(4)

    def shape(*dims):
        return jax.ShapeDtypeStruct(dims, f32)

    face = shape(8, FACE, TILE)
    up, down, far_up, far_down, own, mine, x_up, x_down, y_up, y_down = pl.pallas_call(
        deposit_kernel,
        out_shape=(
            shape(8, slab, LANES), shape(8, slab, LANES), shape(4, slab, LANES), shape(4, slab, LANES),
            shape(4, slab, LANES), shape(8, slab, LANES), face, face, face, face,
        ),
        in_specs=[vmem] * 4 + [smem],
        out_specs=(vmem,) * 10,
        scratch_shapes=[pltpu.VMEM((12 * 3 * slab, LANES), f32)],
        compiler_params=roomy,
        name="deposit",
    )(tiles, cells, fluid_vel.reshape(3, slab, LANES), fluid_frac.reshape(slab, LANES), ghosts)

    if lax.axis_size("gy") == 2:
        y_low = y_high = shifted(jnp.where(lax.axis_index("gy") == 0, y_up, y_down), "gy", 1)
    else:
        y_low, y_high = shifted(y_up, "gy", 1), shifted(y_down, "gy", -1)
    x_low, x_high = shifted(x_up, "gx", 1), shifted(x_down, "gx", -1)
    below, above = shifted(up, "gz", 1), shifted(down, "gz", -1)
    depth = lax.axis_size("gz")
    if depth == 4:
        far_below = far_above = shifted(jnp.where(lax.axis_index("gz") < 2, far_up, far_down), "gz", 2)
    else:
        far_below, far_above = shifted(far_up, "gz", 2), shifted(far_down, "gz", -2)

    forces = pl.pallas_call(
        contact_kernel,
        out_shape=shape(3, NT, TILE),
        in_specs=[vmem] + [smem] * 3 + [vmem] * 4,
        out_specs=vmem,
        scratch_shapes=[
            pltpu.VMEM((NT * NROW, TILE), f32),
            pltpu.VMEM((NT * 128 + 128, TILE), bf16),
            pltpu.VMEM((NFAR * NROW, TILE), f32),
            pltpu.VMEM((NFAR * NROW, TILE), bf16),
            pltpu.VMEM((NFAR * VROW, TILE), f32),
            pltpu.VMEM(((NFAR + 1) * VROW, TILE), bf16),
            pltpu.VMEM(((NT + 1) * VROW, TILE), f32),
        ] + [pltpu.SMEM((SLOTS,), jnp.int32)] * 3,
        compiler_params=roomy,
        name="contact",
    )(tiles, lists, counts, ghosts, x_low, x_high, y_low, y_high)

    velocity_new, fluid_new = pl.pallas_call(
        update_kernel,
        out_shape=(shape(3, NT, TILE), shape(3, slab, LANES)),
        in_specs=[vmem] * 9,
        out_specs=(vmem, vmem),
        scratch_shapes=[pltpu.VMEM((9 * slab, LANES), f32)],
        compiler_params=roomy,
        name="update",
    )(tiles, cells, forces, own, mine, below, above, far_below, far_above)
    return velocity_new.reshape(3, 1, 1, particles), fluid_new.reshape(3, 1, 1, cell_count)


def solution(mesh):
    return jax.shard_map(
        body,
        mesh=mesh,
        in_specs=(
            P(None, "gx", "gy", "gz"),
            P("gx", "gy", "gz", None),
            P("gx", "gy", "gz"),
            P("gx", "gy", "gz", None),
            P("gx", "gy", "gz"),
            P(None, "gx", "gy", "gz"),
            P("gx", "gy", "gz"),
        ),
        out_specs=(P(None, "gx", "gy", "gz"), P(None, "gx", "gy", "gz")),
        check_vma=False,
    )
```

```python
import jax
import jax.numpy as jnp
from jax import lax
from jax.experimental import pallas as pl
from jax.experimental.pallas import tpu as pltpu
from jax.sharding import PartitionSpec as P

TILE = 128
K = 8
NT = 64
GB = 12
FACE = 16
LANES = 128

stiffness = 5.0
damping = 2.0
time_step = 0.25
drag_coef = 64.0
fluid_density = 2.0
radius_ref = 0.25
spring = stiffness / damping

f32 = jnp.float32
bf16 = jnp.bfloat16

NROW = 32
VROW = 16
DUMMY = NT
GROUP = 16
LATER = 4
SLOTS = NT * 5


def parts_of(q):
    first = q.astype(bf16).astype(f32)
    rest = q - first
    second = rest.astype(bf16).astype(f32)
    return first, second, (rest - second).astype(bf16).astype(f32)


ORDER = ((0, 0), (0, 1), (0, 2), (1, 0), (1, 1), (2, 0))


def centred(position):
    return position - 0.5


def geometry(columns):
    x, y, z = (centred(columns[k]) for k in range(3))
    r = columns[6]
    return (x, y, z, r), r * r - (x * x + y * y + z * z)


def near_rows(columns):
    lengths, own = geometry(columns)
    one = jnp.ones_like(own)
    rows = []
    for q in lengths:
        cut = parts_of(q)
        rows += [2.0 * cut[j] for _, j in ORDER]
    return rows + [one] * 3 + list(parts_of(own))


def far_rows(columns):
    lengths, own = geometry(columns)
    one = jnp.ones_like(own)
    rows = []
    for q in lengths:
        cut = parts_of(q)
        rows += [cut[i] for i, _ in ORDER]
    return rows + list(parts_of(own)) + [one] * 3


def value_rows(columns, living):
    cuts = [parts_of((columns[3 + c] - spring * centred(columns[c]))) for c in range(3)]
    return [cuts[c][k] * living for k in range(3) for c in range(3)] + [living]


def load(pairs, sems):
    copies = [pltpu.make_async_copy(source, target, sems.at[k]) for k, (source, target) in enumerate(pairs)]
    for copy in copies:
        copy.start()
    return copies


def pair_sums(left, right, values):
    weight = jnp.maximum(jnp.dot(left, right, preferred_element_type=f32), 0.0)
    coarse = weight.astype(bf16)
    fine = (weight - coarse.astype(f32)).astype(bf16)
    weights = jnp.concatenate(
        [
            jnp.concatenate([coarse[:, :TILE], fine[:, :TILE]], axis=1),
            jnp.concatenate([coarse[:, TILE:], fine[:, TILE:]], axis=1),
        ],
        axis=0,
    )
    both = jnp.dot(values, weights, preferred_element_type=f32)
    return both[:, :TILE] + both[:, TILE:]


def two_near(first, second):
    blank = jnp.zeros((128, TILE), bf16)
    return jnp.concatenate(
        [jnp.concatenate([first, blank], axis=1), jnp.concatenate([blank, second], axis=1)], axis=0
    )


def interior_steps(begin, end, work_ref, near_ref, turned_ref, value_ref, acc_ref):
    def near_block(t, s):
        start = t * 128 + 96 - NROW * jnp.bitwise_and(s, 3)
        return near_ref[pl.ds(pl.multiple_of(start, NROW), 128), :]

    def far_block(s):
        return turned_ref[pl.ds(pl.multiple_of(lax.shift_right_logical(s, 2) * 128, 128), 128), :]

    def value_block(s):
        return value_ref[pl.ds(pl.multiple_of(s * VROW, VROW), VROW), :]

    def step(group, carry):
        sums = []
        for d in range(GROUP):
            word = work_ref[group * GROUP + d]
            t = lax.shift_right_logical(word, 16)
            a = jnp.bitwise_and(lax.shift_right_logical(word, 8), 255)
            b = jnp.bitwise_and(word, 255)
            near, far = jnp.minimum(t, NT - 1), jnp.minimum(b, NT - 1)
            total = pair_sums(
                jnp.concatenate([far_block(a), far_block(far)], axis=1),
                two_near(near_block(near, a), near_block(near, far)),
                jnp.concatenate([value_block(a), value_block(b)], axis=1),
            )
            sums.append((t, total))
        for t, total in sums:
            acc_ref[pl.ds(pl.multiple_of(t * VROW, VROW), VROW), :] += total
        return carry

    lax.fori_loop(begin, end, step, 0)


def first_kernel(
    state_hbm, cell_hbm, vel_hbm, frac_hbm, lists_ref, counts_ref, ghost_ref,
    up_ref, down_ref, far_up_ref, far_down_ref, own_ref, mine_ref,
    xup_ref, xdown_ref, yup_ref, ydown_ref, near16_ref, turned_ref, value16_ref, acc_ref, work_ref,
    state_ref, cell_ref, vel_ref, frac_ref, source_ref, deposit_ref, total_ref, near_ref, far_ref, value_ref, sems,
):
    copies = load(
        [(state_hbm, state_ref), (cell_hbm, cell_ref), (vel_hbm, vel_ref), (frac_hbm, frac_ref)], sems
    )
    acc_ref[...] = jnp.zeros_like(acc_ref)
    value16_ref[pl.ds(DUMMY * VROW, VROW), :] = jnp.zeros((VROW, TILE), bf16)
    near16_ref[pl.ds(NT * 128, 128), :] = jnp.zeros((128, TILE), bf16)
    slab = vel_ref.shape[1]
    wide = 3 * slab
    bands = wide // 2
    first_band = (lax.axis_index("gz") - 1) * (slab // 2)
    for copy in copies:
        copy.wait()

    r = state_ref[6]
    rate = drag_coef * r * r
    sources = [rate * state_ref[3 + c] for c in range(3)] + [rate]
    for c, source in enumerate(sources):
        for k, part in enumerate(parts_of(source)[:2]):
            source_ref[pl.ds(4 * k + c, NT, stride=8), :] = part
    low_of = lax.broadcasted_iota(jnp.int32, (2 * LANES, LANES), 0)

    def add_group(group, total):
        cells = cell_ref[pl.ds(pl.multiple_of(group * 8, 8), 8), :]
        band = lax.shift_right_logical(cells, 8) - first_band
        low = jnp.bitwise_and(cells, 255)
        left, right = [], []
        for t in range(8):
            rows = source_ref[pl.ds(pl.multiple_of(group * 64 + t * 8, 8), 8), :]
            here = jnp.broadcast_to(band[t : t + 1, :], (8, LANES))
            left.append(jnp.concatenate([jnp.where(here == h, rows, 0.0) for h in range(bands)], axis=0).astype(bf16))
            right.append(jnp.where(low[t : t + 1, :] == low_of, 1.0, 0.0).astype(bf16))
        added = lax.dot_general(
            jnp.concatenate(left, axis=1),
            jnp.concatenate(right, axis=1),
            (((1,), (1,)), ((), ())),
            preferred_element_type=f32,
        )
        deposit_ref[0] += added[:, :LANES]
        deposit_ref[1] += added[:, LANES:]
        return total

    deposit_ref[...] = jnp.zeros_like(deposit_ref)
    lax.fori_loop(0, NT // 8, add_group, 0, unroll=2)
    frac = fluid_density * frac_ref[...]
    for c in range(4):
        for k in range(2):
            both = deposit_ref[k, pl.ds(c, bands, stride=8), :] + deposit_ref[k, pl.ds(4 + c, bands, stride=8), :]
            total_ref[pl.ds(k, bands, stride=2), :] = both * time_step
        below, here, above = (total_ref[pl.ds(k * slab, slab), :] for k in range(3))
        own = here + (frac * vel_ref[c] if c < 3 else frac)
        own_ref[c] = own
        mine_ref[c] = below
        mine_ref[4 + c] = above
        up_ref[c] = own
        up_ref[4 + c] = above
        down_ref[c] = own
        down_ref[4 + c] = below
        far_up_ref[c] = above
        far_down_ref[c] = below
    order = lax.broadcasted_iota(jnp.int32, (FACE, TILE), 0)
    for face, ref in enumerate((xdown_ref, xup_ref, ydown_ref, yup_ref)):
        for k in range(7):
            ref[k, 0:GB, :] = state_ref[k, face * GB : (face + 1) * GB, :]
            ref[k, GB:FACE, :] = jnp.zeros((FACE - GB, TILE), f32)
        ref[7] = jnp.where(order < ghost_ref[face], 1.0, 0.0)

    columns = [state_ref[k] for k in range(7)]
    zero = jnp.zeros((NT, TILE), f32)
    one = jnp.ones((NT, TILE), f32)
    for k, row in enumerate(near_rows(columns) + [zero] * 2):
        near_ref[pl.ds(k, NT, stride=NROW), :] = row
    for k, row in enumerate(far_rows(columns) + [zero] * 2):
        far_ref[pl.ds(k, NT, stride=NROW), :] = row
    for k, row in enumerate(value_rows(columns, one) + [zero] * 6):
        value_ref[pl.ds(k, NT, stride=VROW), :] = row

    def prepare(b, n):
        rows = pl.ds(pl.multiple_of(b * 128, 128), 128)
        turned_ref[rows, :] = far_ref[rows, :].T.astype(bf16)
        rows = pl.ds(pl.multiple_of(b * 4 * VROW, 4 * VROW), 4 * VROW)
        value16_ref[rows, :] = value_ref[rows, :].astype(bf16)
        for q in range(4):
            t = b * 4 + q
            near = near_ref[pl.ds(pl.multiple_of(t * NROW, NROW), NROW), :].astype(bf16)
            near16_ref[pl.ds(pl.multiple_of(t * 128, 128), 128), :] = jnp.concatenate(
                [jnp.zeros((96, TILE), bf16), near], axis=0
            )
            count = counts_ref[t]
            for d in range(K // 2):
                second = jnp.where(2 * d + 1 < count, lists_ref[2 * d + 1, t], DUMMY)
                work_ref[n + d] = t * 65536 + lists_ref[2 * d, t] * 256 + second
            n = n + lax.shift_right_logical(count + 1, 1)
        return n

    count = lax.fori_loop(0, NT // 4, prepare, jnp.int32(0), unroll=4)
    for d in range(GROUP):
        work_ref[count + d] = NT * 65536 + DUMMY
    steps = lax.div(count + (GROUP - 1), GROUP)
    work_ref[SLOTS - 1] = steps
    interior_steps(
        0, jnp.maximum(steps - LATER, 0), work_ref, near16_ref, turned_ref, value16_ref, acc_ref
    )


def second_kernel(work_ref, near_ref, turned_ref, value_ref, before_ref, acc_ref):
    acc_ref[...] = before_ref[...]
    steps = work_ref[SLOTS - 1]
    interior_steps(
        jnp.maximum(steps - LATER, 0), steps, work_ref, near_ref, turned_ref, value_ref, acc_ref
    )


def add_ghosts(ghost_ref, near_ref, faces, acc_ref, far_ref, turned_ref, value_ref, value16_ref):
    x, y = lax.axis_index("gx"), lax.axis_index("gy")
    beside = (x > 0, x < lax.axis_size("gx") - 1, y > 0, y < lax.axis_size("gy") - 1)
    columns = [jnp.concatenate([ref[k] for ref in faces], axis=0) for k in range(7)]
    living = jnp.concatenate([jnp.where(beside[f], ref[7], 0.0) for f, ref in enumerate(faces)], axis=0)
    zero = jnp.zeros((4 * FACE, TILE), f32)
    for k, row in enumerate(far_rows(columns) + [zero] * 2):
        far_ref[pl.ds(k, 4 * FACE, stride=NROW), :] = row
    for k, row in enumerate(value_rows(columns, living) + [zero] * 6):
        value_ref[pl.ds(k, 4 * FACE, stride=VROW), :] = row
    value16_ref[...] = value_ref[...].astype(bf16)
    for b in range(FACE):
        turned_ref[b * 128 : (b + 1) * 128, :] = far_ref[b * 128 : (b + 1) * 128, :].T.astype(bf16)
    blank = jnp.zeros((VROW, TILE), bf16)

    def near_block(t, s):
        start = t * 128 + 96 - NROW * (s % 4)
        return near_ref[start : start + 128, :]

    def far_block(s):
        return turned_ref[s // 4 * 128 : (s // 4 + 1) * 128, :]

    def value_block(s):
        return value16_ref[s * VROW : (s + 1) * VROW, :]

    for face in range(4):
        for place in range(0, GB, 2):
            t, s = face * GB + place, face * FACE + place
            total = pair_sums(
                jnp.concatenate([far_block(s), far_block(s + 1)], axis=1),
                two_near(near_block(t, s), near_block(t + 1, s + 1)),
                jnp.concatenate(
                    [
                        jnp.concatenate([value_block(s), blank], axis=1),
                        jnp.concatenate([blank, value_block(s + 1)], axis=1),
                    ],
                    axis=0,
                ),
            )
            for k in range(2):
                alive = jnp.where(place + k < ghost_ref[face], 1.0, 0.0)
                acc_ref[(t + k) * VROW : (t + k + 1) * VROW, :] += total[k * VROW : (k + 1) * VROW] * alive


def last_kernel(
    ghost_ref, state_ref, cell_ref, near_ref, before_ref, own_ref, mine_ref,
    xlow_ref, xhigh_ref, ylow_ref, yhigh_ref, below_ref, above_ref, far_below_ref, far_above_ref,
    new_ref, fluid_ref,
    table_ref, acc_ref, far_ref, turned_ref, value_ref, value16_ref,
):
    acc_ref[...] = before_ref[...]
    add_ghosts(
        ghost_ref, near_ref, (xlow_ref, xhigh_ref, ylow_ref, yhigh_ref), acc_ref,
        far_ref, turned_ref, value_ref, value16_ref,
    )
    slab = own_ref.shape[1]
    wide = 3 * slab
    z, count = lax.axis_index("gz"), lax.axis_size("gz")
    first_row = (z - 1) * slab

    def inside(flag, value):
        return jnp.where(flag, value, 0.0)

    has_below, has_above = z >= 1, z <= count - 2
    has_far_below, has_far_above = z >= 2, z <= count - 3

    def solved(total):
        return [total[c] / total[3] for c in range(3)]

    here = solved([
        own_ref[c] + inside(has_below, below_ref[4 + c]) + inside(has_above, above_ref[4 + c]) for c in range(4)
    ])
    lower = solved([
        jnp.where(has_below, below_ref[c], 1.0) + mine_ref[c] + inside(has_far_below, far_below_ref[c]) for c in range(4)
    ])
    upper = solved([
        jnp.where(has_above, above_ref[c], 1.0) + mine_ref[4 + c] + inside(has_far_above, far_above_ref[c]) for c in range(4)
    ])
    for c in range(3):
        fluid_ref[c] = here[c]
        table_ref[pl.ds(c * wide, slab), :] = lower[c]
        table_ref[pl.ds(c * wide + slab, slab), :] = here[c]
        table_ref[pl.ds(c * wide + 2 * slab, slab), :] = upper[c]

    def update_group(group, carry):
        rows = pl.ds(pl.multiple_of(group * 8, 8), 8)

        def sums(k):
            return acc_ref[pl.ds(group * 8 * VROW + k, 8, stride=VROW), :]

        weight = sums(9)
        cells = cell_ref[rows, :]
        high = lax.shift_right_logical(cells, 7) - first_row
        low = jnp.bitwise_and(cells, LANES - 1)
        at_cell = [jnp.zeros((8, LANES), f32)] * 3
        for h in range(wide):
            chosen = high == h
            for c in range(3):
                line = jnp.broadcast_to(table_ref[c * wide + h : c * wide + h + 1, :], (8, LANES))
                taken = jnp.take_along_axis(line, low, axis=1, mode="promise_in_bounds")
                at_cell[c] = jnp.where(chosen, taken, at_cell[c])
        r = state_ref[6, rows, :]
        ratio = r / radius_ref
        masses = ratio * ratio * ratio
        rate = drag_coef * r * r
        coupling = time_step * rate / masses
        for c in range(3):
            velocity = state_ref[3 + c, rows, :]
            lever = velocity - spring * centred(state_ref[c, rows, :])
            force = -damping * (lever * weight - (sums(c) + sums(3 + c) + sums(6 + c)))
            moved = velocity + time_step * force / masses
            new_ref[c, rows, :] = (moved + coupling * at_cell[c]) / (1.0 + coupling)
        return carry

    lax.fori_loop(0, NT // 8, update_group, 0, unroll=2)


def shifted(value, axis, steps):
    count = lax.axis_size(axis)
    return lax.ppermute(value, axis, [(i, (i + steps) % count) for i in range(count)])


vmem = pl.BlockSpec(memory_space=pltpu.VMEM)
hbm = pl.BlockSpec(memory_space=pl.ANY)
smem = pl.BlockSpec(memory_space=pltpu.SMEM)
roomy = pltpu.CompilerParams(vmem_limit_bytes=24 * 2**20)


def body(state, tile_lists, tile_counts, ghost_counts, cell_index, fluid_vel, fluid_frac):
    particles = state.shape[3]
    cell_count = fluid_vel.shape[3]
    slab = cell_count // LANES
    tiles = state.reshape(7, NT, TILE)
    cells = cell_index.reshape(NT, TILE)
    lists = tile_lists.reshape(NT, K).T
    counts = tile_counts.reshape(NT)
    ghosts = ghost_counts.reshape(4)

    def shape(*dims):
        return jax.ShapeDtypeStruct(dims, f32)

    face = shape(8, FACE, TILE)
    (
        up, down, far_up, far_down, own, mine, x_up, x_down, y_up, y_down, near, turned, value, sums, work
    ) = pl.pallas_call(
        first_kernel,
        out_shape=(
            shape(8, slab, LANES), shape(8, slab, LANES), shape(4, slab, LANES), shape(4, slab, LANES),
            shape(4, slab, LANES), shape(8, slab, LANES), face, face, face, face,
            jax.ShapeDtypeStruct((NT * 128 + 128, TILE), bf16),
            jax.ShapeDtypeStruct((NT * NROW, TILE), bf16),
            jax.ShapeDtypeStruct(((NT + 1) * VROW, TILE), bf16),
            shape((NT + 1) * VROW, TILE),
            jax.ShapeDtypeStruct((SLOTS,), jnp.int32),
        ),
        in_specs=[hbm] * 4 + [smem] * 3,
        out_specs=(vmem,) * 14 + (smem,),
        scratch_shapes=[
            pltpu.VMEM((7, NT, TILE), f32),
            pltpu.VMEM((NT, TILE), jnp.int32),
            pltpu.VMEM((3, slab, LANES), f32),
            pltpu.VMEM((slab, LANES), f32),
            pltpu.VMEM((8 * NT, TILE), f32),
            pltpu.VMEM((2, 12 * slab, LANES), f32),
            pltpu.VMEM((3 * slab, LANES), f32),
            pltpu.VMEM((NT * NROW, TILE), f32),
            pltpu.VMEM((NT * NROW, TILE), f32),
            pltpu.VMEM((NT * VROW, TILE), f32),
            pltpu.SemaphoreType.DMA((4,)),
        ],
        compiler_params=roomy,
        name="first",
    )(
        tiles, cells, fluid_vel.reshape(3, slab, LANES), fluid_frac.reshape(slab, LANES), lists, counts, ghosts
    )

    if lax.axis_size("gy") == 2:
        y_low = y_high = shifted(jnp.where(lax.axis_index("gy") == 0, y_up, y_down), "gy", 1)
    else:
        y_low, y_high = shifted(y_up, "gy", 1), shifted(y_down, "gy", -1)
    x_low, x_high = shifted(x_up, "gx", 1), shifted(x_down, "gx", -1)
    below, above = shifted(up, "gz", 1), shifted(down, "gz", -1)
    depth = lax.axis_size("gz")
    if depth == 4:
        far_below = far_above = shifted(jnp.where(lax.axis_index("gz") < 2, far_up, far_down), "gz", 2)
    else:
        far_below, far_above = shifted(far_up, "gz", 2), shifted(far_down, "gz", -2)

    sums = pl.pallas_call(
        second_kernel,
        out_shape=shape((NT + 1) * VROW, TILE),
        in_specs=[smem] + [vmem] * 4,
        out_specs=vmem,
        compiler_params=roomy,
        name="second",
    )(work, near, turned, value, sums)

    velocity_new, fluid_new = pl.pallas_call(
        last_kernel,
        out_shape=(shape(3, NT, TILE), shape(3, slab, LANES)),
        in_specs=[smem] + [vmem] * 14,
        out_specs=(vmem, vmem),
        scratch_shapes=[
            pltpu.VMEM((9 * slab, LANES), f32),
            pltpu.VMEM(((NT + 1) * VROW, TILE), f32),
            pltpu.VMEM((4 * FACE * NROW, TILE), f32),
            pltpu.VMEM((4 * FACE * NROW, TILE), bf16),
            pltpu.VMEM((4 * FACE * VROW, TILE), f32),
            pltpu.VMEM((4 * FACE * VROW, TILE), bf16),
        ],
        compiler_params=roomy,
        name="last",
    )(
        ghosts, tiles, cells, near, sums, own, mine, x_low, x_high, y_low, y_high, below, above, far_below, far_above
    )
    return velocity_new.reshape(3, 1, 1, particles), fluid_new.reshape(3, 1, 1, cell_count)


def solution(mesh):
    return jax.shard_map(
        body,
        mesh=mesh,
        in_specs=(
            P(None, "gx", "gy", "gz"),
            P("gx", "gy", "gz", None),
            P("gx", "gy", "gz"),
            P("gx", "gy", "gz", None),
            P("gx", "gy", "gz"),
            P(None, "gx", "gy", "gz"),
            P("gx", "gy", "gz"),
        ),
        out_specs=(P(None, "gx", "gy", "gz"), P(None, "gx", "gy", "gz")),
        check_vma=False,
    )
```

```python
import jax
import jax.numpy as jnp
from jax import lax
from jax.experimental import pallas as pl
from jax.experimental.pallas import tpu as pltpu
from jax.sharding import PartitionSpec as P

TILE = 128
K = 8
NT = 64
GB = 12
FACE = 16
LANES = 128

stiffness = 5.0
damping = 2.0
time_step = 0.25
drag_coef = 64.0
fluid_density = 2.0
radius_ref = 0.25
spring = stiffness / damping

f32 = jnp.float32
bf16 = jnp.bfloat16

NROW = 32
VROW = 16
DUMMY = NT
GROUP = 16
LATER = 4
SLOTS = NT * 5


def parts_of(q):
    first = q.astype(bf16).astype(f32)
    rest = q - first
    second = rest.astype(bf16).astype(f32)
    return first, second, (rest - second).astype(bf16).astype(f32)


ORDER = ((0, 0), (0, 1), (0, 2), (1, 0), (1, 1), (2, 0))


def centred(position):
    return position - 0.5


def geometry(columns):
    x, y, z = (centred(columns[k]) for k in range(3))
    r = columns[6]
    return (x, y, z, r), r * r - (x * x + y * y + z * z)


def near_rows(columns):
    lengths, own = geometry(columns)
    one = jnp.ones_like(own)
    rows = []
    for q in lengths:
        cut = parts_of(q)
        rows += [2.0 * cut[j] for _, j in ORDER]
    return rows + [one] * 3 + list(parts_of(own))


def far_rows(columns):
    lengths, own = geometry(columns)
    one = jnp.ones_like(own)
    rows = []
    for q in lengths:
        cut = parts_of(q)
        rows += [cut[i] for i, _ in ORDER]
    return rows + list(parts_of(own)) + [one] * 3


def value_rows(columns, living):
    cuts = [parts_of((columns[3 + c] - spring * centred(columns[c]))) for c in range(3)]
    return [cuts[c][k] * living for k in range(3) for c in range(3)] + [living]


def load(pairs, sems):
    copies = [pltpu.make_async_copy(source, target, sems.at[k]) for k, (source, target) in enumerate(pairs)]
    for copy in copies:
        copy.start()
    return copies


def pair_sums(left, right, values):
    weight = jnp.maximum(jnp.dot(left, right, preferred_element_type=f32), 0.0)
    coarse = weight.astype(bf16)
    fine = (weight - coarse.astype(f32)).astype(bf16)
    weights = jnp.concatenate(
        [
            jnp.concatenate([coarse[:, :TILE], fine[:, :TILE]], axis=1),
            jnp.concatenate([coarse[:, TILE:], fine[:, TILE:]], axis=1),
        ],
        axis=0,
    )
    both = jnp.dot(values, weights, preferred_element_type=f32)
    return both[:, :TILE] + both[:, TILE:]


def two_near(first, second):
    blank = jnp.zeros((128, TILE), bf16)
    return jnp.concatenate(
        [jnp.concatenate([first, blank], axis=1), jnp.concatenate([blank, second], axis=1)], axis=0
    )


def interior_steps(begin, end, work_ref, near_ref, turned_ref, value_ref, acc_ref):
    def near_block(t, s):
        start = t * 128 + 96 - NROW * jnp.bitwise_and(s, 3)
        return near_ref[pl.ds(pl.multiple_of(start, NROW), 128), :]

    def far_block(s):
        return turned_ref[pl.ds(pl.multiple_of(lax.shift_right_logical(s, 2) * 128, 128), 128), :]

    def value_block(s):
        return value_ref[pl.ds(pl.multiple_of(s * VROW, VROW), VROW), :]

    def step(group, carry):
        sums = []
        for d in range(GROUP):
            word = work_ref[group * GROUP + d]
            t = lax.shift_right_logical(word, 16)
            a = jnp.bitwise_and(lax.shift_right_logical(word, 8), 255)
            b = jnp.bitwise_and(word, 255)
            near, far = jnp.minimum(t, NT - 1), jnp.minimum(b, NT - 1)
            total = pair_sums(
                jnp.concatenate([far_block(a), far_block(far)], axis=1),
                two_near(near_block(near, a), near_block(near, far)),
                jnp.concatenate([value_block(a), value_block(b)], axis=1),
            )
            sums.append((t, total))
        for t, total in sums:
            acc_ref[pl.ds(pl.multiple_of(t * VROW, VROW), VROW), :] += total
        return carry

    lax.fori_loop(begin, end, step, 0)


def first_kernel(
    state_hbm, cell_hbm, vel_hbm, frac_hbm, lists_hbm, counts_hbm, ghost_hbm,
    za_ref, zb_ref, far_one_ref, far_two_ref, own_ref, mine_ref, xa_ref, xb_ref, ya_ref, yb_ref,
    state_ref, cell_ref, near16_ref, turned_ref, value16_ref, acc_ref, work_ref,
    vel_ref, frac_ref, source_ref, deposit_ref, total_ref, near_ref, far_ref, value_ref,
    lists_ref, counts_ref, ghost_ref, sems,
):
    copies = load(
        [
            (state_hbm, state_ref), (cell_hbm, cell_ref), (vel_hbm, vel_ref), (frac_hbm, frac_ref),
            (lists_hbm, lists_ref), (counts_hbm, counts_ref), (ghost_hbm, ghost_ref),
        ],
        sems,
    )
    acc_ref[...] = jnp.zeros_like(acc_ref)
    value16_ref[pl.ds(DUMMY * VROW, VROW), :] = jnp.zeros((VROW, TILE), bf16)
    near16_ref[pl.ds(NT * 128, 128), :] = jnp.zeros((128, TILE), bf16)
    slab = vel_ref.shape[1]
    wide = 3 * slab
    bands = wide // 2
    z = lax.axis_index("gz")
    even_x, even_y, even_z = (jnp.bitwise_and(lax.axis_index(axis), 1) == 0 for axis in ("gx", "gy", "gz"))
    lower_half = z < lax.axis_size("gz") // 2
    first_band = (z - 1) * (slab // 2)
    for copy in copies:
        copy.wait()

    r = state_ref[6]
    rate = drag_coef * r * r
    sources = [rate * state_ref[3 + c] for c in range(3)] + [rate]
    for c, source in enumerate(sources):
        for k, part in enumerate(parts_of(source)[:2]):
            source_ref[pl.ds(4 * k + c, NT, stride=8), :] = part
    low_of = lax.broadcasted_iota(jnp.int32, (2 * LANES, LANES), 0)

    def add_group(group, total):
        cells = cell_ref[pl.ds(pl.multiple_of(group * 8, 8), 8), :]
        band = lax.shift_right_logical(cells, 8) - first_band
        low = jnp.bitwise_and(cells, 255)
        left, right = [], []
        for t in range(8):
            rows = source_ref[pl.ds(pl.multiple_of(group * 64 + t * 8, 8), 8), :]
            here = jnp.broadcast_to(band[t : t + 1, :], (8, LANES))
            left.append(jnp.concatenate([jnp.where(here == h, rows, 0.0) for h in range(bands)], axis=0).astype(bf16))
            right.append(jnp.where(low[t : t + 1, :] == low_of, 1.0, 0.0).astype(bf16))
        added = lax.dot_general(
            jnp.concatenate(left, axis=1),
            jnp.concatenate(right, axis=1),
            (((1,), (1,)), ((), ())),
            preferred_element_type=f32,
        )
        deposit_ref[0] += added[:, :LANES]
        deposit_ref[1] += added[:, LANES:]
        return total

    deposit_ref[...] = jnp.zeros_like(deposit_ref)
    lax.fori_loop(0, NT // 8, add_group, 0, unroll=2)
    frac = fluid_density * frac_ref[...]
    for c in range(4):
        for k in range(2):
            both = deposit_ref[k, pl.ds(c, bands, stride=8), :] + deposit_ref[k, pl.ds(4 + c, bands, stride=8), :]
            total_ref[pl.ds(k, bands, stride=2), :] = both * time_step
        below, here, above = (total_ref[pl.ds(k * slab, slab), :] for k in range(3))
        own = here + (frac * vel_ref[c] if c < 3 else frac)
        own_ref[c] = own
        mine_ref[c] = below
        mine_ref[4 + c] = above
        za_ref[c] = own
        zb_ref[c] = own
        za_ref[4 + c] = jnp.where(even_z, above, below)
        zb_ref[4 + c] = jnp.where(even_z, below, above)
        if lax.axis_size("gz") == 4:
            far_one_ref[c] = jnp.where(lower_half, above, below)
            far_two_ref[c] = below
        else:
            far_one_ref[c] = above
            far_two_ref[c] = below
    order = lax.broadcasted_iota(jnp.int32, (FACE, TILE), 0)
    for low, even, a_ref, b_ref in ((0, even_x, xa_ref, xb_ref), (2, even_y, ya_ref, yb_ref)):
        for k in range(7):
            lower = state_ref[k, low * GB : (low + 1) * GB, :]
            upper = state_ref[k, (low + 1) * GB : (low + 2) * GB, :]
            a_ref[k, 0:GB, :] = jnp.where(even, upper, lower)
            b_ref[k, 0:GB, :] = jnp.where(even, lower, upper)
            a_ref[k, GB:FACE, :] = jnp.zeros((FACE - GB, TILE), f32)
            b_ref[k, GB:FACE, :] = jnp.zeros((FACE - GB, TILE), f32)
        lower, upper = ghost_ref[low], ghost_ref[low + 1]
        a_ref[7] = jnp.where(order < jnp.where(even, upper, lower), 1.0, 0.0)
        b_ref[7] = jnp.where(order < jnp.where(even, lower, upper), 1.0, 0.0)

    columns = [state_ref[k] for k in range(7)]
    zero = jnp.zeros((NT, TILE), f32)
    one = jnp.ones((NT, TILE), f32)
    for k, row in enumerate(near_rows(columns) + [zero] * 2):
        near_ref[pl.ds(k, NT, stride=NROW), :] = row
    for k, row in enumerate(far_rows(columns) + [zero] * 2):
        far_ref[pl.ds(k, NT, stride=NROW), :] = row
    for k, row in enumerate(value_rows(columns, one) + [zero] * 6):
        value_ref[pl.ds(k, NT, stride=VROW), :] = row

    def prepare(b, n):
        rows = pl.ds(pl.multiple_of(b * 128, 128), 128)
        turned_ref[rows, :] = far_ref[rows, :].T.astype(bf16)
        rows = pl.ds(pl.multiple_of(b * 4 * VROW, 4 * VROW), 4 * VROW)
        value16_ref[rows, :] = value_ref[rows, :].astype(bf16)
        for q in range(4):
            t = b * 4 + q
            near = near_ref[pl.ds(pl.multiple_of(t * NROW, NROW), NROW), :].astype(bf16)
            near16_ref[pl.ds(pl.multiple_of(t * 128, 128), 128), :] = jnp.concatenate(
                [jnp.zeros((96, TILE), bf16), near], axis=0
            )
            count = counts_ref[t]
            for d in range(K // 2):
                second = jnp.where(2 * d + 1 < count, lists_ref[2 * d + 1, t], DUMMY)
                work_ref[n + d] = t * 65536 + lists_ref[2 * d, t] * 256 + second
            n = n + lax.shift_right_logical(count + 1, 1)
        return n

    count = lax.fori_loop(0, NT // 4, prepare, jnp.int32(0), unroll=4)
    for d in range(GROUP):
        work_ref[count + d] = NT * 65536 + DUMMY
    steps = lax.div(count + (GROUP - 1), GROUP)
    work_ref[SLOTS - 1] = steps
    for f in range(4):
        work_ref[SLOTS - 5 + f] = ghost_ref[f]
    interior_steps(
        0, jnp.maximum(steps - LATER, 0), work_ref, near16_ref, turned_ref, value16_ref, acc_ref
    )


def second_kernel(work_ref, near_ref, turned_ref, value_ref, before_ref, acc_ref):
    acc_ref[...] = before_ref[...]
    steps = work_ref[SLOTS - 1]
    interior_steps(
        jnp.maximum(steps - LATER, 0), steps, work_ref, near_ref, turned_ref, value_ref, acc_ref
    )


def ghost_sums(work_ref, near_ref, faces, sums_ref, far_ref, turned_ref, value_ref, value16_ref):
    x, y = lax.axis_index("gx"), lax.axis_index("gy")
    beside = (x > 0, x < lax.axis_size("gx") - 1, y > 0, y < lax.axis_size("gy") - 1)
    got = []
    for place, (a_ref, b_ref) in zip((x, y), faces):
        even = jnp.bitwise_and(place, 1) == 0
        a, b = ([ref[k] for k in range(8)] for ref in (a_ref, b_ref))
        got.append([jnp.where(even, q, p) for p, q in zip(a, b)])
        got.append([jnp.where(even, p, q) for p, q in zip(a, b)])
    columns = [jnp.concatenate([face[k] for face in got], axis=0) for k in range(7)]
    living = jnp.concatenate([jnp.where(beside[f], face[7], 0.0) for f, face in enumerate(got)], axis=0)
    zero = jnp.zeros((4 * FACE, TILE), f32)
    for k, row in enumerate(far_rows(columns) + [zero] * 2):
        far_ref[pl.ds(k, 4 * FACE, stride=NROW), :] = row
    for k, row in enumerate(value_rows(columns, living) + [zero] * 6):
        value_ref[pl.ds(k, 4 * FACE, stride=VROW), :] = row
    value16_ref[...] = value_ref[...].astype(bf16)
    for b in range(FACE):
        turned_ref[b * 128 : (b + 1) * 128, :] = far_ref[b * 128 : (b + 1) * 128, :].T.astype(bf16)
    blank = jnp.zeros((VROW, TILE), bf16)

    def near_block(t, s):
        start = t * 128 + 96 - NROW * (s % 4)
        return near_ref[start : start + 128, :]

    def far_block(s):
        return turned_ref[s // 4 * 128 : (s // 4 + 1) * 128, :]

    def value_block(s):
        return value16_ref[s * VROW : (s + 1) * VROW, :]

    for face in range(4):
        for place in range(0, GB, 2):
            t, s = face * GB + place, face * FACE + place
            total = pair_sums(
                jnp.concatenate([far_block(s), far_block(s + 1)], axis=1),
                two_near(near_block(t, s), near_block(t + 1, s + 1)),
                jnp.concatenate(
                    [
                        jnp.concatenate([value_block(s), blank], axis=1),
                        jnp.concatenate([blank, value_block(s + 1)], axis=1),
                    ],
                    axis=0,
                ),
            )
            for k in range(2):
                alive = jnp.where(place + k < work_ref[SLOTS - 5 + face], 1.0, 0.0)
                sums_ref[(t + k) * VROW : (t + k + 1) * VROW, :] = total[k * VROW : (k + 1) * VROW] * alive


def last_kernel(
    work_ref, state_ref, cell_ref, near_ref, acc_ref, own_ref, mine_ref,
    xa_ref, xb_ref, ya_ref, yb_ref, za_ref, zb_ref, far_below_ref, far_above_ref,
    new_ref, fluid_ref,
    table_ref, sums_ref, far_ref, turned_ref, value_ref, value16_ref,
):
    ghost_sums(
        work_ref, near_ref, ((xa_ref, xb_ref), (ya_ref, yb_ref)), sums_ref, far_ref, turned_ref, value_ref, value16_ref
    )
    sums_ref[pl.ds(4 * GB * VROW, (NT - 4 * GB) * VROW), :] = jnp.zeros(((NT - 4 * GB) * VROW, TILE), f32)
    slab = own_ref.shape[1]
    wide = 3 * slab
    z, count = lax.axis_index("gz"), lax.axis_size("gz")
    first_row = (z - 1) * slab

    def inside(flag, value):
        return jnp.where(flag, value, 0.0)

    even = jnp.bitwise_and(z, 1) == 0
    below = [jnp.where(even, zb_ref[c], za_ref[c]) for c in range(8)]
    above = [jnp.where(even, za_ref[c], zb_ref[c]) for c in range(8)]
    has_below, has_above = z >= 1, z <= count - 2
    has_far_below, has_far_above = z >= 2, z <= count - 3

    def solved(total):
        return [total[c] / total[3] for c in range(3)]

    here = solved([
        own_ref[c] + inside(has_below, below[4 + c]) + inside(has_above, above[4 + c]) for c in range(4)
    ])
    lower = solved([
        jnp.where(has_below, below[c], 1.0) + mine_ref[c] + inside(has_far_below, far_below_ref[c]) for c in range(4)
    ])
    upper = solved([
        jnp.where(has_above, above[c], 1.0) + mine_ref[4 + c] + inside(has_far_above, far_above_ref[c]) for c in range(4)
    ])
    for c in range(3):
        fluid_ref[c] = here[c]
        table_ref[pl.ds(c * wide, slab), :] = lower[c]
        table_ref[pl.ds(c * wide + slab, slab), :] = here[c]
        table_ref[pl.ds(c * wide + 2 * slab, slab), :] = upper[c]

    def update_group(group, carry):
        rows = pl.ds(pl.multiple_of(group * 8, 8), 8)

        def sums(k):
            at = pl.ds(group * 8 * VROW + k, 8, stride=VROW)
            return acc_ref[at, :] + sums_ref[at, :]

        weight = sums(9)
        cells = cell_ref[rows, :]
        high = lax.shift_right_logical(cells, 7) - first_row
        low = jnp.bitwise_and(cells, LANES - 1)
        at_cell = [jnp.zeros((8, LANES), f32)] * 3
        for h in range(wide):
            chosen = high == h
            for c in range(3):
                line = jnp.broadcast_to(table_ref[c * wide + h : c * wide + h + 1, :], (8, LANES))
                taken = jnp.take_along_axis(line, low, axis=1, mode="promise_in_bounds")
                at_cell[c] = jnp.where(chosen, taken, at_cell[c])
        r = state_ref[6, rows, :]
        ratio = r / radius_ref
        masses = ratio * ratio * ratio
        rate = drag_coef * r * r
        coupling = time_step * rate / masses
        for c in range(3):
            velocity = state_ref[3 + c, rows, :]
            lever = velocity - spring * centred(state_ref[c, rows, :])
            force = -damping * (lever * weight - (sums(c) + sums(3 + c) + sums(6 + c)))
            moved = velocity + time_step * force / masses
            new_ref[c, rows, :] = (moved + coupling * at_cell[c]) / (1.0 + coupling)
        return carry

    lax.fori_loop(0, NT // 8, update_group, 0, unroll=2)


def shifted(value, axis, steps):
    count = lax.axis_size(axis)
    return lax.ppermute(value, axis, [(i, (i + steps) % count) for i in range(count)])


def swapped(first, second, axis):
    count = lax.axis_size(axis)
    first = lax.ppermute(first, axis, [(i, i ^ 1) for i in range(count)])
    if count == 2:
        return first, first
    return first, lax.ppermute(second, axis, [(i, (i + (1 if i % 2 else -1)) % count) for i in range(count)])


vmem = pl.BlockSpec(memory_space=pltpu.VMEM)
hbm = pl.BlockSpec(memory_space=pltpu.HBM)
smem = pl.BlockSpec(memory_space=pltpu.SMEM)
roomy = pltpu.CompilerParams(vmem_limit_bytes=24 * 2**20)


def body(state, tile_lists, tile_counts, ghost_counts, cell_index, fluid_vel, fluid_frac):
    particles = state.shape[3]
    cell_count = fluid_vel.shape[3]
    slab = cell_count // LANES
    tiles = state.reshape(7, NT, TILE)
    cells = cell_index.reshape(NT, TILE)
    lists = tile_lists.reshape(NT, K).T
    counts = tile_counts.reshape(NT)
    ghosts = ghost_counts.reshape(4)

    def shape(*dims):
        return jax.ShapeDtypeStruct(dims, f32)

    face = shape(8, FACE, TILE)
    (
        za, zb, far_one, far_two, own, mine, xa, xb, ya, yb, held, held_cells, near, turned, value, sums, work
    ) = pl.pallas_call(
        first_kernel,
        out_shape=(
            shape(8, slab, LANES), shape(8, slab, LANES), shape(4, slab, LANES), shape(4, slab, LANES),
            shape(4, slab, LANES), shape(8, slab, LANES), face, face, face, face,
            shape(7, NT, TILE),
            jax.ShapeDtypeStruct((NT, TILE), jnp.int32),
            jax.ShapeDtypeStruct((NT * 128 + 128, TILE), bf16),
            jax.ShapeDtypeStruct((NT * NROW, TILE), bf16),
            jax.ShapeDtypeStruct(((NT + 1) * VROW, TILE), bf16),
            shape((NT + 1) * VROW, TILE),
            jax.ShapeDtypeStruct((SLOTS,), jnp.int32),
        ),
        in_specs=[hbm] * 7,
        out_specs=(vmem,) * 16 + (smem,),
        scratch_shapes=[
            pltpu.VMEM((3, slab, LANES), f32),
            pltpu.VMEM((slab, LANES), f32),
            pltpu.VMEM((8 * NT, TILE), f32),
            pltpu.VMEM((2, 12 * slab, LANES), f32),
            pltpu.VMEM((3 * slab, LANES), f32),
            pltpu.VMEM((NT * NROW, TILE), f32),
            pltpu.VMEM((NT * NROW, TILE), f32),
            pltpu.VMEM((NT * VROW, TILE), f32),
            pltpu.SMEM((K, NT), jnp.int32),
            pltpu.SMEM((NT,), jnp.int32),
            pltpu.SMEM((4,), jnp.int32),
            pltpu.SemaphoreType.DMA((7,)),
        ],
        compiler_params=roomy,
        name="first",
    )(
        *(
            pltpu.with_memory_space_constraint(value, pltpu.HBM)
            for value in (
                tiles, cells, fluid_vel.reshape(3, slab, LANES), fluid_frac.reshape(slab, LANES), lists, counts, ghosts
            )
        )
    )

    ya, yb = swapped(ya, yb, "gy")
    xa, xb = swapped(xa, xb, "gx")
    za, zb = swapped(za, zb, "gz")
    if lax.axis_size("gz") == 4:
        far_below = far_above = shifted(far_one, "gz", 2)
    else:
        far_below, far_above = shifted(far_one, "gz", 2), shifted(far_two, "gz", -2)

    sums = pl.pallas_call(
        second_kernel,
        out_shape=shape((NT + 1) * VROW, TILE),
        in_specs=[smem] + [vmem] * 4,
        out_specs=vmem,
        compiler_params=roomy,
        name="second",
    )(work, near, turned, value, sums)

    velocity_new, fluid_new = pl.pallas_call(
        last_kernel,
        out_shape=(shape(3, NT, TILE), shape(3, slab, LANES)),
        in_specs=[smem] + [vmem] * 14,
        out_specs=(vmem, vmem),
        scratch_shapes=[
            pltpu.VMEM((9 * slab, LANES), f32),
            pltpu.VMEM((NT * VROW, TILE), f32),
            pltpu.VMEM((4 * FACE * NROW, TILE), f32),
            pltpu.VMEM((4 * FACE * NROW, TILE), bf16),
            pltpu.VMEM((4 * FACE * VROW, TILE), f32),
            pltpu.VMEM((4 * FACE * VROW, TILE), bf16),
        ],
        compiler_params=roomy,
        name="last",
    )(
        work, held, held_cells, near, sums, own, mine, xa, xb, ya, yb, za, zb, far_below, far_above
    )
    return velocity_new.reshape(3, 1, 1, particles), fluid_new.reshape(3, 1, 1, cell_count)


def solution(mesh):
    return jax.shard_map(
        body,
        mesh=mesh,
        in_specs=(
            P(None, "gx", "gy", "gz"),
            P("gx", "gy", "gz", None),
            P("gx", "gy", "gz"),
            P("gx", "gy", "gz", None),
            P("gx", "gy", "gz"),
            P(None, "gx", "gy", "gz"),
            P("gx", "gy", "gz"),
        ),
        out_specs=(P(None, "gx", "gy", "gz"), P(None, "gx", "gy", "gz")),
        check_vma=False,
    )
```

```python
import jax
import jax.numpy as jnp
from jax import lax
from jax.experimental import pallas as pl
from jax.experimental.pallas import tpu as pltpu
from jax.sharding import PartitionSpec as P

TILE = 128
K = 8
NT = 64
GB = 12
FACE = 16
LANES = 128

stiffness = 5.0
damping = 2.0
time_step = 0.25
drag_coef = 64.0
fluid_density = 2.0
radius_ref = 0.25
spring = stiffness / damping

f32 = jnp.float32
bf16 = jnp.bfloat16

NROW = 32
VROW = 16
DUMMY = NT
GROUP = 16
WIDE = 32
EARLY = 1
KEPT = 64
SLOTS = NT * 5


def parts_of(q):
    first = q.astype(bf16).astype(f32)
    rest = q - first
    second = rest.astype(bf16).astype(f32)
    return first, second, (rest - second).astype(bf16).astype(f32)


ORDER = ((0, 0), (0, 1), (0, 2), (1, 0), (1, 1), (2, 0))


def centred(position):
    return position - 0.5


def geometry(columns):
    x, y, z = (centred(columns[k]) for k in range(3))
    r = columns[6]
    return (x, y, z, r), r * r - (x * x + y * y + z * z)


def near_rows(columns):
    lengths, own = geometry(columns)
    one = jnp.ones_like(own)
    rows = []
    for q in lengths:
        cut = parts_of(q)
        rows += [2.0 * cut[j] for _, j in ORDER]
    return rows + [one] * 3 + list(parts_of(own))


def far_rows(columns):
    lengths, own = geometry(columns)
    one = jnp.ones_like(own)
    rows = []
    for q in lengths:
        cut = parts_of(q)
        rows += [cut[i] for i, _ in ORDER]
    return rows + list(parts_of(own)) + [one] * 3


def value_rows(columns, living):
    cuts = [parts_of((columns[3 + c] - spring * centred(columns[c]))) for c in range(3)]
    return [cuts[c][k] * living for k in range(3) for c in range(3)] + [living]


def load(pairs, sems):
    copies = [pltpu.make_async_copy(source, target, sems.at[k]) for k, (source, target) in enumerate(pairs)]
    for copy in copies:
        copy.start()
    return copies


def pair_sums(far, near, values):
    weight = jnp.concatenate(
        [jnp.dot(left, right, preferred_element_type=f32) for left, right in zip(far, near)], axis=0
    )
    weight = jnp.maximum(weight, 0.0)
    coarse = weight.astype(bf16)
    fine = (weight - coarse.astype(f32)).astype(bf16)
    both = jnp.dot(values, jnp.concatenate([coarse, fine], axis=1), preferred_element_type=f32)
    return both[:, :TILE] + both[:, TILE:]


def interior_steps(begin, steps, size, work_ref, near_ref, turned_ref, value_ref, acc_ref):
    def near_block(t, s):
        start = t * 128 + 96 - NROW * jnp.bitwise_and(s, 3)
        return near_ref[pl.ds(pl.multiple_of(start, NROW), 128), :]

    def far_block(s):
        return turned_ref[pl.ds(pl.multiple_of(lax.shift_right_logical(s, 2) * 128, 128), 128), :]

    def value_block(s):
        return value_ref[pl.ds(pl.multiple_of(s * VROW, VROW), VROW), :]

    def step(group, carry):
        sums = []
        for d in range(size):
            word = work_ref[begin + group * size + d]
            t = lax.shift_right_logical(word, 16)
            a = jnp.bitwise_and(lax.shift_right_logical(word, 8), 255)
            b = jnp.bitwise_and(word, 255)
            near, far = jnp.minimum(t, NT - 1), jnp.minimum(b, NT - 1)
            total = pair_sums(
                (far_block(a), far_block(far)),
                (near_block(near, a), near_block(near, far)),
                jnp.concatenate([value_block(a), value_block(b)], axis=1),
            )
            sums.append((t, total))
        for t, total in sums:
            acc_ref[pl.ds(pl.multiple_of(t * VROW, VROW), VROW), :] += total
        return carry

    lax.fori_loop(0, steps, step, 0)


def first_kernel(
    state_hbm, cell_hbm, vel_hbm, frac_hbm, lists_hbm, counts_hbm, ghost_hbm,
    za_ref, zb_ref, far_one_ref, far_two_ref, own_ref, mine_ref, xa_ref, xb_ref, ya_ref, yb_ref,
    state_ref, cell_ref, near16_ref, turned_ref, value16_ref, acc_ref, work_ref,
    vel_ref, frac_ref, source_ref, deposit_ref, total_ref, near_ref, far_ref, value_ref,
    lists_ref, counts_ref, ghost_ref, sems,
):
    copies = load(
        [
            (state_hbm, state_ref), (cell_hbm, cell_ref), (vel_hbm, vel_ref), (frac_hbm, frac_ref),
            (lists_hbm, lists_ref), (counts_hbm, counts_ref), (ghost_hbm, ghost_ref),
        ],
        sems,
    )
    acc_ref[...] = jnp.zeros_like(acc_ref)
    value16_ref[pl.ds(DUMMY * VROW, VROW), :] = jnp.zeros((VROW, TILE), bf16)
    near16_ref[pl.ds(NT * 128, 128), :] = jnp.zeros((128, TILE), bf16)
    slab = vel_ref.shape[1]
    wide = 3 * slab
    bands = wide // 2
    z = lax.axis_index("gz")
    even_x, even_y, even_z = (jnp.bitwise_and(lax.axis_index(axis), 1) == 0 for axis in ("gx", "gy", "gz"))
    lower_half = z < lax.axis_size("gz") // 2
    first_band = (z - 1) * (slab // 2)
    for copy in copies:
        copy.wait()

    r = state_ref[6]
    rate = drag_coef * r * r
    sources = [rate * state_ref[3 + c] for c in range(3)] + [rate]
    for c, source in enumerate(sources):
        for k, part in enumerate(parts_of(source)[:2]):
            source_ref[pl.ds(4 * k + c, NT, stride=8), :] = part
    low_of = lax.broadcasted_iota(jnp.int32, (2 * LANES, LANES), 0)

    def add_group(group, total):
        cells = cell_ref[pl.ds(pl.multiple_of(group * 8, 8), 8), :]
        band = lax.shift_right_logical(cells, 8) - first_band
        low = jnp.bitwise_and(cells, 255)
        left, right = [], []
        for t in range(8):
            rows = source_ref[pl.ds(pl.multiple_of(group * 64 + t * 8, 8), 8), :]
            here = jnp.broadcast_to(band[t : t + 1, :], (8, LANES))
            left.append(jnp.concatenate([jnp.where(here == h, rows, 0.0) for h in range(bands)], axis=0).astype(bf16))
            right.append(jnp.where(low[t : t + 1, :] == low_of, 1.0, 0.0).astype(bf16))
        added = lax.dot_general(
            jnp.concatenate(left, axis=1),
            jnp.concatenate(right, axis=1),
            (((1,), (1,)), ((), ())),
            preferred_element_type=f32,
        )
        deposit_ref[0] += added[:, :LANES]
        deposit_ref[1] += added[:, LANES:]
        return total

    deposit_ref[...] = jnp.zeros_like(deposit_ref)
    lax.fori_loop(0, NT // 8, add_group, 0, unroll=4)
    frac = fluid_density * frac_ref[...]
    for c in range(4):
        for k in range(2):
            both = deposit_ref[k, pl.ds(c, bands, stride=8), :] + deposit_ref[k, pl.ds(4 + c, bands, stride=8), :]
            total_ref[pl.ds(k, bands, stride=2), :] = both * time_step
        below, here, above = (total_ref[pl.ds(k * slab, slab), :] for k in range(3))
        own = here + (frac * vel_ref[c] if c < 3 else frac)
        own_ref[c] = own
        mine_ref[c] = below
        mine_ref[4 + c] = above
        za_ref[c] = own
        zb_ref[c] = own
        za_ref[4 + c] = jnp.where(even_z, above, below)
        zb_ref[4 + c] = jnp.where(even_z, below, above)
        if lax.axis_size("gz") == 4:
            far_one_ref[c] = jnp.where(lower_half, above, below)
            far_two_ref[c] = below
        else:
            far_one_ref[c] = above
            far_two_ref[c] = below
    order = lax.broadcasted_iota(jnp.int32, (FACE, TILE), 0)
    for low, even, a_ref, b_ref in ((0, even_x, xa_ref, xb_ref), (2, even_y, ya_ref, yb_ref)):
        for k in range(7):
            lower = state_ref[k, low * GB : (low + 1) * GB, :]
            upper = state_ref[k, (low + 1) * GB : (low + 2) * GB, :]
            a_ref[k, 0:GB, :] = jnp.where(even, upper, lower)
            b_ref[k, 0:GB, :] = jnp.where(even, lower, upper)
            a_ref[k, GB:FACE, :] = jnp.zeros((FACE - GB, TILE), f32)
            b_ref[k, GB:FACE, :] = jnp.zeros((FACE - GB, TILE), f32)
        lower, upper = ghost_ref[low], ghost_ref[low + 1]
        a_ref[7] = jnp.where(order < jnp.where(even, upper, lower), 1.0, 0.0)
        b_ref[7] = jnp.where(order < jnp.where(even, lower, upper), 1.0, 0.0)

    columns = [state_ref[k] for k in range(7)]
    zero = jnp.zeros((NT, TILE), f32)
    one = jnp.ones((NT, TILE), f32)
    for k, row in enumerate(near_rows(columns) + [zero] * 2):
        near_ref[pl.ds(k, NT, stride=NROW), :] = row
    for k, row in enumerate(far_rows(columns) + [zero] * 2):
        far_ref[pl.ds(k, NT, stride=NROW), :] = row
    for k, row in enumerate(value_rows(columns, one) + [zero] * 6):
        value_ref[pl.ds(k, NT, stride=VROW), :] = row

    def prepare(b, n):
        rows = pl.ds(pl.multiple_of(b * 128, 128), 128)
        turned_ref[rows, :] = far_ref[rows, :].T.astype(bf16)
        rows = pl.ds(pl.multiple_of(b * 4 * VROW, 4 * VROW), 4 * VROW)
        value16_ref[rows, :] = value_ref[rows, :].astype(bf16)
        for q in range(4):
            t = b * 4 + q
            near = near_ref[pl.ds(pl.multiple_of(t * NROW, NROW), NROW), :].astype(bf16)
            near16_ref[pl.ds(pl.multiple_of(t * 128, 128), 128), :] = jnp.concatenate(
                [jnp.zeros((96, TILE), bf16), near], axis=0
            )
            count = counts_ref[t]
            for d in range(K // 2):
                second = jnp.where(2 * d + 1 < count, lists_ref[2 * d + 1, t], DUMMY)
                work_ref[n + d] = t * 65536 + lists_ref[2 * d, t] * 256 + second
            n = n + lax.shift_right_logical(count + 1, 1)
        return n

    count = lax.fori_loop(0, NT // 4, prepare, jnp.int32(0), unroll=16)
    for d in range(WIDE):
        work_ref[count + d] = NT * 65536 + DUMMY
    ahead = jnp.minimum(jnp.where(z == 0, EARLY, 0), lax.div(jnp.maximum(count - KEPT, 0), GROUP))
    work_ref[SLOTS - 1] = count
    work_ref[SLOTS - 6] = ahead * GROUP
    for f in range(4):
        work_ref[SLOTS - 5 + f] = ghost_ref[f]
    interior_steps(0, ahead, GROUP, work_ref, near16_ref, turned_ref, value16_ref, acc_ref)


def second_kernel(work_ref, near_ref, turned_ref, value_ref, before_ref, acc_ref):
    acc_ref[...] = before_ref[...]
    begin = work_ref[SLOTS - 6]
    left = work_ref[SLOTS - 1] - begin
    wide = lax.div(left + (WIDE - GROUP - 1), WIDE)
    tail = (left > wide * WIDE).astype(jnp.int32)
    refs = (work_ref, near_ref, turned_ref, value_ref, acc_ref)
    interior_steps(begin, wide, WIDE, *refs)
    interior_steps(begin + wide * WIDE, tail, GROUP, *refs)


def ghost_sums(work_ref, near_ref, faces, sums_ref, far_ref, turned_ref, value_ref, value16_ref):
    x, y = lax.axis_index("gx"), lax.axis_index("gy")
    beside = (x > 0, x < lax.axis_size("gx") - 1, y > 0, y < lax.axis_size("gy") - 1)
    got = []
    for place, (a_ref, b_ref) in zip((x, y), faces):
        even = jnp.bitwise_and(place, 1) == 0
        a, b = ([ref[k] for k in range(8)] for ref in (a_ref, b_ref))
        got.append([jnp.where(even, q, p) for p, q in zip(a, b)])
        got.append([jnp.where(even, p, q) for p, q in zip(a, b)])
    columns = [jnp.concatenate([face[k] for face in got], axis=0) for k in range(7)]
    living = jnp.concatenate([jnp.where(beside[f], face[7], 0.0) for f, face in enumerate(got)], axis=0)
    zero = jnp.zeros((4 * FACE, TILE), f32)
    for k, row in enumerate(far_rows(columns) + [zero] * 2):
        far_ref[pl.ds(k, 4 * FACE, stride=NROW), :] = row
    for k, row in enumerate(value_rows(columns, living) + [zero] * 6):
        value_ref[pl.ds(k, 4 * FACE, stride=VROW), :] = row
    value16_ref[...] = value_ref[...].astype(bf16)
    for b in range(FACE):
        turned_ref[b * 128 : (b + 1) * 128, :] = far_ref[b * 128 : (b + 1) * 128, :].T.astype(bf16)
    blank = jnp.zeros((VROW, TILE), bf16)

    def near_block(t, s):
        start = t * 128 + 96 - NROW * (s % 4)
        return near_ref[start : start + 128, :]

    def far_block(s):
        return turned_ref[s // 4 * 128 : (s // 4 + 1) * 128, :]

    def value_block(s):
        return value16_ref[s * VROW : (s + 1) * VROW, :]

    for face in range(4):
        for place in range(0, GB, 2):
            t, s = face * GB + place, face * FACE + place
            total = pair_sums(
                (far_block(s), far_block(s + 1)),
                (near_block(t, s), near_block(t + 1, s + 1)),
                jnp.concatenate(
                    [
                        jnp.concatenate([value_block(s), blank], axis=1),
                        jnp.concatenate([blank, value_block(s + 1)], axis=1),
                    ],
                    axis=0,
                ),
            )
            for k in range(2):
                alive = jnp.where(place + k < work_ref[SLOTS - 5 + face], 1.0, 0.0)
                sums_ref[(t + k) * VROW : (t + k + 1) * VROW, :] = total[k * VROW : (k + 1) * VROW] * alive


def last_kernel(
    work_ref, state_ref, cell_ref, near_ref, acc_ref, own_ref, mine_ref,
    xa_ref, xb_ref, ya_ref, yb_ref, za_ref, zb_ref, far_below_ref, far_above_ref,
    new_ref, fluid_ref,
    table_ref, sums_ref, far_ref, turned_ref, value_ref, value16_ref,
):
    ghost_sums(
        work_ref, near_ref, ((xa_ref, xb_ref), (ya_ref, yb_ref)), sums_ref, far_ref, turned_ref, value_ref, value16_ref
    )
    sums_ref[pl.ds(4 * GB * VROW, (NT - 4 * GB) * VROW), :] = jnp.zeros(((NT - 4 * GB) * VROW, TILE), f32)
    slab = own_ref.shape[1]
    wide = 3 * slab
    z, count = lax.axis_index("gz"), lax.axis_size("gz")
    first_row = (z - 1) * slab

    def inside(flag, value):
        return jnp.where(flag, value, 0.0)

    even = jnp.bitwise_and(z, 1) == 0
    below = [jnp.where(even, zb_ref[c], za_ref[c]) for c in range(8)]
    above = [jnp.where(even, za_ref[c], zb_ref[c]) for c in range(8)]
    has_below, has_above = z >= 1, z <= count - 2
    has_far_below, has_far_above = z >= 2, z <= count - 3

    def solved(total):
        return [total[c] / total[3] for c in range(3)]

    here = solved([
        own_ref[c] + inside(has_below, below[4 + c]) + inside(has_above, above[4 + c]) for c in range(4)
    ])
    lower = solved([
        jnp.where(has_below, below[c], 1.0) + mine_ref[c] + inside(has_far_below, far_below_ref[c]) for c in range(4)
    ])
    upper = solved([
        jnp.where(has_above, above[c], 1.0) + mine_ref[4 + c] + inside(has_far_above, far_above_ref[c]) for c in range(4)
    ])
    for c in range(3):
        fluid_ref[c] = here[c]
        table_ref[pl.ds(c * wide, slab), :] = lower[c]
        table_ref[pl.ds(c * wide + slab, slab), :] = here[c]
        table_ref[pl.ds(c * wide + 2 * slab, slab), :] = upper[c]

    def update_group(group, carry):
        rows = pl.ds(pl.multiple_of(group * 8, 8), 8)

        def sums(k):
            at = pl.ds(group * 8 * VROW + k, 8, stride=VROW)
            return acc_ref[at, :] + sums_ref[at, :]

        weight = sums(9)
        cells = cell_ref[rows, :]
        high = lax.shift_right_logical(cells, 7) - first_row
        low = jnp.bitwise_and(cells, LANES - 1)
        at_cell = [jnp.zeros((8, LANES), f32)] * 3
        for h in range(wide):
            chosen = high == h
            for c in range(3):
                line = jnp.broadcast_to(table_ref[c * wide + h : c * wide + h + 1, :], (8, LANES))
                taken = jnp.take_along_axis(line, low, axis=1, mode="promise_in_bounds")
                at_cell[c] = jnp.where(chosen, taken, at_cell[c])
        r = state_ref[6, rows, :]
        ratio = r / radius_ref
        masses = ratio * ratio * ratio
        rate = drag_coef * r * r
        coupling = time_step * rate / masses
        for c in range(3):
            velocity = state_ref[3 + c, rows, :]
            lever = velocity - spring * centred(state_ref[c, rows, :])
            force = -damping * (lever * weight - (sums(c) + sums(3 + c) + sums(6 + c)))
            moved = velocity + time_step * force / masses
            new_ref[c, rows, :] = (moved + coupling * at_cell[c]) / (1.0 + coupling)
        return carry

    lax.fori_loop(0, NT // 8, update_group, 0, unroll=8)


def shifted(value, axis, steps):
    count = lax.axis_size(axis)
    return lax.ppermute(value, axis, [(i, (i + steps) % count) for i in range(count)])


def swapped(first, second, axis):
    count = lax.axis_size(axis)
    first = lax.ppermute(first, axis, [(i, i ^ 1) for i in range(count)])
    if count == 2:
        return first, first
    return first, lax.ppermute(second, axis, [(i, (i + (1 if i % 2 else -1)) % count) for i in range(count)])


vmem = pl.BlockSpec(memory_space=pltpu.VMEM)
hbm = pl.BlockSpec(memory_space=pltpu.HBM)
smem = pl.BlockSpec(memory_space=pltpu.SMEM)
roomy = pltpu.CompilerParams(vmem_limit_bytes=24 * 2**20)


def body(state, tile_lists, tile_counts, ghost_counts, cell_index, fluid_vel, fluid_frac):
    particles = state.shape[3]
    cell_count = fluid_vel.shape[3]
    slab = cell_count // LANES
    tiles = state.reshape(7, NT, TILE)
    cells = cell_index.reshape(NT, TILE)
    lists = tile_lists.reshape(NT, K).T
    counts = tile_counts.reshape(NT)
    ghosts = ghost_counts.reshape(4)

    def shape(*dims):
        return jax.ShapeDtypeStruct(dims, f32)

    face = shape(8, FACE, TILE)
    (
        za, zb, far_one, far_two, own, mine, xa, xb, ya, yb, held, held_cells, near, turned, value, sums, work
    ) = pl.pallas_call(
        first_kernel,
        out_shape=(
            shape(8, slab, LANES), shape(8, slab, LANES), shape(4, slab, LANES), shape(4, slab, LANES),
            shape(4, slab, LANES), shape(8, slab, LANES), face, face, face, face,
            shape(7, NT, TILE),
            jax.ShapeDtypeStruct((NT, TILE), jnp.int32),
            jax.ShapeDtypeStruct((NT * 128 + 128, TILE), bf16),
            jax.ShapeDtypeStruct((NT * NROW, TILE), bf16),
            jax.ShapeDtypeStruct(((NT + 1) * VROW, TILE), bf16),
            shape((NT + 1) * VROW, TILE),
            jax.ShapeDtypeStruct((SLOTS,), jnp.int32),
        ),
        in_specs=[hbm] * 7,
        out_specs=(vmem,) * 16 + (smem,),
        scratch_shapes=[
            pltpu.VMEM((3, slab, LANES), f32),
            pltpu.VMEM((slab, LANES), f32),
            pltpu.VMEM((8 * NT, TILE), f32),
            pltpu.VMEM((2, 12 * slab, LANES), f32),
            pltpu.VMEM((3 * slab, LANES), f32),
            pltpu.VMEM((NT * NROW, TILE), f32),
            pltpu.VMEM((NT * NROW, TILE), f32),
            pltpu.VMEM((NT * VROW, TILE), f32),
            pltpu.SMEM((K, NT), jnp.int32),
            pltpu.SMEM((NT,), jnp.int32),
            pltpu.SMEM((4,), jnp.int32),
            pltpu.SemaphoreType.DMA((7,)),
        ],
        compiler_params=roomy,
        name="first",
    )(
        *(
            pltpu.with_memory_space_constraint(value, pltpu.HBM)
            for value in (
                tiles, cells, fluid_vel.reshape(3, slab, LANES), fluid_frac.reshape(slab, LANES), lists, counts, ghosts
            )
        )
    )

    ya, yb = swapped(ya, yb, "gy")
    xa, xb = swapped(xa, xb, "gx")
    zb, ya = lax.optimization_barrier((zb, ya))
    za, zb = swapped(za, zb, "gz")
    if lax.axis_size("gz") == 4:
        far_below = far_above = shifted(far_one, "gz", 2)
    else:
        far_below, far_above = shifted(far_one, "gz", 2), shifted(far_two, "gz", -2)

    sums = pl.pallas_call(
        second_kernel,
        out_shape=shape((NT + 1) * VROW, TILE),
        in_specs=[smem] + [vmem] * 4,
        out_specs=vmem,
        compiler_params=roomy,
        name="second",
    )(work, near, turned, value, sums)

    velocity_new, fluid_new = pl.pallas_call(
        last_kernel,
        out_shape=(shape(3, NT, TILE), shape(3, slab, LANES)),
        in_specs=[smem] + [vmem] * 14,
        out_specs=(vmem, vmem),
        scratch_shapes=[
            pltpu.VMEM((9 * slab, LANES), f32),
            pltpu.VMEM((NT * VROW, TILE), f32),
            pltpu.VMEM((4 * FACE * NROW, TILE), f32),
            pltpu.VMEM((4 * FACE * NROW, TILE), bf16),
            pltpu.VMEM((4 * FACE * VROW, TILE), f32),
            pltpu.VMEM((4 * FACE * VROW, TILE), bf16),
        ],
        compiler_params=roomy,
        name="last",
    )(
        work, held, held_cells, near, sums, own, mine, xa, xb, ya, yb, za, zb, far_below, far_above
    )
    return velocity_new.reshape(3, 1, 1, particles), fluid_new.reshape(3, 1, 1, cell_count)


def solution(mesh):
    return jax.shard_map(
        body,
        mesh=mesh,
        in_specs=(
            P(None, "gx", "gy", "gz"),
            P("gx", "gy", "gz", None),
            P("gx", "gy", "gz"),
            P("gx", "gy", "gz", None),
            P("gx", "gy", "gz"),
            P(None, "gx", "gy", "gz"),
            P("gx", "gy", "gz"),
        ),
        out_specs=(P(None, "gx", "gy", "gz"), P(None, "gx", "gy", "gz")),
        check_vma=False,
    )
```

```python
import functools

import jax
import jax.numpy as jnp
from jax import lax
from jax.experimental import pallas as pl
from jax.experimental.pallas import tpu as pltpu
from jax.sharding import PartitionSpec as P

TILE = 128
K = 8
NT = 64
GB = 12
FACE = 16
LANES = 128

stiffness = 5.0
damping = 2.0
time_step = 0.25
drag_coef = 64.0
fluid_density = 2.0
radius_ref = 0.25
spring = stiffness / damping

f32 = jnp.float32
bf16 = jnp.bfloat16

NROW = 32
VROW = 16
DUMMY = NT
GHOST = NT + 4
NFAR = GHOST + 4 * FACE
WIDE = 32
GROUP = 16
EARLY = 2
KEPT = 64
SLOTS = NT * 6


def parts_of(q):
    first = q.astype(bf16).astype(f32)
    rest = q - first
    second = rest.astype(bf16).astype(f32)
    return first, second, (rest - second).astype(bf16).astype(f32)


ORDER = ((0, 0), (0, 1), (0, 2), (1, 0), (1, 1), (2, 0))


def centred(position):
    return position - 0.5


def geometry(columns):
    x, y, z = (centred(columns[k]) for k in range(3))
    r = columns[6]
    return (x, y, z, r), r * r - (x * x + y * y + z * z)


def near_rows(columns):
    lengths, own = geometry(columns)
    one = jnp.ones_like(own)
    rows = []
    for q in lengths:
        cut = parts_of(q)
        rows += [2.0 * cut[j] for _, j in ORDER]
    return rows + [one] * 3 + list(parts_of(own))


def far_rows(columns):
    lengths, own = geometry(columns)
    one = jnp.ones_like(own)
    rows = []
    for q in lengths:
        cut = parts_of(q)
        rows += [cut[i] for i, _ in ORDER]
    return rows + list(parts_of(own)) + [one] * 3


def value_rows(columns, living):
    cuts = [parts_of((columns[3 + c] - spring * centred(columns[c]))) for c in range(3)]
    return [cuts[c][k] * living for k in range(3) for c in range(3)] + [living]


def load(pairs, sems):
    copies = [pltpu.make_async_copy(source, target, sems.at[k]) for k, (source, target) in enumerate(pairs)]
    for copy in copies:
        copy.start()
    return copies


def pair_sums(far, near, values):
    weight = jnp.concatenate(
        [jnp.dot(left, right, preferred_element_type=f32) for left, right in zip(far, near)], axis=0
    )
    weight = jnp.maximum(weight, 0.0)
    coarse = weight.astype(bf16)
    fine = (weight - coarse.astype(f32)).astype(bf16)
    both = jnp.dot(values, jnp.concatenate([coarse, fine], axis=1), preferred_element_type=f32)
    return both[:, :TILE] + both[:, TILE:]


def interior_steps(begin, steps, size, carry, work_ref, near_ref, turned_ref, value_ref, acc_ref):
    def near_block(t, s):
        start = t * 128 + 96 - NROW * jnp.bitwise_and(s, 3)
        return near_ref[pl.ds(pl.multiple_of(start, NROW), 128), :]

    def far_block(s):
        return turned_ref[pl.ds(pl.multiple_of(lax.shift_right_logical(s, 2) * 128, 128), 128), :]

    def value_block(s):
        return value_ref[pl.ds(pl.multiple_of(s * VROW, VROW), VROW), :]

    def step(group, carry):
        sums = []
        for d in range(size):
            word = work_ref[begin + group * size + d]
            t = lax.shift_right_logical(word, 16)
            a = jnp.bitwise_and(lax.shift_right_logical(word, 8), 255)
            b = jnp.bitwise_and(word, 255)
            near = jnp.minimum(t, NT - 1)
            total = pair_sums(
                (far_block(a), far_block(b)),
                (near_block(near, a), near_block(near, b)),
                jnp.concatenate([value_block(a), value_block(b)], axis=1),
            )
            sums.append((t, total))
        last, running = carry
        for t, total in sums:
            running = total + jnp.where(t == last, running, 0.0)
            acc_ref[pl.ds(pl.multiple_of(t * VROW, VROW), VROW), :] = running
            last = t
        return last, running

    return lax.fori_loop(0, steps, step, carry)


def deposit_kernel(
    state_hbm, cell_hbm, vel_hbm, frac_hbm, ghost_hbm,
    parts_ref, xa_ref, xb_ref, ya_ref, yb_ref, state_ref, cell_ref,
    vel_ref, frac_ref, source_ref, deposit_ref, total_ref, ghost_ref, sems,
):
    copies = load(
        [
            (state_hbm, state_ref), (cell_hbm, cell_ref), (vel_hbm, vel_ref), (frac_hbm, frac_ref),
            (ghost_hbm, ghost_ref),
        ],
        sems,
    )
    slab = vel_ref.shape[1]
    wide = 3 * slab
    bands = wide // 2
    even_x, even_y = (jnp.bitwise_and(lax.axis_index(axis), 1) == 0 for axis in ("gx", "gy"))
    first_band = (lax.axis_index("gz") - 1) * (slab // 2)
    for copy in copies:
        copy.wait()

    r = state_ref[6]
    rate = drag_coef * r * r
    sources = [rate * state_ref[3 + c] for c in range(3)] + [rate]
    for c, source in enumerate(sources):
        for k, part in enumerate(parts_of(source)[:2]):
            source_ref[pl.ds(4 * k + c, NT, stride=8), :] = part
    low_of = lax.broadcasted_iota(jnp.int32, (2 * LANES, LANES), 0)

    def add_group(group, total):
        cells = cell_ref[pl.ds(pl.multiple_of(group * 8, 8), 8), :]
        band = lax.shift_right_logical(cells, 8) - first_band
        low = jnp.bitwise_and(cells, 255)
        left, right = [], []
        for t in range(8):
            rows = source_ref[pl.ds(pl.multiple_of(group * 64 + t * 8, 8), 8), :]
            here = jnp.broadcast_to(band[t : t + 1, :], (8, LANES))
            left.append(jnp.concatenate([jnp.where(here == h, rows, 0.0) for h in range(bands)], axis=0).astype(bf16))
            right.append(jnp.where(low[t : t + 1, :] == low_of, 1.0, 0.0).astype(bf16))
        added = lax.dot_general(
            jnp.concatenate(left, axis=1),
            jnp.concatenate(right, axis=1),
            (((1,), (1,)), ((), ())),
            preferred_element_type=f32,
        )
        deposit_ref[0] += added[:, :LANES]
        deposit_ref[1] += added[:, LANES:]
        return total

    deposit_ref[...] = jnp.zeros_like(deposit_ref)
    lax.fori_loop(0, NT // 8, add_group, 0, unroll=8)
    frac = fluid_density * frac_ref[...]
    for c in range(4):
        for k in range(2):
            both = deposit_ref[k, pl.ds(c, bands, stride=8), :] + deposit_ref[k, pl.ds(4 + c, bands, stride=8), :]
            total_ref[pl.ds(k, bands, stride=2), :] = both * time_step
        below, here, above = (total_ref[pl.ds(k * slab, slab), :] for k in range(3))
        parts_ref[c] = above
        parts_ref[4 + c] = here + (frac * vel_ref[c] if c < 3 else frac)
        parts_ref[8 + c] = below
    order = lax.broadcasted_iota(jnp.int32, (FACE, TILE), 0)
    for low, even, a_ref, b_ref in ((0, even_x, xa_ref, xb_ref), (2, even_y, ya_ref, yb_ref)):
        for k in range(7):
            lower = state_ref[k, low * GB : (low + 1) * GB, :]
            upper = state_ref[k, (low + 1) * GB : (low + 2) * GB, :]
            a_ref[k, 0:GB, :] = jnp.where(even, upper, lower)
            b_ref[k, 0:GB, :] = jnp.where(even, lower, upper)
            a_ref[k, GB:FACE, :] = jnp.zeros((FACE - GB, TILE), f32)
            b_ref[k, GB:FACE, :] = jnp.zeros((FACE - GB, TILE), f32)
        lower, upper = ghost_ref[low], ghost_ref[low + 1]
        a_ref[7] = jnp.where(order < jnp.where(even, upper, lower), 1.0, 0.0)
        b_ref[7] = jnp.where(order < jnp.where(even, lower, upper), 1.0, 0.0)

def inner_outer():
    z = lax.axis_index("gz")
    lower = z < 2
    return lower, jnp.bitwise_and(z, 1) == jnp.where(lower, 1, 0)


def put_rows(ref, first, rows, stride, filled):
    tiles = rows[0].shape[0]
    for k, row in enumerate(rows + [jnp.zeros_like(rows[0])] * (filled - len(rows))):
        ref[pl.ds(first * stride + k, tiles, stride=stride), :] = row


def facing(flag, ref):
    return [jnp.where(flag, ref[c], ref[8 + c]) for c in range(4)]


def ghost_slots():
    slot_of, beside = [], []
    for axis in ("gx", "gy"):
        place, count = lax.axis_index(axis), lax.axis_size(axis)
        first = max(slot_of, default=-1) + 1
        slot_of += [first, first if count == 2 else first + 1]
        beside += [place > 0, place < count - 1]
    return slot_of, beside


def feature_kernel(paired, lists_hbm, counts_hbm, ghost_hbm, state_ref, *refs):
    if paired:
        parts_ref, beside_ref, *refs = refs
    near16_ref, turned_ref, value16_ref, acc_ref, work_ref, *refs = refs
    if paired:
        across_ref, *refs = refs
    near_ref, far_ref, value_ref, lists_ref, counts_ref, ghost_ref, sems = refs
    copies = load([(lists_hbm, lists_ref), (counts_hbm, counts_ref), (ghost_hbm, ghost_ref)], sems)
    if paired:
        lower, inner = inner_outer()
        mine, other = facing(lower, parts_ref), facing(lower, beside_ref)
        for c in range(4):
            across_ref[c] = jnp.where(inner, parts_ref[4 + c] + other[c], beside_ref[4 + c] + mine[c])
            across_ref[4 + c] = jnp.where(inner, mine[c], other[c])
    near16_ref[pl.ds(NT * 128, 128), :] = jnp.zeros((128, TILE), bf16)
    turned_ref[DUMMY * NROW : GHOST * NROW, :] = jnp.zeros((4 * NROW, TILE), bf16)
    value16_ref[DUMMY * VROW : GHOST * VROW, :] = jnp.zeros((4 * VROW, TILE), bf16)

    columns = [state_ref[k] for k in range(7)]
    put_rows(near_ref, 0, near_rows(columns), NROW, NROW)
    put_rows(far_ref, 0, far_rows(columns), NROW, NROW)
    put_rows(value_ref, 0, value_rows(columns, jnp.ones((NT, TILE), f32)), VROW, VROW)
    slot_of, beside = ghost_slots()
    for copy in copies:
        copy.wait()
    alive = [jnp.where(beside[face], ghost_ref[face], 0) for face in range(4)]
    n = jnp.int32(0)
    for b in [*range(4 * GB // 4, NT // 4), *range(4 * GB // 4)]:
        if b == 0:
            without_ghosts = n
        rows = slice(b * 128, (b + 1) * 128)
        turned_ref[rows, :] = far_ref[rows, :].T.astype(bf16)
        rows = slice(b * 4 * VROW, (b + 1) * 4 * VROW)
        value16_ref[rows, :] = value_ref[rows, :].astype(bf16)
        for t in range(4 * b, 4 * b + 4):
            near16_ref[t * 128 : (t + 1) * 128, :] = jnp.concatenate(
                [jnp.zeros((96, TILE), bf16), near_ref[t * NROW : (t + 1) * NROW, :].astype(bf16)], axis=0
            )
            count = counts_ref[t]
            face, place = t // GB, t % GB
            if face < 4:
                ghost = GHOST + slot_of[face] * FACE + place
                entries = count + (place < alive[face]).astype(jnp.int32)
            else:
                ghost, entries = DUMMY, count
            for d in range((K + 1 + (face < 4)) // 2):
                a = lists_ref[min(2 * d, K - 1), t]
                if face < 4 and d > 0:
                    a = jnp.where(2 * d < count, a, ghost)
                b_ = jnp.where(2 * d + 1 < entries, ghost, DUMMY)
                if 2 * d + 1 < K:
                    b_ = jnp.where(2 * d + 1 < count, lists_ref[2 * d + 1, t], b_)
                work_ref[n + d] = t * 65536 + a * 256 + b_
            n = n + lax.shift_right_logical(entries + 1, 1)
    for d in range(WIDE):
        work_ref[n + d] = NT * 65536 + DUMMY
    work_ref[SLOTS - 1] = n
    if paired:
        ahead = jnp.minimum(without_ghosts, jnp.maximum(n - KEPT, 0))
        ahead = jnp.where(lower, jnp.minimum(lax.div(ahead, GROUP), EARLY), 0)
        work_ref[SLOTS - 2] = ahead * GROUP
        carry = (jnp.int32(-1), jnp.zeros((VROW, TILE), f32))
        interior_steps(0, ahead, GROUP, carry, work_ref, near16_ref, turned_ref, value16_ref, acc_ref)
    else:
        work_ref[SLOTS - 2] = 0


def interior_kernel(
    work_ref, near_ref, own_turned_ref, own_value_ref, before_ref, xa_ref, xb_ref, ya_ref, yb_ref,
    acc_ref, turned_ref, value_ref, far_ref, cut_ref,
):
    slots = []
    for axis, a_ref, b_ref in (("gx", xa_ref, xb_ref), ("gy", ya_ref, yb_ref)):
        even = jnp.bitwise_and(lax.axis_index(axis), 1) == 0
        a, b = ([ref[k] for k in range(8)] for ref in (a_ref, b_ref))
        if lax.axis_size(axis) == 2:
            slots.append(a)
        else:
            slots.append([jnp.where(even, q, p) for p, q in zip(a, b)])
            slots.append([jnp.where(even, p, q) for p, q in zip(a, b)])
    columns = [jnp.concatenate([slot[k] for slot in slots], axis=0) for k in range(8)]
    put_rows(far_ref, 0, far_rows(columns), NROW, NROW)
    put_rows(cut_ref, 0, value_rows(columns, columns[7]), VROW, VROW)
    acc_ref[...] = before_ref[...]
    turned_ref[0 : GHOST * NROW, :] = own_turned_ref[...]
    value_ref[0 : GHOST * VROW, :] = own_value_ref[...]
    ghosts = len(slots) * FACE
    value_ref[GHOST * VROW : (GHOST + ghosts) * VROW, :] = cut_ref[0 : ghosts * VROW, :].astype(bf16)
    for b in range(ghosts // 4):
        turned_ref[GHOST * NROW + b * 128 : GHOST * NROW + (b + 1) * 128, :] = (
            far_ref[b * 128 : (b + 1) * 128, :].T.astype(bf16)
        )
    begin = work_ref[SLOTS - 2]
    left = work_ref[SLOTS - 1] - begin
    wide = lax.div(left + (WIDE - GROUP - 1), WIDE)
    tail = (left > wide * WIDE).astype(jnp.int32)
    refs = (work_ref, near_ref, turned_ref, value_ref, acc_ref)
    before = lax.shift_right_logical(work_ref[jnp.maximum(begin - 1, 0)], 16)
    rows = pl.ds(pl.multiple_of(before * VROW, VROW), VROW)
    carry = (jnp.where(begin > 0, before, -1), before_ref[rows, :])
    carry = interior_steps(begin, wide, WIDE, carry, *refs)
    interior_steps(begin + wide * WIDE, tail, GROUP, carry, *refs)


def solved(total):
    return [total[c] / total[3] for c in range(3)]


def added(*terms):
    return [sum(values[1:], values[0]) for values in zip(*terms)]


def paired_slabs(parts_ref, beside_ref, across_ref):
    lower, inner = inner_outer()
    own, other = ([ref[4 + c] for c in range(4)] for ref in (parts_ref, beside_ref))
    mine_to, other_to = facing(lower, parts_ref), facing(lower, beside_ref)
    away = jnp.logical_not(lower)
    mine_from, other_from = facing(away, parts_ref), facing(away, beside_ref)
    summed, single = ([across_ref[k + c] for c in range(4)] for k in (0, 4))

    def chosen(first, second):
        return [jnp.where(inner, p, q) for p, q in zip(first, second)]

    here = solved(chosen(added(own, other_to, single), added(own, other_from)))
    near = solved(chosen(added(other, mine_from), added(other, mine_to, single)))
    past = solved(added(summed, mine_to))
    even = jnp.bitwise_and(lax.axis_index("gz"), 1) == 0
    below = [jnp.where(even, p, q) for p, q in zip(past, near)]
    above = [jnp.where(even, q, p) for p, q in zip(past, near)]
    return below, here, above


def ring_slabs(parts_ref, below_ref, above_ref, far_below_ref, far_above_ref):
    z, count = lax.axis_index("gz"), lax.axis_size("gz")

    def rows(ref, first):
        return [ref[first + c] for c in range(4)]

    def inside(flag, values, other=0.0):
        return [jnp.where(flag, value, other) for value in values]

    has_below, has_above = z >= 1, z <= count - 2
    here = added(rows(parts_ref, 4), inside(has_below, rows(below_ref, 0)), inside(has_above, rows(above_ref, 4)))
    below = added(
        inside(has_below, rows(below_ref, 4), 1.0), rows(parts_ref, 8), inside(z >= 2, rows(far_below_ref, 0))
    )
    above = added(
        inside(has_above, rows(above_ref, 0), 1.0), rows(parts_ref, 0), inside(z <= count - 3, rows(far_above_ref, 0))
    )
    return solved(below), solved(here), solved(above)


def update_kernel(paired, state_ref, cell_ref, acc_ref, parts_ref, *refs):
    slabs, refs = (refs[:2], refs[2:]) if paired else (refs[:4], refs[4:])
    new_ref, fluid_ref, table_ref = refs
    slab = parts_ref.shape[1]
    wide = 3 * slab
    first_row = (lax.axis_index("gz") - 1) * slab
    lower, here, upper = (paired_slabs if paired else ring_slabs)(parts_ref, *slabs)
    for c in range(3):
        fluid_ref[c] = here[c]
        table_ref[pl.ds(c * wide, slab), :] = lower[c]
        table_ref[pl.ds(c * wide + slab, slab), :] = here[c]
        table_ref[pl.ds(c * wide + 2 * slab, slab), :] = upper[c]

    def update_group(group, carry):
        rows = pl.ds(pl.multiple_of(group * 8, 8), 8)

        def sums(k):
            return acc_ref[pl.ds(group * 8 * VROW + k, 8, stride=VROW), :]

        weight = sums(9)
        cells = cell_ref[rows, :]
        high = lax.shift_right_logical(cells, 7) - first_row
        low = jnp.bitwise_and(cells, LANES - 1)
        at_cell = [jnp.zeros((8, LANES), f32)] * 3
        for h in range(wide):
            chosen = high == h
            for c in range(3):
                line = jnp.broadcast_to(table_ref[c * wide + h : c * wide + h + 1, :], (8, LANES))
                taken = jnp.take_along_axis(line, low, axis=1, mode="promise_in_bounds")
                at_cell[c] = jnp.where(chosen, taken, at_cell[c])
        r = state_ref[6, rows, :]
        ratio = r / radius_ref
        masses = ratio * ratio * ratio
        rate = drag_coef * r * r
        coupling = time_step * rate / masses
        for c in range(3):
            velocity = state_ref[3 + c, rows, :]
            lever = velocity - spring * centred(state_ref[c, rows, :])
            force = -damping * (lever * weight - (sums(c) + sums(3 + c) + sums(6 + c)))
            moved = velocity + time_step * force / masses
            new_ref[c, rows, :] = (moved + coupling * at_cell[c]) / (1.0 + coupling)
        return carry

    lax.fori_loop(0, NT // 8, update_group, 0, unroll=8)


def shifted(value, axis, steps):
    count = lax.axis_size(axis)
    return lax.ppermute(value, axis, [(i, (i + steps) % count) for i in range(count)])


def swapped(first, second, axis):
    count = lax.axis_size(axis)
    first = lax.ppermute(first, axis, [(i, i ^ 1) for i in range(count)])
    if count == 2:
        return first, first
    return first, lax.ppermute(second, axis, [(i, (i + (1 if i % 2 else -1)) % count) for i in range(count)])


vmem = pl.BlockSpec(memory_space=pltpu.VMEM)
hbm = pl.BlockSpec(memory_space=pltpu.HBM)
smem = pl.BlockSpec(memory_space=pltpu.SMEM)
roomy = pltpu.CompilerParams(vmem_limit_bytes=24 * 2**20)


def body(state, tile_lists, tile_counts, ghost_counts, cell_index, fluid_vel, fluid_frac):
    particles = state.shape[3]
    cell_count = fluid_vel.shape[3]
    slab = cell_count // LANES
    tiles = state.reshape(7, NT, TILE)
    cells = cell_index.reshape(NT, TILE)
    lists = tile_lists.reshape(NT, K).T
    counts = tile_counts.reshape(NT)
    ghosts = ghost_counts.reshape(4)

    def shape(*dims):
        return jax.ShapeDtypeStruct(dims, f32)

    def held(*values):
        return [pltpu.with_memory_space_constraint(value, pltpu.HBM) for value in values]

    face = shape(8, FACE, TILE)
    paired = lax.axis_size("gz") == 4
    parts, xa, xb, ya, yb, state_vmem, cells_vmem = pl.pallas_call(
        deposit_kernel,
        out_shape=(
            shape(12, slab, LANES), face, face, face, face,
            shape(7, NT, TILE), jax.ShapeDtypeStruct((NT, TILE), jnp.int32),
        ),
        in_specs=[hbm] * 5,
        out_specs=(vmem,) * 7,
        scratch_shapes=[
            pltpu.VMEM((3, slab, LANES), f32),
            pltpu.VMEM((slab, LANES), f32),
            pltpu.VMEM((8 * NT, TILE), f32),
            pltpu.VMEM((2, 12 * slab, LANES), f32),
            pltpu.VMEM((3 * slab, LANES), f32),
            pltpu.SMEM((4,), jnp.int32),
            pltpu.SemaphoreType.DMA((5,)),
        ],
        compiler_params=roomy,
        name="deposit",
    )(*held(tiles, cells, fluid_vel.reshape(3, slab, LANES), fluid_frac.reshape(slab, LANES), ghosts))

    if paired:
        beside = lax.ppermute(parts, "gz", [(i, i ^ 1) for i in range(4)])
        slabs = (beside,)
    else:
        slabs = (
            shifted(parts[0:8], "gz", 1), shifted(parts[4:12], "gz", -1),
            shifted(parts[0:4], "gz", 2), shifted(parts[8:12], "gz", -2),
        )
    ya, yb = swapped(ya, yb, "gy")
    xa, xb = swapped(xa, xb, "gx")

    near, turned, value, sums, work, *across = pl.pallas_call(
        functools.partial(feature_kernel, paired),
        out_shape=(
            jax.ShapeDtypeStruct((NT * 128 + 128, TILE), bf16),
            jax.ShapeDtypeStruct((GHOST * NROW, TILE), bf16),
            jax.ShapeDtypeStruct((GHOST * VROW, TILE), bf16),
            shape((NT + 1) * VROW, TILE),
            jax.ShapeDtypeStruct((SLOTS,), jnp.int32),
        ) + ((shape(8, slab, LANES),) if paired else ()),
        in_specs=[hbm] * 3 + [vmem] * (3 if paired else 1),
        out_specs=(vmem,) * 4 + (smem,) + ((vmem,) if paired else ()),
        scratch_shapes=[
            pltpu.VMEM((NT * NROW, TILE), f32),
            pltpu.VMEM((NT * NROW, TILE), f32),
            pltpu.VMEM((NT * VROW, TILE), f32),
            pltpu.SMEM((K, NT), jnp.int32),
            pltpu.SMEM((NT,), jnp.int32),
            pltpu.SMEM((4,), jnp.int32),
            pltpu.SemaphoreType.DMA((3,)),
        ],
        compiler_params=roomy,
        name="feature",
    )(*held(lists, counts, ghosts), state_vmem, *((parts, beside) if paired else ()))
    if paired:
        slabs += (lax.ppermute(across[0], "gz", [(i, i ^ 2) for i in range(4)]),)

    sums = pl.pallas_call(
        interior_kernel,
        out_shape=shape((NT + 1) * VROW, TILE),
        in_specs=[smem] + [vmem] * 8,
        out_specs=vmem,
        scratch_shapes=[
            pltpu.VMEM((NFAR * NROW, TILE), bf16),
            pltpu.VMEM((NFAR * VROW, TILE), bf16),
            pltpu.VMEM((4 * FACE * NROW, TILE), f32),
            pltpu.VMEM((4 * FACE * VROW, TILE), f32),
        ],
        compiler_params=roomy,
        name="interior",
    )(work, near, turned, value, sums, xa, xb, ya, yb)

    velocity_new, fluid_new = pl.pallas_call(
        functools.partial(update_kernel, paired),
        out_shape=(shape(3, NT, TILE), shape(3, slab, LANES)),
        in_specs=[vmem] * (4 + len(slabs)),
        out_specs=(vmem, vmem),
        scratch_shapes=[pltpu.VMEM((9 * slab, LANES), f32)],
        compiler_params=roomy,
        name="update",
    )(state_vmem, cells_vmem, sums, parts, *slabs)
    return velocity_new.reshape(3, 1, 1, particles), fluid_new.reshape(3, 1, 1, cell_count)


def solution(mesh):
    return jax.shard_map(
        body,
        mesh=mesh,
        in_specs=(
            P(None, "gx", "gy", "gz"),
            P("gx", "gy", "gz", None),
            P("gx", "gy", "gz"),
            P("gx", "gy", "gz", None),
            P("gx", "gy", "gz"),
            P(None, "gx", "gy", "gz"),
            P("gx", "gy", "gz"),
        ),
        out_specs=(P(None, "gx", "gy", "gz"), P(None, "gx", "gy", "gz")),
        check_vma=False,
    )
```

```python
import functools

import jax
import jax.numpy as jnp
from jax import lax
from jax.experimental import pallas as pl
from jax.experimental.pallas import tpu as pltpu
from jax.sharding import PartitionSpec as P

TILE = 128
K = 8
NT = 64
GB = 12
FACE = 16
LANES = 128

stiffness = 5.0
damping = 2.0
time_step = 0.25
drag_coef = 64.0
fluid_density = 2.0
radius_ref = 0.25
spring = stiffness / damping

f32 = jnp.float32
bf16 = jnp.bfloat16

NROW = 32
VROW = 16
DUMMY = NT
GHOST = NT + 4
NFAR = GHOST + 4 * FACE
SIZES = (64, 32, 16)
GROUP = 16
EARLY = 2
KEPT = 64
SLOTS = NT * 6


def parts_of(q):
    first = q.astype(bf16).astype(f32)
    rest = q - first
    second = rest.astype(bf16).astype(f32)
    return first, second, (rest - second).astype(bf16).astype(f32)


ORDER = ((0, 0), (0, 1), (0, 2), (1, 0), (1, 1), (2, 0))


def centred(position):
    return position - 0.5


def geometry(columns):
    x, y, z = (centred(columns[k]) for k in range(3))
    r = columns[6]
    return (x, y, z, r), r * r - (x * x + y * y + z * z)


def near_rows(columns):
    lengths, own = geometry(columns)
    one = jnp.ones_like(own)
    rows = []
    for q in lengths:
        cut = parts_of(q)
        rows += [2.0 * cut[j] for _, j in ORDER]
    return rows + [one] * 3 + list(parts_of(own))


def far_rows(columns):
    lengths, own = geometry(columns)
    one = jnp.ones_like(own)
    rows = []
    for q in lengths:
        cut = parts_of(q)
        rows += [cut[i] for i, _ in ORDER]
    return rows + list(parts_of(own)) + [one] * 3


def value_rows(columns, living):
    cuts = [parts_of((columns[3 + c] - spring * centred(columns[c]))) for c in range(3)]
    return [cuts[c][k] * living for k in range(3) for c in range(3)] + [living]


def load(pairs, sems):
    copies = [pltpu.make_async_copy(source, target, sems.at[k]) for k, (source, target) in enumerate(pairs)]
    for copy in copies:
        copy.start()
    return copies


def pair_sums(far, near, values):
    weight = jnp.concatenate(
        [jnp.dot(left, right, preferred_element_type=f32) for left, right in zip(far, near)], axis=0
    )
    weight = jnp.maximum(weight, 0.0)
    coarse = weight.astype(bf16)
    fine = (weight - coarse.astype(f32)).astype(bf16)
    both = jnp.dot(values, jnp.concatenate([coarse, fine], axis=1), preferred_element_type=f32)
    return both[:, :TILE] + both[:, TILE:]


def interior_steps(begin, steps, size, carry, work_ref, near_ref, turned_ref, value_ref, acc_ref):
    def near_block(t, s):
        start = t * 128 + 96 - NROW * jnp.bitwise_and(s, 3)
        return near_ref[pl.ds(pl.multiple_of(start, NROW), 128), :]

    def far_block(s):
        return turned_ref[pl.ds(pl.multiple_of(lax.shift_right_logical(s, 2) * 128, 128), 128), :]

    def value_block(s):
        return value_ref[pl.ds(pl.multiple_of(s * VROW, VROW), VROW), :]

    def step(group, carry):
        sums = []
        for d in range(size):
            word = work_ref[begin + group * size + d]
            t = lax.shift_right_logical(word, 16)
            a = jnp.bitwise_and(lax.shift_right_logical(word, 8), 255)
            b = jnp.bitwise_and(word, 255)
            near = jnp.minimum(t, NT - 1)
            total = pair_sums(
                (far_block(a), far_block(b)),
                (near_block(near, a), near_block(near, b)),
                jnp.concatenate([value_block(a), value_block(b)], axis=1),
            )
            sums.append((t, total))
        last, running = carry
        for t, total in sums:
            running = total + jnp.where(t == last, running, 0.0)
            acc_ref[pl.ds(pl.multiple_of(t * VROW, VROW), VROW), :] = running
            last = t
        return last, running

    return lax.fori_loop(0, steps, step, carry)


def deposit_kernel(
    state_hbm, cell_hbm, vel_hbm, frac_hbm, ghost_hbm,
    parts_ref, xa_ref, xb_ref, ya_ref, yb_ref, state_ref, cell_ref,
    vel_ref, frac_ref, source_ref, deposit_ref, total_ref, ghost_ref, sems,
):
    copies = load(
        [
            (state_hbm, state_ref), (cell_hbm, cell_ref), (vel_hbm, vel_ref), (frac_hbm, frac_ref),
            (ghost_hbm, ghost_ref),
        ],
        sems,
    )
    slab = vel_ref.shape[1]
    wide = 3 * slab
    bands = wide // 2
    even_x, even_y = (jnp.bitwise_and(lax.axis_index(axis), 1) == 0 for axis in ("gx", "gy"))
    first_band = (lax.axis_index("gz") - 1) * (slab // 2)
    for copy in copies:
        copy.wait()

    r = state_ref[6]
    rate = drag_coef * r * r
    sources = [rate * state_ref[3 + c] for c in range(3)] + [rate]
    for c, source in enumerate(sources):
        for k, part in enumerate(parts_of(source)[:2]):
            source_ref[pl.ds(4 * k + c, NT, stride=8), :] = part
    low_of = lax.broadcasted_iota(jnp.int32, (2 * LANES, LANES), 0)

    def add_group(group, total):
        cells = cell_ref[pl.ds(pl.multiple_of(group * 8, 8), 8), :]
        band = lax.shift_right_logical(cells, 8) - first_band
        low = jnp.bitwise_and(cells, 255)
        left, right = [], []
        for t in range(8):
            rows = source_ref[pl.ds(pl.multiple_of(group * 64 + t * 8, 8), 8), :]
            here = jnp.broadcast_to(band[t : t + 1, :], (8, LANES))
            left.append(jnp.concatenate([jnp.where(here == h, rows, 0.0) for h in range(bands)], axis=0).astype(bf16))
            right.append(jnp.where(low[t : t + 1, :] == low_of, 1.0, 0.0).astype(bf16))
        added = lax.dot_general(
            jnp.concatenate(left, axis=1),
            jnp.concatenate(right, axis=1),
            (((1,), (1,)), ((), ())),
            preferred_element_type=f32,
        )
        deposit_ref[0] += added[:, :LANES]
        deposit_ref[1] += added[:, LANES:]
        return total

    deposit_ref[...] = jnp.zeros_like(deposit_ref)
    lax.fori_loop(0, NT // 8, add_group, 0, unroll=8)
    frac = fluid_density * frac_ref[...]
    for c in range(4):
        for k in range(2):
            both = deposit_ref[k, pl.ds(c, bands, stride=8), :] + deposit_ref[k, pl.ds(4 + c, bands, stride=8), :]
            total_ref[pl.ds(k, bands, stride=2), :] = both * time_step
        below, here, above = (total_ref[pl.ds(k * slab, slab), :] for k in range(3))
        parts_ref[c] = above
        parts_ref[4 + c] = here + (frac * vel_ref[c] if c < 3 else frac)
        parts_ref[8 + c] = below
    order = lax.broadcasted_iota(jnp.int32, (FACE, TILE), 0)
    for low, even, a_ref, b_ref in ((0, even_x, xa_ref, xb_ref), (2, even_y, ya_ref, yb_ref)):
        for k in range(7):
            lower = state_ref[k, low * GB : (low + 1) * GB, :]
            upper = state_ref[k, (low + 1) * GB : (low + 2) * GB, :]
            a_ref[k, 0:GB, :] = jnp.where(even, upper, lower)
            b_ref[k, 0:GB, :] = jnp.where(even, lower, upper)
            a_ref[k, GB:FACE, :] = jnp.zeros((FACE - GB, TILE), f32)
            b_ref[k, GB:FACE, :] = jnp.zeros((FACE - GB, TILE), f32)
        lower, upper = ghost_ref[low], ghost_ref[low + 1]
        a_ref[7] = jnp.where(order < jnp.where(even, upper, lower), 1.0, 0.0)
        b_ref[7] = jnp.where(order < jnp.where(even, lower, upper), 1.0, 0.0)

def inner_outer():
    z = lax.axis_index("gz")
    lower = z < 2
    return lower, jnp.bitwise_and(z, 1) == jnp.where(lower, 1, 0)


def put_rows(ref, first, rows, stride, filled):
    tiles = rows[0].shape[0]
    all_rows = jnp.stack(rows + [jnp.zeros_like(rows[0])] * (filled - len(rows)), axis=0)
    ref[first * stride : (first + tiles) * stride, :] = jnp.swapaxes(all_rows, 0, 1).reshape(tiles * stride, TILE)


def facing(flag, ref):
    return [jnp.where(flag, ref[c], ref[8 + c]) for c in range(4)]


def ghost_slots():
    slot_of, beside = [], []
    for axis in ("gx", "gy"):
        place, count = lax.axis_index(axis), lax.axis_size(axis)
        first = max(slot_of, default=-1) + 1
        slot_of += [first, first if count == 2 else first + 1]
        beside += [place > 0, place < count - 1]
    return slot_of, beside


def feature_kernel(paired, lists_hbm, counts_hbm, ghost_hbm, state_ref, *refs):
    if paired:
        parts_ref, beside_ref, *refs = refs
    near16_ref, turned_ref, value16_ref, acc_ref, work_ref, *refs = refs
    if paired:
        across_ref, *refs = refs
    near_ref, far_ref, value_ref, lists_ref, counts_ref, ghost_ref, sems = refs
    copies = load([(lists_hbm, lists_ref), (counts_hbm, counts_ref), (ghost_hbm, ghost_ref)], sems)
    if paired:
        lower, inner = inner_outer()
        mine, other = facing(lower, parts_ref), facing(lower, beside_ref)
        for c in range(4):
            across_ref[c] = jnp.where(inner, parts_ref[4 + c] + other[c], beside_ref[4 + c] + mine[c])
            across_ref[4 + c] = jnp.where(inner, mine[c], other[c])
    near16_ref[pl.ds(NT * 128, 128), :] = jnp.zeros((128, TILE), bf16)
    turned_ref[DUMMY * NROW : GHOST * NROW, :] = jnp.zeros((4 * NROW, TILE), bf16)
    value16_ref[DUMMY * VROW : GHOST * VROW, :] = jnp.zeros((4 * VROW, TILE), bf16)

    columns = [state_ref[k] for k in range(7)]
    put_rows(near_ref, 0, near_rows(columns), NROW, NROW)
    put_rows(far_ref, 0, far_rows(columns), NROW, NROW)
    put_rows(value_ref, 0, value_rows(columns, jnp.ones((NT, TILE), f32)), VROW, VROW)
    slot_of, beside = ghost_slots()
    for copy in copies:
        copy.wait()
    alive = [jnp.where(beside[face], ghost_ref[face], 0) for face in range(4)]
    n = jnp.int32(0)
    for b in [*range(4 * GB // 4, NT // 4), *range(4 * GB // 4)]:
        if b == 0:
            without_ghosts = n
        rows = slice(b * 128, (b + 1) * 128)
        turned_ref[rows, :] = far_ref[rows, :].T.astype(bf16)
        rows = slice(b * 4 * VROW, (b + 1) * 4 * VROW)
        value16_ref[rows, :] = value_ref[rows, :].astype(bf16)
        for t in range(4 * b, 4 * b + 4):
            near16_ref[t * 128 : (t + 1) * 128, :] = jnp.concatenate(
                [jnp.zeros((96, TILE), bf16), near_ref[t * NROW : (t + 1) * NROW, :].astype(bf16)], axis=0
            )
            count = counts_ref[t]
            face, place = t // GB, t % GB
            if face < 4:
                ghost = GHOST + slot_of[face] * FACE + place
                entries = count + (place < alive[face]).astype(jnp.int32)
            else:
                ghost, entries = DUMMY, count
            for d in range((K + 1 + (face < 4)) // 2):
                a = lists_ref[min(2 * d, K - 1), t]
                if face < 4 and d > 0:
                    a = jnp.where(2 * d < count, a, ghost)
                b_ = jnp.where(2 * d + 1 < entries, ghost, DUMMY)
                if 2 * d + 1 < K:
                    b_ = jnp.where(2 * d + 1 < count, lists_ref[2 * d + 1, t], b_)
                work_ref[n + d] = t * 65536 + a * 256 + b_
            n = n + lax.shift_right_logical(entries + 1, 1)
    for d in range(SIZES[0]):
        work_ref[n + d] = NT * 65536 + DUMMY
    work_ref[SLOTS - 1] = n
    if paired:
        ahead = jnp.minimum(without_ghosts, jnp.maximum(n - KEPT, 0))
        ahead = jnp.where(lower, jnp.minimum(lax.div(ahead, GROUP), EARLY), 0)
        work_ref[SLOTS - 2] = ahead * GROUP
        carry = (jnp.int32(-1), jnp.zeros((VROW, TILE), f32))
        interior_steps(0, ahead, GROUP, carry, work_ref, near16_ref, turned_ref, value16_ref, acc_ref)
    else:
        work_ref[SLOTS - 2] = 0


def interior_kernel(
    work_ref, near_ref, own_turned_ref, own_value_ref, before_ref, xa_ref, xb_ref, ya_ref, yb_ref,
    acc_ref, turned_ref, value_ref, far_ref, cut_ref,
):
    slots = []
    for axis, a_ref, b_ref in (("gx", xa_ref, xb_ref), ("gy", ya_ref, yb_ref)):
        even = jnp.bitwise_and(lax.axis_index(axis), 1) == 0
        a, b = ([ref[k] for k in range(8)] for ref in (a_ref, b_ref))
        if lax.axis_size(axis) == 2:
            slots.append(a)
        else:
            slots.append([jnp.where(even, q, p) for p, q in zip(a, b)])
            slots.append([jnp.where(even, p, q) for p, q in zip(a, b)])
    columns = [jnp.concatenate([slot[k] for slot in slots], axis=0) for k in range(8)]
    put_rows(far_ref, 0, far_rows(columns), NROW, NROW)
    put_rows(cut_ref, 0, value_rows(columns, columns[7]), VROW, VROW)
    @pl.when(work_ref[SLOTS - 2] > 0)
    def _():
        acc_ref[...] = before_ref[...]

    turned_ref[0 : GHOST * NROW, :] = own_turned_ref[...]
    value_ref[0 : GHOST * VROW, :] = own_value_ref[...]
    ghosts = len(slots) * FACE
    value_ref[GHOST * VROW : (GHOST + ghosts) * VROW, :] = cut_ref[0 : ghosts * VROW, :].astype(bf16)
    for b in range(ghosts // 4):
        turned_ref[GHOST * NROW + b * 128 : GHOST * NROW + (b + 1) * 128, :] = (
            far_ref[b * 128 : (b + 1) * 128, :].T.astype(bf16)
        )
    begin = work_ref[SLOTS - 2]
    left = work_ref[SLOTS - 1] - begin
    refs = (work_ref, near_ref, turned_ref, value_ref, acc_ref)
    before = lax.shift_right_logical(work_ref[jnp.maximum(begin - 1, 0)], 16)
    rows = pl.ds(pl.multiple_of(before * VROW, VROW), VROW)
    carry = (jnp.where(begin > 0, before, -1), before_ref[rows, :])
    for size in SIZES:
        steps = lax.div(left + (GROUP - 1 if size > GROUP else size - 1), size)
        carry = interior_steps(begin, steps, size, carry, *refs)
        begin, left = begin + steps * size, jnp.maximum(left - steps * size, 0)


def solved(total):
    return [total[c] / total[3] for c in range(3)]


def added(*terms):
    return [sum(values[1:], values[0]) for values in zip(*terms)]


def paired_slabs(parts_ref, beside_ref, across_ref):
    lower, inner = inner_outer()
    own, other = ([ref[4 + c] for c in range(4)] for ref in (parts_ref, beside_ref))
    mine_to, other_to = facing(lower, parts_ref), facing(lower, beside_ref)
    away = jnp.logical_not(lower)
    mine_from, other_from = facing(away, parts_ref), facing(away, beside_ref)
    summed, single = ([across_ref[k + c] for c in range(4)] for k in (0, 4))

    def chosen(first, second):
        return [jnp.where(inner, p, q) for p, q in zip(first, second)]

    here = solved(chosen(added(own, other_to, single), added(own, other_from)))
    near = solved(chosen(added(other, mine_from), added(other, mine_to, single)))
    past = solved(added(summed, mine_to))
    even = jnp.bitwise_and(lax.axis_index("gz"), 1) == 0
    below = [jnp.where(even, p, q) for p, q in zip(past, near)]
    above = [jnp.where(even, q, p) for p, q in zip(past, near)]
    return below, here, above


def ring_slabs(parts_ref, below_ref, above_ref, far_below_ref, far_above_ref):
    z, count = lax.axis_index("gz"), lax.axis_size("gz")

    def rows(ref, first):
        return [ref[first + c] for c in range(4)]

    def inside(flag, values, other=0.0):
        return [jnp.where(flag, value, other) for value in values]

    has_below, has_above = z >= 1, z <= count - 2
    here = added(rows(parts_ref, 4), inside(has_below, rows(below_ref, 0)), inside(has_above, rows(above_ref, 4)))
    below = added(
        inside(has_below, rows(below_ref, 4), 1.0), rows(parts_ref, 8), inside(z >= 2, rows(far_below_ref, 0))
    )
    above = added(
        inside(has_above, rows(above_ref, 0), 1.0), rows(parts_ref, 0), inside(z <= count - 3, rows(far_above_ref, 0))
    )
    return solved(below), solved(here), solved(above)


def update_kernel(paired, state_ref, cell_ref, acc_ref, parts_ref, *refs):
    slabs, refs = (refs[:2], refs[2:]) if paired else (refs[:4], refs[4:])
    new_ref, fluid_ref, table_ref = refs
    slab = parts_ref.shape[1]
    wide = 3 * slab
    first_row = (lax.axis_index("gz") - 1) * slab
    lower, here, upper = (paired_slabs if paired else ring_slabs)(parts_ref, *slabs)
    for c in range(3):
        fluid_ref[c] = here[c]
        table_ref[pl.ds(c * wide, slab), :] = lower[c]
        table_ref[pl.ds(c * wide + slab, slab), :] = here[c]
        table_ref[pl.ds(c * wide + 2 * slab, slab), :] = upper[c]

    def update_group(group, carry):
        rows = pl.ds(pl.multiple_of(group * 8, 8), 8)

        def sums(k):
            return acc_ref[pl.ds(group * 8 * VROW + k, 8, stride=VROW), :]

        weight = sums(9)
        cells = cell_ref[rows, :]
        high = lax.shift_right_logical(cells, 7) - first_row
        low = jnp.bitwise_and(cells, LANES - 1)
        at_cell = [jnp.zeros((8, LANES), f32)] * 3
        for h in range(wide):
            chosen = high == h
            for c in range(3):
                line = jnp.broadcast_to(table_ref[c * wide + h : c * wide + h + 1, :], (8, LANES))
                taken = jnp.take_along_axis(line, low, axis=1, mode="promise_in_bounds")
                at_cell[c] = jnp.where(chosen, taken, at_cell[c])
        r = state_ref[6, rows, :]
        ratio = r / radius_ref
        masses = ratio * ratio * ratio
        rate = drag_coef * r * r
        coupling = time_step * rate / masses
        for c in range(3):
            velocity = state_ref[3 + c, rows, :]
            lever = velocity - spring * centred(state_ref[c, rows, :])
            force = -damping * (lever * weight - (sums(c) + sums(3 + c) + sums(6 + c)))
            moved = velocity + time_step * force / masses
            new_ref[c, rows, :] = (moved + coupling * at_cell[c]) / (1.0 + coupling)
        return carry

    lax.fori_loop(0, NT // 8, update_group, 0, unroll=8)


def shifted(value, axis, steps):
    count = lax.axis_size(axis)
    return lax.ppermute(value, axis, [(i, (i + steps) % count) for i in range(count)])


def swapped(first, second, axis):
    count = lax.axis_size(axis)
    first = lax.ppermute(first, axis, [(i, i ^ 1) for i in range(count)])
    if count == 2:
        return first, first
    return first, lax.ppermute(second, axis, [(i, (i + (1 if i % 2 else -1)) % count) for i in range(count)])


vmem = pl.BlockSpec(memory_space=pltpu.VMEM)
hbm = pl.BlockSpec(memory_space=pltpu.HBM)
smem = pl.BlockSpec(memory_space=pltpu.SMEM)
roomy = pltpu.CompilerParams(vmem_limit_bytes=24 * 2**20)


def body(state, tile_lists, tile_counts, ghost_counts, cell_index, fluid_vel, fluid_frac):
    particles = state.shape[3]
    cell_count = fluid_vel.shape[3]
    slab = cell_count // LANES
    tiles = state.reshape(7, NT, TILE)
    cells = cell_index.reshape(NT, TILE)
    lists = tile_lists.reshape(NT, K).T
    counts = tile_counts.reshape(NT)
    ghosts = ghost_counts.reshape(4)

    def shape(*dims):
        return jax.ShapeDtypeStruct(dims, f32)

    def held(*values):
        return [pltpu.with_memory_space_constraint(value, pltpu.HBM) for value in values]

    face = shape(8, FACE, TILE)
    paired = lax.axis_size("gz") == 4
    parts, xa, xb, ya, yb, state_vmem, cells_vmem = pl.pallas_call(
        deposit_kernel,
        out_shape=(
            shape(12, slab, LANES), face, face, face, face,
            shape(7, NT, TILE), jax.ShapeDtypeStruct((NT, TILE), jnp.int32),
        ),
        in_specs=[hbm] * 5,
        out_specs=(vmem,) * 7,
        scratch_shapes=[
            pltpu.VMEM((3, slab, LANES), f32),
            pltpu.VMEM((slab, LANES), f32),
            pltpu.VMEM((8 * NT, TILE), f32),
            pltpu.VMEM((2, 12 * slab, LANES), f32),
            pltpu.VMEM((3 * slab, LANES), f32),
            pltpu.SMEM((4,), jnp.int32),
            pltpu.SemaphoreType.DMA((5,)),
        ],
        compiler_params=roomy,
        name="deposit",
    )(*held(tiles, cells, fluid_vel.reshape(3, slab, LANES), fluid_frac.reshape(slab, LANES), ghosts))

    if paired:
        beside = lax.ppermute(parts, "gz", [(i, i ^ 1) for i in range(4)])
        slabs = (beside,)
    else:
        slabs = (
            shifted(parts[0:8], "gz", 1), shifted(parts[4:12], "gz", -1),
            shifted(parts[0:4], "gz", 2), shifted(parts[8:12], "gz", -2),
        )
    ya, yb = swapped(ya, yb, "gy")
    xa, xb = swapped(xa, xb, "gx")

    near, turned, value, sums, work, *across = pl.pallas_call(
        functools.partial(feature_kernel, paired),
        out_shape=(
            jax.ShapeDtypeStruct((NT * 128 + 128, TILE), bf16),
            jax.ShapeDtypeStruct((GHOST * NROW, TILE), bf16),
            jax.ShapeDtypeStruct((GHOST * VROW, TILE), bf16),
            shape((NT + 1) * VROW, TILE),
            jax.ShapeDtypeStruct((SLOTS,), jnp.int32),
        ) + ((shape(8, slab, LANES),) if paired else ()),
        in_specs=[hbm] * 3 + [vmem] * (3 if paired else 1),
        out_specs=(vmem,) * 4 + (smem,) + ((vmem,) if paired else ()),
        scratch_shapes=[
            pltpu.VMEM((NT * NROW, TILE), f32),
            pltpu.VMEM((NT * NROW, TILE), f32),
            pltpu.VMEM((NT * VROW, TILE), f32),
            pltpu.SMEM((K, NT), jnp.int32),
            pltpu.SMEM((NT,), jnp.int32),
            pltpu.SMEM((4,), jnp.int32),
            pltpu.SemaphoreType.DMA((3,)),
        ],
        compiler_params=roomy,
        name="feature",
    )(*held(lists, counts, ghosts), state_vmem, *((parts, beside) if paired else ()))
    if paired:
        slabs += (lax.ppermute(across[0], "gz", [(i, i ^ 2) for i in range(4)]),)

    sums = pl.pallas_call(
        interior_kernel,
        out_shape=shape((NT + 1) * VROW, TILE),
        in_specs=[smem] + [vmem] * 8,
        out_specs=vmem,
        scratch_shapes=[
            pltpu.VMEM((NFAR * NROW, TILE), bf16),
            pltpu.VMEM((NFAR * VROW, TILE), bf16),
            pltpu.VMEM((4 * FACE * NROW, TILE), f32),
            pltpu.VMEM((4 * FACE * VROW, TILE), f32),
        ],
        compiler_params=roomy,
        name="interior",
    )(work, near, turned, value, sums, xa, xb, ya, yb)

    velocity_new, fluid_new = pl.pallas_call(
        functools.partial(update_kernel, paired),
        out_shape=(shape(3, NT, TILE), shape(3, slab, LANES)),
        in_specs=[vmem] * (4 + len(slabs)),
        out_specs=(vmem, vmem),
        scratch_shapes=[pltpu.VMEM((9 * slab, LANES), f32)],
        compiler_params=roomy,
        name="update",
    )(state_vmem, cells_vmem, sums, parts, *slabs)
    return velocity_new.reshape(3, 1, 1, particles), fluid_new.reshape(3, 1, 1, cell_count)


def solution(mesh):
    return jax.shard_map(
        body,
        mesh=mesh,
        in_specs=(
            P(None, "gx", "gy", "gz"),
            P("gx", "gy", "gz", None),
            P("gx", "gy", "gz"),
            P("gx", "gy", "gz", None),
            P("gx", "gy", "gz"),
            P(None, "gx", "gy", "gz"),
            P("gx", "gy", "gz"),
        ),
        out_specs=(P(None, "gx", "gy", "gz"), P(None, "gx", "gy", "gz")),
        check_vma=False,
    )
```

```python
import functools

import jax
import jax.numpy as jnp
from jax import lax
from jax.experimental import pallas as pl
from jax.experimental.pallas import tpu as pltpu
from jax.sharding import PartitionSpec as P

TILE = 128
K = 8
NT = 64
GB = 12
FACE = 16
LANES = 128

stiffness = 5.0
damping = 2.0
time_step = 0.25
drag_coef = 64.0
fluid_density = 2.0
radius_ref = 0.25
spring = stiffness / damping

f32 = jnp.float32
bf16 = jnp.bfloat16

NROW = 32
VROW = 16
DUMMY = NT
GHOST = NT + 4
NFAR = GHOST + 4 * FACE
SIZES = (64, 32, 16)
GROUP = 16
EARLY = 2


def parts_of(q):
    first = q.astype(bf16).astype(f32)
    rest = q - first
    second = rest.astype(bf16).astype(f32)
    return first, second, (rest - second).astype(bf16).astype(f32)


ORDER = ((0, 0), (0, 1), (0, 2), (1, 0), (1, 1), (2, 0))


def centred(position):
    return position - 0.5


def geometry(columns):
    x, y, z = (centred(columns[k]) for k in range(3))
    r = columns[6]
    return (x, y, z, r), r * r - (x * x + y * y + z * z)


def near_rows(columns):
    lengths, own = geometry(columns)
    one = jnp.ones_like(own)
    rows = []
    for q in lengths:
        cut = parts_of(q)
        rows += [2.0 * cut[j] for _, j in ORDER]
    return rows + [one] * 3 + list(parts_of(own))


def far_rows(columns):
    lengths, own = geometry(columns)
    one = jnp.ones_like(own)
    rows = []
    for q in lengths:
        cut = parts_of(q)
        rows += [cut[i] for i, _ in ORDER]
    return rows + list(parts_of(own)) + [one] * 3


def value_rows(columns, living):
    cuts = [parts_of((columns[3 + c] - spring * centred(columns[c]))) for c in range(3)]
    return [cuts[c][k] * living for k in range(3) for c in range(3)] + [living]


def load(pairs, sems):
    copies = [pltpu.make_async_copy(source, target, sems.at[k]) for k, (source, target) in enumerate(pairs)]
    for copy in copies:
        copy.start()
    return copies


def pair_sums(far, near, values):
    weight = jnp.concatenate(
        [jnp.dot(left, right, preferred_element_type=f32) for left, right in zip(far, near)], axis=0
    )
    weight = jnp.maximum(weight, 0.0)
    coarse = weight.astype(bf16)
    fine = (weight - coarse.astype(f32)).astype(bf16)
    both = jnp.dot(values, jnp.concatenate([coarse, fine], axis=1), preferred_element_type=f32)
    return both[:, :TILE] + both[:, TILE:]


def double_pair(k, d, lists_ref, counts_ref, faces_ref):
    inside = k < NT
    t = jnp.bitwise_and(k + 4 * GB, NT - 1)
    face = lax.shift_right_logical(t * 171, 11)
    place = t - face * GB
    count = counts_ref[t]
    entries = count + (place < faces_ref[face]).astype(jnp.int32)
    ghost = faces_ref[8 + face] + place
    at = 2 * d
    first = jnp.where(at < count, lists_ref[jnp.minimum(at, K - 1), t], ghost)
    second = jnp.where(
        at + 1 < count, lists_ref[jnp.minimum(at + 1, K - 1), t], jnp.where(at + 1 < entries, ghost, DUMMY)
    )
    done = at + 2 >= entries
    following = (k + done.astype(jnp.int32), jnp.where(done, 0, d + 1))
    return jnp.where(inside, t, NT), jnp.where(inside, first, DUMMY), jnp.where(inside, second, DUMMY), following


def interior_steps(steps, size, carry, tables, near_ref, turned_ref, value_ref, acc_ref):
    def near_block(t, s):
        start = t * 128 + 96 - NROW * jnp.bitwise_and(s, 3)
        return near_ref[pl.ds(pl.multiple_of(start, NROW), 128), :]

    def far_block(s):
        return turned_ref[pl.ds(pl.multiple_of(lax.shift_right_logical(s, 2) * 128, 128), 128), :]

    def value_block(s):
        return value_ref[pl.ds(pl.multiple_of(s * VROW, VROW), VROW), :]

    def step(group, carry):
        (k, d), running = carry
        sums = []
        for _ in range(size):
            t, a, b, following = double_pair(k, d, *tables)
            near = jnp.minimum(t, NT - 1)
            total = pair_sums(
                (far_block(a), far_block(b)),
                (near_block(near, a), near_block(near, b)),
                jnp.concatenate([value_block(a), value_block(b)], axis=1),
            )
            sums.append((t, d, total))
            k, d = following
        for t, at, total in sums:
            running = total + jnp.where(at > 0, running, 0.0)
            acc_ref[pl.ds(pl.multiple_of(t * VROW, VROW), VROW), :] = running
        return (k, d), running

    return lax.fori_loop(0, steps, step, carry)


def deposit_kernel(
    state_hbm, cell_hbm, vel_hbm, frac_hbm, ghost_hbm,
    parts_ref, xa_ref, xb_ref, ya_ref, yb_ref, state_ref, cell_ref,
    vel_ref, frac_ref, source_ref, deposit_ref, total_ref, ghost_ref, sems,
):
    copies = load(
        [
            (state_hbm, state_ref), (cell_hbm, cell_ref), (vel_hbm, vel_ref), (frac_hbm, frac_ref),
            (ghost_hbm, ghost_ref),
        ],
        sems,
    )
    slab = vel_ref.shape[1]
    wide = 3 * slab
    bands = wide // 2
    even_x, even_y = (jnp.bitwise_and(lax.axis_index(axis), 1) == 0 for axis in ("gx", "gy"))
    first_band = (lax.axis_index("gz") - 1) * (slab // 2)
    for copy in copies:
        copy.wait()

    r = state_ref[6]
    rate = drag_coef * r * r
    sources = [rate * state_ref[3 + c] for c in range(3)] + [rate]
    for c, source in enumerate(sources):
        for k, part in enumerate(parts_of(source)[:2]):
            source_ref[pl.ds(4 * k + c, NT, stride=8), :] = part
    low_of = lax.broadcasted_iota(jnp.int32, (2 * LANES, LANES), 0)

    def add_group(group, total):
        cells = cell_ref[pl.ds(pl.multiple_of(group * 8, 8), 8), :]
        band = lax.shift_right_logical(cells, 8) - first_band
        low = jnp.bitwise_and(cells, 255)
        left, right = [], []
        for t in range(8):
            rows = source_ref[pl.ds(pl.multiple_of(group * 64 + t * 8, 8), 8), :]
            here = jnp.broadcast_to(band[t : t + 1, :], (8, LANES))
            left.append(jnp.concatenate([jnp.where(here == h, rows, 0.0) for h in range(bands)], axis=0).astype(bf16))
            right.append(jnp.where(low[t : t + 1, :] == low_of, 1.0, 0.0).astype(bf16))
        added = lax.dot_general(
            jnp.concatenate(left, axis=1),
            jnp.concatenate(right, axis=1),
            (((1,), (1,)), ((), ())),
            preferred_element_type=f32,
        )
        deposit_ref[0] += added[:, :LANES]
        deposit_ref[1] += added[:, LANES:]
        return total

    deposit_ref[...] = jnp.zeros_like(deposit_ref)
    lax.fori_loop(0, NT // 8, add_group, 0, unroll=8)
    frac = fluid_density * frac_ref[...]
    for c in range(4):
        for k in range(2):
            both = deposit_ref[k, pl.ds(c, bands, stride=8), :] + deposit_ref[k, pl.ds(4 + c, bands, stride=8), :]
            total_ref[pl.ds(k, bands, stride=2), :] = both * time_step
        below, here, above = (total_ref[pl.ds(k * slab, slab), :] for k in range(3))
        parts_ref[c] = above
        parts_ref[4 + c] = here + (frac * vel_ref[c] if c < 3 else frac)
        parts_ref[8 + c] = below
    order = lax.broadcasted_iota(jnp.int32, (FACE, TILE), 0)
    for low, even, a_ref, b_ref in ((0, even_x, xa_ref, xb_ref), (2, even_y, ya_ref, yb_ref)):
        for k in range(7):
            lower = state_ref[k, low * GB : (low + 1) * GB, :]
            upper = state_ref[k, (low + 1) * GB : (low + 2) * GB, :]
            a_ref[k, 0:GB, :] = jnp.where(even, upper, lower)
            b_ref[k, 0:GB, :] = jnp.where(even, lower, upper)
            a_ref[k, GB:FACE, :] = jnp.zeros((FACE - GB, TILE), f32)
            b_ref[k, GB:FACE, :] = jnp.zeros((FACE - GB, TILE), f32)
        lower, upper = ghost_ref[low], ghost_ref[low + 1]
        a_ref[7] = jnp.where(order < jnp.where(even, upper, lower), 1.0, 0.0)
        b_ref[7] = jnp.where(order < jnp.where(even, lower, upper), 1.0, 0.0)

def inner_outer():
    z = lax.axis_index("gz")
    lower = z < 2
    return lower, jnp.bitwise_and(z, 1) == jnp.where(lower, 1, 0)


def put_rows(ref, first, rows, stride, filled):
    tiles = rows[0].shape[0]
    all_rows = jnp.stack(rows + [jnp.zeros_like(rows[0])] * (filled - len(rows)), axis=0)
    ref[first * stride : (first + tiles) * stride, :] = jnp.swapaxes(all_rows, 0, 1).reshape(tiles * stride, TILE)


def facing(flag, ref):
    return [jnp.where(flag, ref[c], ref[8 + c]) for c in range(4)]


def ghost_slots():
    slot_of, beside = [], []
    for axis in ("gx", "gy"):
        place, count = lax.axis_index(axis), lax.axis_size(axis)
        first = max(slot_of, default=-1) + 1
        slot_of += [first, first if count == 2 else first + 1]
        beside += [place > 0, place < count - 1]
    return slot_of, beside


def put_faces(faces_ref, ghost_ref=None):
    slot_of, beside = ghost_slots()
    for face in range(8):
        faces_ref[face] = jnp.where(beside[face], ghost_ref[face], 0) if ghost_ref is not None and face < 4 else 0
        faces_ref[8 + face] = GHOST + slot_of[face] * FACE if face < 4 else DUMMY


def early_words(without_ghosts):
    if lax.axis_size("gz") != 4:
        return jnp.int32(0)
    return jnp.where(inner_outer()[0], GROUP * jnp.minimum(lax.div(without_ghosts, GROUP), EARLY), 0)


def bare_words(counts_ref):
    counts = [lax.shift_right_logical(counts_ref[t] + 1, 1) for t in range(4 * GB, NT)]
    total = sum(counts)
    early = early_words(total)
    k, d, passed = jnp.int32(0), early, jnp.int32(0)
    for place, count in enumerate(counts):
        passed = passed + count
        k = jnp.where(passed <= early, place + 1, k)
        d = jnp.where(passed <= early, early - passed, d)
    return total, early, (k, d)


def feature_kernel(paired, lists_hbm, counts_hbm, state_ref, *refs):
    if paired:
        parts_ref, beside_ref, *refs = refs
    near16_ref, turned_ref, value16_ref, acc_ref, *refs = refs
    if paired:
        across_ref, *refs = refs
    near_ref, far_ref, value_ref, lists_ref, counts_ref, faces_ref, sems = refs
    copies = load([(lists_hbm, lists_ref), (counts_hbm, counts_ref)], sems)
    if paired:
        lower, inner = inner_outer()
        mine, other = facing(lower, parts_ref), facing(lower, beside_ref)
        for c in range(4):
            across_ref[c] = jnp.where(inner, parts_ref[4 + c] + other[c], beside_ref[4 + c] + mine[c])
            across_ref[4 + c] = jnp.where(inner, mine[c], other[c])
    near16_ref[pl.ds(NT * 128, 128), :] = jnp.zeros((128, TILE), bf16)
    turned_ref[DUMMY * NROW : GHOST * NROW, :] = jnp.zeros((4 * NROW, TILE), bf16)
    value16_ref[DUMMY * VROW : GHOST * VROW, :] = jnp.zeros((4 * VROW, TILE), bf16)

    columns = [state_ref[k] for k in range(7)]
    put_rows(near_ref, 0, near_rows(columns), NROW, NROW)
    put_rows(far_ref, 0, far_rows(columns), NROW, NROW)
    put_rows(value_ref, 0, value_rows(columns, jnp.ones((NT, TILE), f32)), VROW, VROW)
    for b in range(NT // 4):
        rows = slice(b * 128, (b + 1) * 128)
        turned_ref[rows, :] = far_ref[rows, :].T.astype(bf16)
        rows = slice(b * 4 * VROW, (b + 1) * 4 * VROW)
        value16_ref[rows, :] = value_ref[rows, :].astype(bf16)
    for t in range(NT):
        near16_ref[t * 128 : (t + 1) * 128, :] = jnp.concatenate(
            [jnp.zeros((96, TILE), bf16), near_ref[t * NROW : (t + 1) * NROW, :].astype(bf16)], axis=0
        )
    for copy in copies:
        copy.wait()
    if paired:
        @pl.when(lower)
        def _():
            put_faces(faces_ref)
            _, words, _ = bare_words(counts_ref)
            carry = ((jnp.int32(0), jnp.int32(0)), jnp.zeros((VROW, TILE), f32))
            tables = (lists_ref, counts_ref, faces_ref)
            interior_steps(
                lax.div(words, GROUP), GROUP, carry, tables, near16_ref, turned_ref, value16_ref, acc_ref
            )


def interior_kernel(
    lists_hbm, counts_hbm, ghost_hbm, near_ref, own_turned_ref, own_value_ref, before_ref,
    xa_ref, xb_ref, ya_ref, yb_ref,
    acc_ref, turned_ref, value_ref, far_ref, cut_ref, lists_ref, counts_ref, ghost_ref, faces_ref, sems,
):
    copies = load([(lists_hbm, lists_ref), (counts_hbm, counts_ref), (ghost_hbm, ghost_ref)], sems)
    slots = []
    for axis, a_ref, b_ref in (("gx", xa_ref, xb_ref), ("gy", ya_ref, yb_ref)):
        even = jnp.bitwise_and(lax.axis_index(axis), 1) == 0
        a, b = ([ref[k] for k in range(8)] for ref in (a_ref, b_ref))
        if lax.axis_size(axis) == 2:
            slots.append(a)
        else:
            slots.append([jnp.where(even, q, p) for p, q in zip(a, b)])
            slots.append([jnp.where(even, p, q) for p, q in zip(a, b)])
    columns = [jnp.concatenate([slot[k] for slot in slots], axis=0) for k in range(8)]
    put_rows(far_ref, 0, far_rows(columns), NROW, NROW)
    put_rows(cut_ref, 0, value_rows(columns, columns[7]), VROW, VROW)
    turned_ref[0 : GHOST * NROW, :] = own_turned_ref[...]
    value_ref[0 : GHOST * VROW, :] = own_value_ref[...]
    ghosts = len(slots) * FACE
    value_ref[GHOST * VROW : (GHOST + ghosts) * VROW, :] = cut_ref[0 : ghosts * VROW, :].astype(bf16)
    for b in range(ghosts // 4):
        turned_ref[GHOST * NROW + b * 128 : GHOST * NROW + (b + 1) * 128, :] = (
            far_ref[b * 128 : (b + 1) * 128, :].T.astype(bf16)
        )
    for copy in copies:
        copy.wait()
    put_faces(faces_ref, ghost_ref)
    bare, begin, place = bare_words(counts_ref)
    left = bare - begin
    for t in range(4 * GB):
        ghost = (t % GB < faces_ref[t // GB]).astype(jnp.int32)
        left = left + lax.shift_right_logical(counts_ref[t] + ghost + 1, 1)

    @pl.when(begin > 0)
    def _():
        rows = slice(4 * GB * VROW, NT * VROW)
        acc_ref[rows, :] = before_ref[rows, :]

    tile = jnp.bitwise_and(place[0] + 4 * GB, NT - 1)
    carry = (place, before_ref[pl.ds(pl.multiple_of(tile * VROW, VROW), VROW), :])
    tables = (lists_ref, counts_ref, faces_ref)
    for size in SIZES:
        steps = lax.div(left + (GROUP - 1 if size > GROUP else size - 1), size)
        carry = interior_steps(steps, size, carry, tables, near_ref, turned_ref, value_ref, acc_ref)
        left = jnp.maximum(left - steps * size, 0)


def solved(total):
    return [total[c] / total[3] for c in range(3)]


def added(*terms):
    return [sum(values[1:], values[0]) for values in zip(*terms)]


def paired_slabs(parts_ref, beside_ref, across_ref):
    lower, inner = inner_outer()
    own, other = ([ref[4 + c] for c in range(4)] for ref in (parts_ref, beside_ref))
    mine_to, other_to = facing(lower, parts_ref), facing(lower, beside_ref)
    away = jnp.logical_not(lower)
    mine_from, other_from = facing(away, parts_ref), facing(away, beside_ref)
    summed, single = ([across_ref[k + c] for c in range(4)] for k in (0, 4))

    def chosen(first, second):
        return [jnp.where(inner, p, q) for p, q in zip(first, second)]

    here = solved(chosen(added(own, other_to, single), added(own, other_from)))
    near = solved(chosen(added(other, mine_from), added(other, mine_to, single)))
    past = solved(added(summed, mine_to))
    even = jnp.bitwise_and(lax.axis_index("gz"), 1) == 0
    below = [jnp.where(even, p, q) for p, q in zip(past, near)]
    above = [jnp.where(even, q, p) for p, q in zip(past, near)]
    return below, here, above


def ring_slabs(parts_ref, below_ref, above_ref, far_below_ref, far_above_ref):
    z, count = lax.axis_index("gz"), lax.axis_size("gz")

    def rows(ref, first):
        return [ref[first + c] for c in range(4)]

    def inside(flag, values, other=0.0):
        return [jnp.where(flag, value, other) for value in values]

    has_below, has_above = z >= 1, z <= count - 2
    here = added(rows(parts_ref, 4), inside(has_below, rows(below_ref, 0)), inside(has_above, rows(above_ref, 4)))
    below = added(
        inside(has_below, rows(below_ref, 4), 1.0), rows(parts_ref, 8), inside(z >= 2, rows(far_below_ref, 0))
    )
    above = added(
        inside(has_above, rows(above_ref, 0), 1.0), rows(parts_ref, 0), inside(z <= count - 3, rows(far_above_ref, 0))
    )
    return solved(below), solved(here), solved(above)


def update_kernel(paired, state_ref, cell_ref, acc_ref, parts_ref, *refs):
    slabs, refs = (refs[:2], refs[2:]) if paired else (refs[:4], refs[4:])
    new_ref, fluid_ref, table_ref = refs
    slab = parts_ref.shape[1]
    wide = 3 * slab
    first_row = (lax.axis_index("gz") - 1) * slab
    lower, here, upper = (paired_slabs if paired else ring_slabs)(parts_ref, *slabs)
    for c in range(3):
        fluid_ref[c] = here[c]
        table_ref[pl.ds(c * wide, slab), :] = lower[c]
        table_ref[pl.ds(c * wide + slab, slab), :] = here[c]
        table_ref[pl.ds(c * wide + 2 * slab, slab), :] = upper[c]

    def update_group(group, carry):
        rows = pl.ds(pl.multiple_of(group * 8, 8), 8)

        def sums(k):
            return acc_ref[pl.ds(group * 8 * VROW + k, 8, stride=VROW), :]

        weight = sums(9)
        cells = cell_ref[rows, :]
        high = lax.shift_right_logical(cells, 7) - first_row
        low = jnp.bitwise_and(cells, LANES - 1)
        at_cell = [jnp.zeros((8, LANES), f32)] * 3
        for h in range(wide):
            chosen = high == h
            for c in range(3):
                line = jnp.broadcast_to(table_ref[c * wide + h : c * wide + h + 1, :], (8, LANES))
                taken = jnp.take_along_axis(line, low, axis=1, mode="promise_in_bounds")
                at_cell[c] = jnp.where(chosen, taken, at_cell[c])
        r = state_ref[6, rows, :]
        ratio = r / radius_ref
        masses = ratio * ratio * ratio
        rate = drag_coef * r * r
        coupling = time_step * rate / masses
        for c in range(3):
            velocity = state_ref[3 + c, rows, :]
            lever = velocity - spring * centred(state_ref[c, rows, :])
            force = -damping * (lever * weight - (sums(c) + sums(3 + c) + sums(6 + c)))
            moved = velocity + time_step * force / masses
            new_ref[c, rows, :] = (moved + coupling * at_cell[c]) / (1.0 + coupling)
        return carry

    lax.fori_loop(0, NT // 8, update_group, 0, unroll=8)


def shifted(value, axis, steps):
    count = lax.axis_size(axis)
    return lax.ppermute(value, axis, [(i, (i + steps) % count) for i in range(count)])


def swapped(first, second, axis):
    count = lax.axis_size(axis)
    first = lax.ppermute(first, axis, [(i, i ^ 1) for i in range(count)])
    if count == 2:
        return first, first
    return first, lax.ppermute(second, axis, [(i, (i + (1 if i % 2 else -1)) % count) for i in range(count)])


vmem = pl.BlockSpec(memory_space=pltpu.VMEM)
hbm = pl.BlockSpec(memory_space=pltpu.HBM)
roomy = pltpu.CompilerParams(vmem_limit_bytes=24 * 2**20)


def body(state, tile_lists, tile_counts, ghost_counts, cell_index, fluid_vel, fluid_frac):
    particles = state.shape[3]
    cell_count = fluid_vel.shape[3]
    slab = cell_count // LANES
    tiles = state.reshape(7, NT, TILE)
    cells = cell_index.reshape(NT, TILE)
    lists = tile_lists.reshape(NT, K).T
    counts = tile_counts.reshape(NT)
    ghosts = ghost_counts.reshape(4)

    def shape(*dims):
        return jax.ShapeDtypeStruct(dims, f32)

    def held(*values):
        return [pltpu.with_memory_space_constraint(value, pltpu.HBM) for value in values]

    face = shape(8, FACE, TILE)
    paired = lax.axis_size("gz") == 4
    parts, xa, xb, ya, yb, state_vmem, cells_vmem = pl.pallas_call(
        deposit_kernel,
        out_shape=(
            shape(12, slab, LANES), face, face, face, face,
            shape(7, NT, TILE), jax.ShapeDtypeStruct((NT, TILE), jnp.int32),
        ),
        in_specs=[hbm] * 5,
        out_specs=(vmem,) * 7,
        scratch_shapes=[
            pltpu.VMEM((3, slab, LANES), f32),
            pltpu.VMEM((slab, LANES), f32),
            pltpu.VMEM((8 * NT, TILE), f32),
            pltpu.VMEM((2, 12 * slab, LANES), f32),
            pltpu.VMEM((3 * slab, LANES), f32),
            pltpu.SMEM((4,), jnp.int32),
            pltpu.SemaphoreType.DMA((5,)),
        ],
        compiler_params=roomy,
        name="deposit",
    )(*held(tiles, cells, fluid_vel.reshape(3, slab, LANES), fluid_frac.reshape(slab, LANES), ghosts))

    if paired:
        beside = lax.ppermute(parts, "gz", [(i, i ^ 1) for i in range(4)])
        slabs = (beside,)
    else:
        slabs = (
            shifted(parts[0:8], "gz", 1), shifted(parts[4:12], "gz", -1),
            shifted(parts[0:4], "gz", 2), shifted(parts[8:12], "gz", -2),
        )
    ya, yb = swapped(ya, yb, "gy")
    xa, xb = swapped(xa, xb, "gx")

    near, turned, value, sums, *across = pl.pallas_call(
        functools.partial(feature_kernel, paired),
        out_shape=(
            jax.ShapeDtypeStruct((NT * 128 + 128, TILE), bf16),
            jax.ShapeDtypeStruct((GHOST * NROW, TILE), bf16),
            jax.ShapeDtypeStruct((GHOST * VROW, TILE), bf16),
            shape((NT + 1) * VROW, TILE),
        ) + ((shape(8, slab, LANES),) if paired else ()),
        in_specs=[hbm] * 2 + [vmem] * (3 if paired else 1),
        out_specs=(vmem,) * (5 if paired else 4),
        scratch_shapes=[
            pltpu.VMEM((NT * NROW, TILE), f32),
            pltpu.VMEM((NT * NROW, TILE), f32),
            pltpu.VMEM((NT * VROW, TILE), f32),
            pltpu.SMEM((K, NT), jnp.int32),
            pltpu.SMEM((NT,), jnp.int32),
            pltpu.SMEM((16,), jnp.int32),
            pltpu.SemaphoreType.DMA((2,)),
        ],
        compiler_params=roomy,
        name="feature",
    )(*held(lists, counts), state_vmem, *((parts, beside) if paired else ()))
    if paired:
        slabs += (lax.ppermute(across[0], "gz", [(i, i ^ 2) for i in range(4)]),)

    sums = pl.pallas_call(
        interior_kernel,
        out_shape=shape((NT + 1) * VROW, TILE),
        in_specs=[hbm] * 3 + [vmem] * 8,
        out_specs=vmem,
        scratch_shapes=[
            pltpu.VMEM((NFAR * NROW, TILE), bf16),
            pltpu.VMEM((NFAR * VROW, TILE), bf16),
            pltpu.VMEM((4 * FACE * NROW, TILE), f32),
            pltpu.VMEM((4 * FACE * VROW, TILE), f32),
            pltpu.SMEM((K, NT), jnp.int32),
            pltpu.SMEM((NT,), jnp.int32),
            pltpu.SMEM((4,), jnp.int32),
            pltpu.SMEM((16,), jnp.int32),
            pltpu.SemaphoreType.DMA((3,)),
        ],
        compiler_params=roomy,
        name="interior",
    )(*held(lists, counts, ghosts), near, turned, value, sums, xa, xb, ya, yb)

    velocity_new, fluid_new = pl.pallas_call(
        functools.partial(update_kernel, paired),
        out_shape=(shape(3, NT, TILE), shape(3, slab, LANES)),
        in_specs=[vmem] * (4 + len(slabs)),
        out_specs=(vmem, vmem),
        scratch_shapes=[pltpu.VMEM((9 * slab, LANES), f32)],
        compiler_params=roomy,
        name="update",
    )(state_vmem, cells_vmem, sums, parts, *slabs)
    return velocity_new.reshape(3, 1, 1, particles), fluid_new.reshape(3, 1, 1, cell_count)


def solution(mesh):
    return jax.shard_map(
        body,
        mesh=mesh,
        in_specs=(
            P(None, "gx", "gy", "gz"),
            P("gx", "gy", "gz", None),
            P("gx", "gy", "gz"),
            P("gx", "gy", "gz", None),
            P("gx", "gy", "gz"),
            P(None, "gx", "gy", "gz"),
            P("gx", "gy", "gz"),
        ),
        out_specs=(P(None, "gx", "gy", "gz"), P(None, "gx", "gy", "gz")),
        check_vma=False,
    )
```

```python
import functools

import jax
import jax.numpy as jnp
from jax import lax
from jax.experimental import pallas as pl
from jax.experimental.pallas import tpu as pltpu
from jax.sharding import PartitionSpec as P

TILE = 128
K = 8
NT = 64
GB = 12
FACE = 16
LANES = 128

stiffness = 5.0
damping = 2.0
time_step = 0.25
drag_coef = 64.0
fluid_density = 2.0
radius_ref = 0.25
spring = stiffness / damping

f32 = jnp.float32
bf16 = jnp.bfloat16

NROW = 32
VROW = 16
DUMMY = NT
GHOST = NT + 4
NFAR = GHOST + 4 * FACE
SIZES = (64, 32, 16)
GROUP = 16
EARLY = (32, 8)


def parts_of(q):
    first = q.astype(bf16).astype(f32)
    rest = q - first
    second = rest.astype(bf16).astype(f32)
    return first, second, (rest - second).astype(bf16).astype(f32)


ORDER = ((0, 0), (0, 1), (0, 2), (1, 0), (1, 1), (2, 0))


def centred(position):
    return position - 0.5


def geometry(columns):
    x, y, z = (centred(columns[k]) for k in range(3))
    r = columns[6]
    return (x, y, z, r), r * r - (x * x + y * y + z * z)


def near_rows(columns):
    lengths, own = geometry(columns)
    one = jnp.ones_like(own)
    rows = []
    for q in lengths:
        cut = parts_of(q)
        rows += [2.0 * cut[j] for _, j in ORDER]
    return rows + [one] * 3 + list(parts_of(own))


def far_rows(columns):
    lengths, own = geometry(columns)
    one = jnp.ones_like(own)
    rows = []
    for q in lengths:
        cut = parts_of(q)
        rows += [cut[i] for i, _ in ORDER]
    return rows + list(parts_of(own)) + [one] * 3


def value_rows(columns, living):
    cuts = [parts_of((columns[3 + c] - spring * centred(columns[c]))) for c in range(3)]
    return [cuts[c][k] * living for k in range(3) for c in range(3)] + [living]


def load(pairs, sems):
    copies = [pltpu.make_async_copy(source, target, sems.at[k]) for k, (source, target) in enumerate(pairs)]
    for copy in copies:
        copy.start()
    return copies


def pair_sums(far, near, values):
    weight = jnp.concatenate(
        [jnp.dot(left, right, preferred_element_type=f32) for left, right in zip(far, near)], axis=0
    )
    weight = jnp.maximum(weight, 0.0)
    coarse = weight.astype(bf16)
    fine = (weight - coarse.astype(f32)).astype(bf16)
    both = jnp.dot(values, jnp.concatenate([coarse, fine], axis=1), preferred_element_type=f32)
    return both[:, :TILE] + both[:, TILE:]


def double_pair(k, d, lists_ref, counts_ref, faces_ref):
    inside = k < NT
    t = jnp.bitwise_and(k + 4 * GB, NT - 1)
    face = lax.shift_right_logical(t * 171, 11)
    place = t - face * GB
    count = counts_ref[t]
    entries = count + (place < faces_ref[face]).astype(jnp.int32)
    ghost = faces_ref[8 + face] + place
    at = 2 * d
    first = jnp.where(at < count, lists_ref[jnp.minimum(at, K - 1), t], ghost)
    second = jnp.where(
        at + 1 < count, lists_ref[jnp.minimum(at + 1, K - 1), t], jnp.where(at + 1 < entries, ghost, DUMMY)
    )
    done = at + 2 >= entries
    following = (k + done.astype(jnp.int32), jnp.where(done, 0, d + 1))
    return jnp.where(inside, t, NT), jnp.where(inside, first, DUMMY), jnp.where(inside, second, DUMMY), following


def interior_steps(steps, size, carry, tables, near_ref, turned_ref, value_ref, acc_ref):
    def near_block(t, s):
        start = t * 128 + 96 - NROW * jnp.bitwise_and(s, 3)
        return near_ref[pl.ds(pl.multiple_of(start, NROW), 128), :]

    def far_block(s):
        return turned_ref[pl.ds(pl.multiple_of(lax.shift_right_logical(s, 2) * 128, 128), 128), :]

    def value_block(s):
        return value_ref[pl.ds(pl.multiple_of(s * VROW, VROW), VROW), :]

    def step(group, carry):
        (k, d), running = carry
        sums = []
        for _ in range(size):
            t, a, b, following = double_pair(k, d, *tables)
            near = jnp.minimum(t, NT - 1)
            total = pair_sums(
                (far_block(a), far_block(b)),
                (near_block(near, a), near_block(near, b)),
                jnp.concatenate([value_block(a), value_block(b)], axis=1),
            )
            sums.append((t, d, total))
            k, d = following
        for t, at, total in sums:
            running = total + jnp.where(at > 0, running, 0.0)
            acc_ref[pl.ds(pl.multiple_of(t * VROW, VROW), VROW), :] = running
        return (k, d), running

    return lax.fori_loop(0, steps, step, carry)


def deposit_kernel(
    state_hbm, cell_hbm, vel_hbm, frac_hbm, ghost_hbm,
    parts_ref, xa_ref, xb_ref, ya_ref, yb_ref, state_ref, cell_ref,
    vel_ref, frac_ref, source_ref, deposit_ref, total_ref, ghost_ref, sems,
):
    copies = load(
        [
            (state_hbm, state_ref), (cell_hbm, cell_ref), (vel_hbm, vel_ref), (frac_hbm, frac_ref),
            (ghost_hbm, ghost_ref),
        ],
        sems,
    )
    slab = vel_ref.shape[1]
    wide = 3 * slab
    bands = wide // 2
    even_x, even_y = (jnp.bitwise_and(lax.axis_index(axis), 1) == 0 for axis in ("gx", "gy"))
    first_band = (lax.axis_index("gz") - 1) * (slab // 2)
    for copy in copies:
        copy.wait()

    r = state_ref[6]
    rate = drag_coef * r * r
    sources = [rate * state_ref[3 + c] for c in range(3)] + [rate]
    for c, source in enumerate(sources):
        for k, part in enumerate(parts_of(source)[:2]):
            source_ref[pl.ds(4 * k + c, NT, stride=8), :] = part
    low_of = lax.broadcasted_iota(jnp.int32, (2 * LANES, LANES), 0)

    def add_group(group, total):
        cells = cell_ref[pl.ds(pl.multiple_of(group * 8, 8), 8), :]
        band = lax.shift_right_logical(cells, 8) - first_band
        low = jnp.bitwise_and(cells, 255)
        left, right = [], []
        for t in range(8):
            rows = source_ref[pl.ds(pl.multiple_of(group * 64 + t * 8, 8), 8), :]
            here = jnp.broadcast_to(band[t : t + 1, :], (8, LANES))
            left.append(jnp.concatenate([jnp.where(here == h, rows, 0.0) for h in range(bands)], axis=0).astype(bf16))
            right.append(jnp.where(low[t : t + 1, :] == low_of, 1.0, 0.0).astype(bf16))
        added = lax.dot_general(
            jnp.concatenate(left, axis=1),
            jnp.concatenate(right, axis=1),
            (((1,), (1,)), ((), ())),
            preferred_element_type=f32,
        )
        deposit_ref[0] += added[:, :LANES]
        deposit_ref[1] += added[:, LANES:]
        return total

    deposit_ref[...] = jnp.zeros_like(deposit_ref)
    lax.fori_loop(0, NT // 8, add_group, 0, unroll=8)
    frac = fluid_density * frac_ref[...]
    for c in range(4):
        for k in range(2):
            both = deposit_ref[k, pl.ds(c, bands, stride=8), :] + deposit_ref[k, pl.ds(4 + c, bands, stride=8), :]
            total_ref[pl.ds(k, bands, stride=2), :] = both * time_step
        below, here, above = (total_ref[pl.ds(k * slab, slab), :] for k in range(3))
        parts_ref[c] = above
        parts_ref[4 + c] = here + (frac * vel_ref[c] if c < 3 else frac)
        parts_ref[8 + c] = below
    order = lax.broadcasted_iota(jnp.int32, (FACE, TILE), 0)
    for low, even, a_ref, b_ref in ((0, even_x, xa_ref, xb_ref), (2, even_y, ya_ref, yb_ref)):
        for k in range(7):
            lower = state_ref[k, low * GB : (low + 1) * GB, :]
            upper = state_ref[k, (low + 1) * GB : (low + 2) * GB, :]
            a_ref[k, 0:GB, :] = jnp.where(even, upper, lower)
            b_ref[k, 0:GB, :] = jnp.where(even, lower, upper)
            a_ref[k, GB:FACE, :] = jnp.zeros((FACE - GB, TILE), f32)
            b_ref[k, GB:FACE, :] = jnp.zeros((FACE - GB, TILE), f32)
        lower, upper = ghost_ref[low], ghost_ref[low + 1]
        a_ref[7] = jnp.where(order < jnp.where(even, upper, lower), 1.0, 0.0)
        b_ref[7] = jnp.where(order < jnp.where(even, lower, upper), 1.0, 0.0)

def inner_outer():
    z = lax.axis_index("gz")
    lower = z < 2
    return lower, jnp.bitwise_and(z, 1) == jnp.where(lower, 1, 0)


def put_rows(ref, first, rows, stride, filled):
    tiles = rows[0].shape[0]
    all_rows = jnp.stack(rows + [jnp.zeros_like(rows[0])] * (filled - len(rows)), axis=0)
    ref[first * stride : (first + tiles) * stride, :] = jnp.swapaxes(all_rows, 0, 1).reshape(tiles * stride, TILE)


def facing(flag, ref):
    return [jnp.where(flag, ref[c], ref[8 + c]) for c in range(4)]


def ghost_slots():
    slot_of, beside = [], []
    for axis in ("gx", "gy"):
        place, count = lax.axis_index(axis), lax.axis_size(axis)
        first = max(slot_of, default=-1) + 1
        slot_of += [first, first if count == 2 else first + 1]
        beside += [place > 0, place < count - 1]
    return slot_of, beside


def put_faces(faces_ref, ghost_ref=None):
    slot_of, beside = ghost_slots()
    for face in range(8):
        faces_ref[face] = jnp.where(beside[face], ghost_ref[face], 0) if ghost_ref is not None and face < 4 else 0
        faces_ref[8 + face] = GHOST + slot_of[face] * FACE if face < 4 else DUMMY


def early_words(without_ghosts):
    if lax.axis_size("gz") != 4:
        return jnp.int32(0)
    words = jnp.int32(0)
    for size in EARLY:
        words = words + jnp.where(without_ghosts - words >= size, size, 0)
    return jnp.where(inner_outer()[0], words, 0)


def bare_words(counts_ref):
    counts = [lax.shift_right_logical(counts_ref[t] + 1, 1) for t in range(4 * GB, NT)]
    total = sum(counts)
    early = early_words(total)
    k, d, passed = jnp.int32(0), early, jnp.int32(0)
    for place, count in enumerate(counts):
        passed = passed + count
        k = jnp.where(passed <= early, place + 1, k)
        d = jnp.where(passed <= early, early - passed, d)
    return total, early, (k, d)


def feature_kernel(paired, lists_hbm, counts_hbm, state_ref, *refs):
    if paired:
        parts_ref, beside_ref, *refs = refs
    near16_ref, turned_ref, value16_ref, acc_ref, *refs = refs
    if paired:
        across_ref, *refs = refs
    near_ref, far_ref, value_ref, lists_ref, counts_ref, faces_ref, sems = refs
    copies = load([(lists_hbm, lists_ref), (counts_hbm, counts_ref)], sems)
    if paired:
        lower, inner = inner_outer()
        mine, other = facing(lower, parts_ref), facing(lower, beside_ref)
        for c in range(4):
            across_ref[c] = jnp.where(inner, parts_ref[4 + c] + other[c], beside_ref[4 + c] + mine[c])
            across_ref[4 + c] = jnp.where(inner, mine[c], other[c])
    near16_ref[pl.ds(NT * 128, 128), :] = jnp.zeros((128, TILE), bf16)
    turned_ref[DUMMY * NROW : GHOST * NROW, :] = jnp.zeros((4 * NROW, TILE), bf16)
    value16_ref[DUMMY * VROW : GHOST * VROW, :] = jnp.zeros((4 * VROW, TILE), bf16)

    columns = [state_ref[k] for k in range(7)]
    put_rows(near_ref, 0, near_rows(columns), NROW, NROW)
    put_rows(far_ref, 0, far_rows(columns), NROW, NROW)
    put_rows(value_ref, 0, value_rows(columns, jnp.ones((NT, TILE), f32)), VROW, VROW)
    for b in range(NT // 4):
        rows = slice(b * 128, (b + 1) * 128)
        turned_ref[rows, :] = far_ref[rows, :].T.astype(bf16)
        rows = slice(b * 4 * VROW, (b + 1) * 4 * VROW)
        value16_ref[rows, :] = value_ref[rows, :].astype(bf16)
    for t in range(NT):
        near16_ref[t * 128 : (t + 1) * 128, :] = jnp.concatenate(
            [jnp.zeros((96, TILE), bf16), near_ref[t * NROW : (t + 1) * NROW, :].astype(bf16)], axis=0
        )
    for copy in copies:
        copy.wait()
    if paired:
        @pl.when(lower)
        def _():
            put_faces(faces_ref)
            _, words, _ = bare_words(counts_ref)
            carry = ((jnp.int32(0), jnp.int32(0)), jnp.zeros((VROW, TILE), f32))
            tables = (lists_ref, counts_ref, faces_ref)
            for size in EARLY:
                steps = (words >= size).astype(jnp.int32)
                carry = interior_steps(
                    steps, size, carry, tables, near16_ref, turned_ref, value16_ref, acc_ref
                )
                words = words - steps * size


def interior_kernel(
    lists_hbm, counts_hbm, ghost_hbm, near_ref, own_turned_ref, own_value_ref, before_ref,
    xa_ref, xb_ref, ya_ref, yb_ref,
    acc_ref, turned_ref, value_ref, far_ref, cut_ref, lists_ref, counts_ref, ghost_ref, faces_ref, sems,
):
    copies = load([(lists_hbm, lists_ref), (counts_hbm, counts_ref), (ghost_hbm, ghost_ref)], sems)
    slots = []
    for axis, a_ref, b_ref in (("gx", xa_ref, xb_ref), ("gy", ya_ref, yb_ref)):
        even = jnp.bitwise_and(lax.axis_index(axis), 1) == 0
        a, b = ([ref[k] for k in range(8)] for ref in (a_ref, b_ref))
        if lax.axis_size(axis) == 2:
            slots.append(a)
        else:
            slots.append([jnp.where(even, q, p) for p, q in zip(a, b)])
            slots.append([jnp.where(even, p, q) for p, q in zip(a, b)])
    columns = [jnp.concatenate([slot[k] for slot in slots], axis=0) for k in range(8)]
    put_rows(far_ref, 0, far_rows(columns), NROW, NROW)
    put_rows(cut_ref, 0, value_rows(columns, columns[7]), VROW, VROW)
    turned_ref[0 : GHOST * NROW, :] = own_turned_ref[...]
    value_ref[0 : GHOST * VROW, :] = own_value_ref[...]
    ghosts = len(slots) * FACE
    value_ref[GHOST * VROW : (GHOST + ghosts) * VROW, :] = cut_ref[0 : ghosts * VROW, :].astype(bf16)
    for b in range(ghosts // 4):
        turned_ref[GHOST * NROW + b * 128 : GHOST * NROW + (b + 1) * 128, :] = (
            far_ref[b * 128 : (b + 1) * 128, :].T.astype(bf16)
        )
    for copy in copies:
        copy.wait()
    put_faces(faces_ref, ghost_ref)
    bare, begin, place = bare_words(counts_ref)
    left = bare - begin
    for t in range(4 * GB):
        ghost = (t % GB < faces_ref[t // GB]).astype(jnp.int32)
        left = left + lax.shift_right_logical(counts_ref[t] + ghost + 1, 1)

    @pl.when(begin > 0)
    def _():
        rows = slice(4 * GB * VROW, NT * VROW)
        acc_ref[rows, :] = before_ref[rows, :]

    tile = jnp.bitwise_and(place[0] + 4 * GB, NT - 1)
    carry = (place, before_ref[pl.ds(pl.multiple_of(tile * VROW, VROW), VROW), :])
    tables = (lists_ref, counts_ref, faces_ref)
    for size in SIZES:
        steps = lax.div(left + (GROUP - 1 if size > GROUP else size - 1), size)
        carry = interior_steps(steps, size, carry, tables, near_ref, turned_ref, value_ref, acc_ref)
        left = jnp.maximum(left - steps * size, 0)


def solved(total):
    return [total[c] / total[3] for c in range(3)]


def added(*terms):
    return [sum(values[1:], values[0]) for values in zip(*terms)]


def paired_slabs(parts_ref, beside_ref, across_ref):
    lower, inner = inner_outer()
    own, other = ([ref[4 + c] for c in range(4)] for ref in (parts_ref, beside_ref))
    mine_to, other_to = facing(lower, parts_ref), facing(lower, beside_ref)
    away = jnp.logical_not(lower)
    mine_from, other_from = facing(away, parts_ref), facing(away, beside_ref)
    summed, single = ([across_ref[k + c] for c in range(4)] for k in (0, 4))

    def chosen(first, second):
        return [jnp.where(inner, p, q) for p, q in zip(first, second)]

    here = solved(chosen(added(own, other_to, single), added(own, other_from)))
    near = solved(chosen(added(other, mine_from), added(other, mine_to, single)))
    past = solved(added(summed, mine_to))
    even = jnp.bitwise_and(lax.axis_index("gz"), 1) == 0
    below = [jnp.where(even, p, q) for p, q in zip(past, near)]
    above = [jnp.where(even, q, p) for p, q in zip(past, near)]
    return below, here, above


def ring_slabs(parts_ref, below_ref, above_ref, far_below_ref, far_above_ref):
    z, count = lax.axis_index("gz"), lax.axis_size("gz")

    def rows(ref, first):
        return [ref[first + c] for c in range(4)]

    def inside(flag, values, other=0.0):
        return [jnp.where(flag, value, other) for value in values]

    has_below, has_above = z >= 1, z <= count - 2
    here = added(rows(parts_ref, 4), inside(has_below, rows(below_ref, 0)), inside(has_above, rows(above_ref, 4)))
    below = added(
        inside(has_below, rows(below_ref, 4), 1.0), rows(parts_ref, 8), inside(z >= 2, rows(far_below_ref, 0))
    )
    above = added(
        inside(has_above, rows(above_ref, 0), 1.0), rows(parts_ref, 0), inside(z <= count - 3, rows(far_above_ref, 0))
    )
    return solved(below), solved(here), solved(above)


def update_kernel(paired, state_ref, cell_ref, acc_ref, parts_ref, *refs):
    slabs, refs = (refs[:2], refs[2:]) if paired else (refs[:4], refs[4:])
    new_ref, fluid_ref, table_ref = refs
    slab = parts_ref.shape[1]
    wide = 3 * slab
    first_row = (lax.axis_index("gz") - 1) * slab
    lower, here, upper = (paired_slabs if paired else ring_slabs)(parts_ref, *slabs)
    for c in range(3):
        fluid_ref[c] = here[c]
        table_ref[pl.ds(c * wide, slab), :] = lower[c]
        table_ref[pl.ds(c * wide + slab, slab), :] = here[c]
        table_ref[pl.ds(c * wide + 2 * slab, slab), :] = upper[c]

    def update_group(group, carry):
        rows = pl.ds(pl.multiple_of(group * 8, 8), 8)

        def sums(k):
            return acc_ref[pl.ds(group * 8 * VROW + k, 8, stride=VROW), :]

        weight = sums(9)
        cells = cell_ref[rows, :]
        high = lax.shift_right_logical(cells, 7) - first_row
        low = jnp.bitwise_and(cells, LANES - 1)
        at_cell = [jnp.zeros((8, LANES), f32)] * 3
        for h in range(wide):
            chosen = high == h
            for c in range(3):
                line = jnp.broadcast_to(table_ref[c * wide + h : c * wide + h + 1, :], (8, LANES))
                taken = jnp.take_along_axis(line, low, axis=1, mode="promise_in_bounds")
                at_cell[c] = jnp.where(chosen, taken, at_cell[c])
        r = state_ref[6, rows, :]
        ratio = r / radius_ref
        masses = ratio * ratio * ratio
        rate = drag_coef * r * r
        coupling = time_step * rate / masses
        for c in range(3):
            velocity = state_ref[3 + c, rows, :]
            lever = velocity - spring * centred(state_ref[c, rows, :])
            force = -damping * (lever * weight - (sums(c) + sums(3 + c) + sums(6 + c)))
            moved = velocity + time_step * force / masses
            new_ref[c, rows, :] = (moved + coupling * at_cell[c]) / (1.0 + coupling)
        return carry

    lax.fori_loop(0, NT // 8, update_group, 0, unroll=8)


def shifted(value, axis, steps):
    count = lax.axis_size(axis)
    return lax.ppermute(value, axis, [(i, (i + steps) % count) for i in range(count)])


def rung(first, second, axis):
    count = lax.axis_size(axis)
    first = lax.ppermute(first, axis, [(i, i ^ 1) for i in range(count)])
    return first, lax.ppermute(second, axis, [(i, (i + (1 if i % 2 else -1)) % count) for i in range(count)])


def swapped(first, second, axis, core):
    count = lax.axis_size(axis)
    first = lax.ppermute(first, axis, [(i, i ^ 1) for i in range(count)])
    cores = lax.axis_size(core)
    pairs = []
    for i in range(count):
        partner = i + 1 if i % 2 else i - 1
        for c in range(cores):
            to = (partner, c) if 0 <= partner < count else (i, c ^ 1)
            pairs.append((i * cores + c, to[0] * cores + to[1]))
    return first, lax.ppermute(second, (axis, core), pairs)


vmem = pl.BlockSpec(memory_space=pltpu.VMEM)
hbm = pl.BlockSpec(memory_space=pltpu.HBM)
roomy = pltpu.CompilerParams(vmem_limit_bytes=24 * 2**20)


def body(state, tile_lists, tile_counts, ghost_counts, cell_index, fluid_vel, fluid_frac):
    particles = state.shape[3]
    cell_count = fluid_vel.shape[3]
    slab = cell_count // LANES
    tiles = state.reshape(7, NT, TILE)
    cells = cell_index.reshape(NT, TILE)
    lists = tile_lists.reshape(NT, K).T
    counts = tile_counts.reshape(NT)
    ghosts = ghost_counts.reshape(4)

    def shape(*dims):
        return jax.ShapeDtypeStruct(dims, f32)

    def held(*values):
        return [pltpu.with_memory_space_constraint(value, pltpu.HBM) for value in values]

    face = shape(8, FACE, TILE)
    paired = lax.axis_size("gz") == 4
    parts, xa, xb, ya, yb, state_vmem, cells_vmem = pl.pallas_call(
        deposit_kernel,
        out_shape=(
            shape(12, slab, LANES), face, face, face, face,
            shape(7, NT, TILE), jax.ShapeDtypeStruct((NT, TILE), jnp.int32),
        ),
        in_specs=[hbm] * 5,
        out_specs=(vmem,) * 7,
        scratch_shapes=[
            pltpu.VMEM((3, slab, LANES), f32),
            pltpu.VMEM((slab, LANES), f32),
            pltpu.VMEM((8 * NT, TILE), f32),
            pltpu.VMEM((2, 12 * slab, LANES), f32),
            pltpu.VMEM((3 * slab, LANES), f32),
            pltpu.SMEM((4,), jnp.int32),
            pltpu.SemaphoreType.DMA((5,)),
        ],
        compiler_params=roomy,
        name="deposit",
    )(*held(tiles, cells, fluid_vel.reshape(3, slab, LANES), fluid_frac.reshape(slab, LANES), ghosts))

    if paired:
        beside = lax.ppermute(parts, "gz", [(i, i ^ 1) for i in range(4)])
        slabs = (beside,)
    else:
        slabs = (
            shifted(parts[0:8], "gz", 1), shifted(parts[4:12], "gz", -1),
            shifted(parts[0:4], "gz", 2), shifted(parts[8:12], "gz", -2),
        )
    if lax.axis_size("gy") == 2:
        ya = yb = lax.ppermute(ya, "gy", [(0, 1), (1, 0)])
    else:
        ya, yb = rung(ya, yb, "gy")
    xa, xb = swapped(xa, xb, "gx", "gy")

    near, turned, value, sums, *across = pl.pallas_call(
        functools.partial(feature_kernel, paired),
        out_shape=(
            jax.ShapeDtypeStruct((NT * 128 + 128, TILE), bf16),
            jax.ShapeDtypeStruct((GHOST * NROW, TILE), bf16),
            jax.ShapeDtypeStruct((GHOST * VROW, TILE), bf16),
            shape((NT + 1) * VROW, TILE),
        ) + ((shape(8, slab, LANES),) if paired else ()),
        in_specs=[hbm] * 2 + [vmem] * (3 if paired else 1),
        out_specs=(vmem,) * (5 if paired else 4),
        scratch_shapes=[
            pltpu.VMEM((NT * NROW, TILE), f32),
            pltpu.VMEM((NT * NROW, TILE), f32),
            pltpu.VMEM((NT * VROW, TILE), f32),
            pltpu.SMEM((K, NT), jnp.int32),
            pltpu.SMEM((NT,), jnp.int32),
            pltpu.SMEM((16,), jnp.int32),
            pltpu.SemaphoreType.DMA((2,)),
        ],
        compiler_params=roomy,
        name="feature",
    )(*held(lists, counts), state_vmem, *((parts, beside) if paired else ()))
    if paired:
        slabs += (lax.ppermute(across[0], "gz", [(i, i ^ 2) for i in range(4)]),)

    sums = pl.pallas_call(
        interior_kernel,
        out_shape=shape((NT + 1) * VROW, TILE),
        in_specs=[hbm] * 3 + [vmem] * 8,
        out_specs=vmem,
        scratch_shapes=[
            pltpu.VMEM((NFAR * NROW, TILE), bf16),
            pltpu.VMEM((NFAR * VROW, TILE), bf16),
            pltpu.VMEM((4 * FACE * NROW, TILE), f32),
            pltpu.VMEM((4 * FACE * VROW, TILE), f32),
            pltpu.SMEM((K, NT), jnp.int32),
            pltpu.SMEM((NT,), jnp.int32),
            pltpu.SMEM((4,), jnp.int32),
            pltpu.SMEM((16,), jnp.int32),
            pltpu.SemaphoreType.DMA((3,)),
        ],
        compiler_params=roomy,
        name="interior",
    )(*held(lists, counts, ghosts), near, turned, value, sums, xa, xb, ya, yb)

    velocity_new, fluid_new = pl.pallas_call(
        functools.partial(update_kernel, paired),
        out_shape=(shape(3, NT, TILE), shape(3, slab, LANES)),
        in_specs=[vmem] * (4 + len(slabs)),
        out_specs=(vmem, vmem),
        scratch_shapes=[pltpu.VMEM((9 * slab, LANES), f32)],
        compiler_params=roomy,
        name="update",
    )(state_vmem, cells_vmem, sums, parts, *slabs)
    return velocity_new.reshape(3, 1, 1, particles), fluid_new.reshape(3, 1, 1, cell_count)


def solution(mesh):
    return jax.shard_map(
        body,
        mesh=mesh,
        in_specs=(
            P(None, "gx", "gy", "gz"),
            P("gx", "gy", "gz", None),
            P("gx", "gy", "gz"),
            P("gx", "gy", "gz", None),
            P("gx", "gy", "gz"),
            P(None, "gx", "gy", "gz"),
            P("gx", "gy", "gz"),
        ),
        out_specs=(P(None, "gx", "gy", "gz"), P(None, "gx", "gy", "gz")),
        check_vma=False,
    )
```

```python
import functools

import jax
import jax.numpy as jnp
from jax import lax
from jax.experimental import pallas as pl
from jax.experimental.pallas import tpu as pltpu
from jax.sharding import PartitionSpec as P

TILE = 128
K = 8
NT = 64
GB = 12
FACE = 16
LANES = 128

stiffness = 5.0
damping = 2.0
time_step = 0.25
drag_coef = 64.0
fluid_density = 2.0
radius_ref = 0.25
spring = stiffness / damping

f32 = jnp.float32
bf16 = jnp.bfloat16

NROW = 32
VROW = 16
DUMMY = NT
GHOST = NT + 4
NFAR = GHOST + 4 * FACE
SIZES = (64, 32, 16)
GROUP = 16
EARLY = (32, 8)


def parts_of(q):
    first = q.astype(bf16).astype(f32)
    rest = q - first
    second = rest.astype(bf16).astype(f32)
    return first, second, (rest - second).astype(bf16).astype(f32)


ORDER = ((0, 0), (0, 1), (0, 2), (1, 0), (1, 1), (2, 0))


def centred(position):
    return position - 0.5


def geometry(columns):
    x, y, z = (centred(columns[k]) for k in range(3))
    r = columns[6]
    return (x, y, z, r), r * r - (x * x + y * y + z * z)


def near_rows(columns):
    lengths, own = geometry(columns)
    one = jnp.ones_like(own)
    rows = []
    for q in lengths:
        cut = parts_of(q)
        rows += [2.0 * cut[j] for _, j in ORDER]
    return rows + [one] * 3 + list(parts_of(own))


def far_rows(columns):
    lengths, own = geometry(columns)
    one = jnp.ones_like(own)
    rows = []
    for q in lengths:
        cut = parts_of(q)
        rows += [cut[i] for i, _ in ORDER]
    return rows + list(parts_of(own)) + [one] * 3


def value_rows(columns, living):
    cuts = [parts_of((columns[3 + c] - spring * centred(columns[c]))) for c in range(3)]
    return [cuts[c][k] * living for k in range(3) for c in range(3)] + [living]


def load(pairs, sems):
    copies = [pltpu.make_async_copy(source, target, sems.at[k]) for k, (source, target) in enumerate(pairs)]
    for copy in copies:
        copy.start()
    return copies


def pair_sums(far, near, values):
    weight = jnp.concatenate(
        [jnp.dot(left, right, preferred_element_type=f32) for left, right in zip(far, near)], axis=0
    )
    weight = jnp.maximum(weight, 0.0)
    coarse = weight.astype(bf16)
    fine = (weight - coarse.astype(f32)).astype(bf16)
    both = jnp.dot(values, jnp.concatenate([coarse, fine], axis=1), preferred_element_type=f32)
    return both[:, :TILE] + both[:, TILE:]


def double_pair(k, d, lists_ref, counts_ref, faces_ref):
    inside = k < NT
    t = jnp.bitwise_and(k + 4 * GB, NT - 1)
    face = lax.shift_right_logical(t * 171, 11)
    place = t - face * GB
    count = counts_ref[t]
    entries = count + (place < faces_ref[face]).astype(jnp.int32)
    ghost = faces_ref[8 + face] + place
    at = 2 * d
    first = jnp.where(at < count, lists_ref[jnp.minimum(at, K - 1), t], ghost)
    second = jnp.where(
        at + 1 < count, lists_ref[jnp.minimum(at + 1, K - 1), t], jnp.where(at + 1 < entries, ghost, DUMMY)
    )
    done = at + 2 >= entries
    following = (k + done.astype(jnp.int32), jnp.where(done, 0, d + 1))
    return jnp.where(inside, t, NT), jnp.where(inside, first, DUMMY), jnp.where(inside, second, DUMMY), following


def interior_steps(steps, size, carry, tables, near_ref, turned_ref, value_ref, acc_ref):
    def near_block(t, s):
        start = t * 128 + 96 - NROW * jnp.bitwise_and(s, 3)
        return near_ref[pl.ds(pl.multiple_of(start, NROW), 128), :]

    def far_block(s):
        return turned_ref[pl.ds(pl.multiple_of(lax.shift_right_logical(s, 2) * 128, 128), 128), :]

    def value_block(s):
        return value_ref[pl.ds(pl.multiple_of(s * VROW, VROW), VROW), :]

    def step(group, carry):
        (k, d), running = carry
        sums = []
        for _ in range(size):
            t, a, b, following = double_pair(k, d, *tables)
            near = jnp.minimum(t, NT - 1)
            total = pair_sums(
                (far_block(a), far_block(b)),
                (near_block(near, a), near_block(near, b)),
                jnp.concatenate([value_block(a), value_block(b)], axis=1),
            )
            sums.append((t, d, total))
            k, d = following
        for t, at, total in sums:
            running = total + jnp.where(at > 0, running, 0.0)
            acc_ref[pl.ds(pl.multiple_of(t * VROW, VROW), VROW), :] = running
        return (k, d), running

    return lax.fori_loop(0, steps, step, carry)


def deposit_kernel(
    state_hbm, cell_hbm, vel_hbm, frac_hbm, ghost_hbm,
    parts_ref, xa_ref, xb_ref, ya_ref, yb_ref, state_ref, cell_ref,
    vel_ref, frac_ref, source_ref, deposit_ref, total_ref, ghost_ref, sems,
):
    copies = load(
        [
            (state_hbm, state_ref), (cell_hbm, cell_ref), (vel_hbm, vel_ref), (frac_hbm, frac_ref),
            (ghost_hbm, ghost_ref),
        ],
        sems,
    )
    slab = vel_ref.shape[1]
    wide = 3 * slab
    bands = wide // 2
    even_x, even_y = (jnp.bitwise_and(lax.axis_index(axis), 1) == 0 for axis in ("gx", "gy"))
    first_band = (lax.axis_index("gz") - 1) * (slab // 2)
    for copy in copies:
        copy.wait()

    r = state_ref[6]
    rate = drag_coef * r * r
    sources = [rate * state_ref[3 + c] for c in range(3)] + [rate]
    for c, source in enumerate(sources):
        for k, part in enumerate(parts_of(source)[:2]):
            source_ref[pl.ds(4 * k + c, NT, stride=8), :] = part
    low_of = lax.broadcasted_iota(jnp.int32, (2 * LANES, LANES), 0)

    def add_group(group, total):
        cells = cell_ref[pl.ds(pl.multiple_of(group * 8, 8), 8), :]
        band = lax.shift_right_logical(cells, 8) - first_band
        low = jnp.bitwise_and(cells, 255)
        left, right = [], []
        for t in range(8):
            rows = source_ref[pl.ds(pl.multiple_of(group * 64 + t * 8, 8), 8), :]
            here = jnp.broadcast_to(band[t : t + 1, :], (8, LANES))
            left.append(jnp.concatenate([jnp.where(here == h, rows, 0.0) for h in range(bands)], axis=0).astype(bf16))
            right.append(jnp.where(low[t : t + 1, :] == low_of, 1.0, 0.0).astype(bf16))
        added = lax.dot_general(
            jnp.concatenate(left, axis=1),
            jnp.concatenate(right, axis=1),
            (((1,), (1,)), ((), ())),
            preferred_element_type=f32,
        )
        deposit_ref[0] += added[:, :LANES]
        deposit_ref[1] += added[:, LANES:]
        return total

    deposit_ref[...] = jnp.zeros_like(deposit_ref)
    lax.fori_loop(0, NT // 8, add_group, 0, unroll=8)
    frac = fluid_density * frac_ref[...]
    for c in range(4):
        for k in range(2):
            both = deposit_ref[k, pl.ds(c, bands, stride=8), :] + deposit_ref[k, pl.ds(4 + c, bands, stride=8), :]
            total_ref[pl.ds(k, bands, stride=2), :] = both * time_step
        below, here, above = (total_ref[pl.ds(k * slab, slab), :] for k in range(3))
        parts_ref[c] = above
        parts_ref[4 + c] = here + (frac * vel_ref[c] if c < 3 else frac)
        parts_ref[8 + c] = below
    order = lax.broadcasted_iota(jnp.int32, (FACE, TILE), 0)
    for low, even, a_ref, b_ref in ((0, even_x, xa_ref, xb_ref), (2, even_y, ya_ref, yb_ref)):
        for k in range(7):
            lower = state_ref[k, low * GB : (low + 1) * GB, :]
            upper = state_ref[k, (low + 1) * GB : (low + 2) * GB, :]
            a_ref[k, 0:GB, :] = jnp.where(even, upper, lower)
            b_ref[k, 0:GB, :] = jnp.where(even, lower, upper)
            a_ref[k, GB:FACE, :] = jnp.zeros((FACE - GB, TILE), f32)
            b_ref[k, GB:FACE, :] = jnp.zeros((FACE - GB, TILE), f32)
        lower, upper = ghost_ref[low], ghost_ref[low + 1]
        a_ref[7] = jnp.where(order < jnp.where(even, upper, lower), 1.0, 0.0)
        b_ref[7] = jnp.where(order < jnp.where(even, lower, upper), 1.0, 0.0)

def inner_outer():
    z = lax.axis_index("gz")
    lower = z < 2
    return lower, jnp.bitwise_and(z, 1) == jnp.where(lower, 1, 0)


def put_rows(ref, first, rows, stride, filled):
    tiles = rows[0].shape[0]
    all_rows = jnp.stack(rows + [jnp.zeros_like(rows[0])] * (filled - len(rows)), axis=0)
    ref[first * stride : (first + tiles) * stride, :] = jnp.swapaxes(all_rows, 0, 1).reshape(tiles * stride, TILE)


def facing(flag, ref):
    return [jnp.where(flag, ref[c], ref[8 + c]) for c in range(4)]


def ghost_slots():
    slot_of, beside = [], []
    for axis in ("gx", "gy"):
        place, count = lax.axis_index(axis), lax.axis_size(axis)
        first = max(slot_of, default=-1) + 1
        slot_of += [first, first if count == 2 else first + 1]
        beside += [place > 0, place < count - 1]
    return slot_of, beside


def put_faces(faces_ref, ghost_ref=None):
    slot_of, beside = ghost_slots()
    for face in range(8):
        faces_ref[face] = jnp.where(beside[face], ghost_ref[face], 0) if ghost_ref is not None and face < 4 else 0
        faces_ref[8 + face] = GHOST + slot_of[face] * FACE if face < 4 else DUMMY


def early_words(without_ghosts):
    if lax.axis_size("gz") != 4:
        return jnp.int32(0)
    words = jnp.int32(0)
    for size in EARLY:
        words = words + jnp.where(without_ghosts - words >= size, size, 0)
    return jnp.where(inner_outer()[0], words, 0)


def bare_words(counts_ref):
    counts = [lax.shift_right_logical(counts_ref[t] + 1, 1) for t in range(4 * GB, NT)]
    total = sum(counts)
    early = early_words(total)
    k, d, passed = jnp.int32(0), early, jnp.int32(0)
    for place, count in enumerate(counts):
        passed = passed + count
        k = jnp.where(passed <= early, place + 1, k)
        d = jnp.where(passed <= early, early - passed, d)
    return total, early, (k, d)


def feature_kernel(paired, lists_hbm, counts_hbm, state_ref, *refs):
    if paired:
        parts_ref, beside_ref, *refs = refs
    near16_ref, turned_ref, value16_ref, acc_ref, *refs = refs
    if paired:
        across_ref, *refs = refs
    near_ref, far_ref, value_ref, lists_ref, counts_ref, faces_ref, sems = refs
    copies = load([(lists_hbm, lists_ref), (counts_hbm, counts_ref)], sems)
    if paired:
        lower, inner = inner_outer()
        mine, other = facing(lower, parts_ref), facing(lower, beside_ref)
        for c in range(4):
            across_ref[c] = jnp.where(inner, parts_ref[4 + c] + other[c], beside_ref[4 + c] + mine[c])
            across_ref[4 + c] = jnp.where(inner, mine[c], other[c])
    near16_ref[pl.ds(NT * 128, 128), :] = jnp.zeros((128, TILE), bf16)
    turned_ref[DUMMY * NROW : GHOST * NROW, :] = jnp.zeros((4 * NROW, TILE), bf16)
    value16_ref[DUMMY * VROW : GHOST * VROW, :] = jnp.zeros((4 * VROW, TILE), bf16)

    columns = [state_ref[k] for k in range(7)]
    put_rows(near_ref, 0, near_rows(columns), NROW, NROW)
    put_rows(far_ref, 0, far_rows(columns), NROW, NROW)
    put_rows(value_ref, 0, value_rows(columns, jnp.ones((NT, TILE), f32)), VROW, VROW)
    for b in range(NT // 4):
        rows = slice(b * 128, (b + 1) * 128)
        turned_ref[rows, :] = far_ref[rows, :].T.astype(bf16)
        rows = slice(b * 4 * VROW, (b + 1) * 4 * VROW)
        value16_ref[rows, :] = value_ref[rows, :].astype(bf16)
    for t in range(NT):
        near16_ref[t * 128 : (t + 1) * 128, :] = jnp.concatenate(
            [jnp.zeros((96, TILE), bf16), near_ref[t * NROW : (t + 1) * NROW, :].astype(bf16)], axis=0
        )
    for copy in copies:
        copy.wait()
    if paired:
        @pl.when(lower)
        def _():
            put_faces(faces_ref)
            _, words, _ = bare_words(counts_ref)
            carry = ((jnp.int32(0), jnp.int32(0)), jnp.zeros((VROW, TILE), f32))
            tables = (lists_ref, counts_ref, faces_ref)
            for size in EARLY:
                steps = (words >= size).astype(jnp.int32)
                carry = interior_steps(
                    steps, size, carry, tables, near16_ref, turned_ref, value16_ref, acc_ref
                )
                words = words - steps * size


def interior_kernel(
    lists_hbm, counts_hbm, ghost_hbm, near_ref, own_turned_ref, own_value_ref, before_ref,
    xa_ref, xb_ref, ya_ref, yb_ref,
    acc_ref, turned_ref, value_ref, far_ref, cut_ref, lists_ref, counts_ref, ghost_ref, faces_ref, sems,
):
    copies = load([(lists_hbm, lists_ref), (counts_hbm, counts_ref), (ghost_hbm, ghost_ref)], sems)
    slots = []
    for axis, a_ref, b_ref in (("gx", xa_ref, xb_ref), ("gy", ya_ref, yb_ref)):
        even = jnp.bitwise_and(lax.axis_index(axis), 1) == 0
        a, b = ([ref[k] for k in range(8)] for ref in (a_ref, b_ref))
        if lax.axis_size(axis) == 2:
            slots.append(a)
        else:
            slots.append([jnp.where(even, q, p) for p, q in zip(a, b)])
            slots.append([jnp.where(even, p, q) for p, q in zip(a, b)])
    columns = [jnp.concatenate([slot[k] for slot in slots], axis=0) for k in range(8)]
    put_rows(far_ref, 0, far_rows(columns), NROW, NROW)
    put_rows(cut_ref, 0, value_rows(columns, columns[7]), VROW, VROW)
    turned_ref[0 : GHOST * NROW, :] = own_turned_ref[...]
    value_ref[0 : GHOST * VROW, :] = own_value_ref[...]
    ghosts = len(slots) * FACE
    value_ref[GHOST * VROW : (GHOST + ghosts) * VROW, :] = cut_ref[0 : ghosts * VROW, :].astype(bf16)
    for b in range(ghosts // 4):
        turned_ref[GHOST * NROW + b * 128 : GHOST * NROW + (b + 1) * 128, :] = (
            far_ref[b * 128 : (b + 1) * 128, :].T.astype(bf16)
        )
    for copy in copies:
        copy.wait()
    put_faces(faces_ref, ghost_ref)
    bare, begin, place = bare_words(counts_ref)
    left = bare - begin
    for t in range(4 * GB):
        ghost = (t % GB < faces_ref[t // GB]).astype(jnp.int32)
        left = left + lax.shift_right_logical(counts_ref[t] + ghost + 1, 1)

    @pl.when(begin > 0)
    def _():
        rows = slice(4 * GB * VROW, NT * VROW)
        acc_ref[rows, :] = before_ref[rows, :]

    tile = jnp.bitwise_and(place[0] + 4 * GB, NT - 1)
    carry = (place, before_ref[pl.ds(pl.multiple_of(tile * VROW, VROW), VROW), :])
    tables = (lists_ref, counts_ref, faces_ref)
    for size in SIZES:
        steps = lax.div(left + (GROUP - 1 if size > GROUP else size - 1), size)
        carry = interior_steps(steps, size, carry, tables, near_ref, turned_ref, value_ref, acc_ref)
        left = jnp.maximum(left - steps * size, 0)


def solved(total):
    inverse = 1.0 / total[3]
    return [total[c] * inverse for c in range(3)]


def added(*terms):
    return [sum(values[1:], values[0]) for values in zip(*terms)]


def paired_slabs(parts_ref, beside_ref, across_ref):
    lower, inner = inner_outer()
    own, other = ([ref[4 + c] for c in range(4)] for ref in (parts_ref, beside_ref))
    mine_to, other_to = facing(lower, parts_ref), facing(lower, beside_ref)
    away = jnp.logical_not(lower)
    mine_from, other_from = facing(away, parts_ref), facing(away, beside_ref)
    summed, single = ([across_ref[k + c] for c in range(4)] for k in (0, 4))

    def chosen(first, second):
        return [jnp.where(inner, p, q) for p, q in zip(first, second)]

    here = solved(chosen(added(own, other_to, single), added(own, other_from)))
    near = solved(chosen(added(other, mine_from), added(other, mine_to, single)))
    past = solved(added(summed, mine_to))
    even = jnp.bitwise_and(lax.axis_index("gz"), 1) == 0
    below = [jnp.where(even, p, q) for p, q in zip(past, near)]
    above = [jnp.where(even, q, p) for p, q in zip(past, near)]
    return below, here, above


def ring_slabs(parts_ref, below_ref, above_ref, far_below_ref, far_above_ref):
    z, count = lax.axis_index("gz"), lax.axis_size("gz")

    def rows(ref, first):
        return [ref[first + c] for c in range(4)]

    def inside(flag, values, other=0.0):
        return [jnp.where(flag, value, other) for value in values]

    has_below, has_above = z >= 1, z <= count - 2
    here = added(rows(parts_ref, 4), inside(has_below, rows(below_ref, 0)), inside(has_above, rows(above_ref, 4)))
    below = added(
        inside(has_below, rows(below_ref, 4), 1.0), rows(parts_ref, 8), inside(z >= 2, rows(far_below_ref, 0))
    )
    above = added(
        inside(has_above, rows(above_ref, 0), 1.0), rows(parts_ref, 0), inside(z <= count - 3, rows(far_above_ref, 0))
    )
    return solved(below), solved(here), solved(above)


def update_kernel(paired, state_ref, cell_ref, acc_ref, parts_ref, *refs):
    slabs, refs = (refs[:2], refs[2:]) if paired else (refs[:4], refs[4:])
    new_ref, fluid_ref, table_ref = refs
    slab = parts_ref.shape[1]
    wide = 3 * slab
    first_row = (lax.axis_index("gz") - 1) * slab
    lower, here, upper = (paired_slabs if paired else ring_slabs)(parts_ref, *slabs)
    for c in range(3):
        fluid_ref[c] = here[c]
        table_ref[pl.ds(c * wide, slab), :] = lower[c]
        table_ref[pl.ds(c * wide + slab, slab), :] = here[c]
        table_ref[pl.ds(c * wide + 2 * slab, slab), :] = upper[c]

    def update_group(group, carry):
        rows = pl.ds(pl.multiple_of(group * 8, 8), 8)

        def sums(k):
            return acc_ref[pl.ds(group * 8 * VROW + k, 8, stride=VROW), :]

        weight = sums(9)
        cells = cell_ref[rows, :]
        high = lax.shift_right_logical(cells, 7) - first_row
        low = jnp.bitwise_and(cells, LANES - 1)
        at_cell = [jnp.zeros((8, LANES), f32)] * 3
        for h in range(wide):
            chosen = high == h
            for c in range(3):
                line = jnp.broadcast_to(table_ref[c * wide + h : c * wide + h + 1, :], (8, LANES))
                taken = jnp.take_along_axis(line, low, axis=1, mode="promise_in_bounds")
                at_cell[c] = jnp.where(chosen, taken, at_cell[c])
        r = state_ref[6, rows, :]
        lag = time_step * drag_coef * radius_ref**3
        push = time_step * radius_ref**3 / (r * r * r)
        share = 1.0 / (r + lag)
        for c in range(3):
            velocity = state_ref[3 + c, rows, :]
            lever = velocity - spring * centred(state_ref[c, rows, :])
            force = -damping * (lever * weight - (sums(c) + sums(3 + c) + sums(6 + c)))
            moved = velocity + push * force
            new_ref[c, rows, :] = (r * moved + lag * at_cell[c]) * share
        return carry

    lax.fori_loop(0, NT // 8, update_group, 0, unroll=8)


def shifted(value, axis, steps):
    count = lax.axis_size(axis)
    return lax.ppermute(value, axis, [(i, (i + steps) % count) for i in range(count)])


def rung(first, second, axis):
    count = lax.axis_size(axis)
    first = lax.ppermute(first, axis, [(i, i ^ 1) for i in range(count)])
    return first, lax.ppermute(second, axis, [(i, (i + (1 if i % 2 else -1)) % count) for i in range(count)])


def swapped(first, second, axis, core):
    count = lax.axis_size(axis)
    first = lax.ppermute(first, axis, [(i, i ^ 1) for i in range(count)])
    cores = lax.axis_size(core)
    pairs = []
    for i in range(count):
        partner = i + 1 if i % 2 else i - 1
        for c in range(cores):
            to = (partner, c) if 0 <= partner < count else (i, c ^ 1)
            pairs.append((i * cores + c, to[0] * cores + to[1]))
    return first, lax.ppermute(second, (axis, core), pairs)


vmem = pl.BlockSpec(memory_space=pltpu.VMEM)
hbm = pl.BlockSpec(memory_space=pltpu.HBM)
roomy = pltpu.CompilerParams(vmem_limit_bytes=24 * 2**20)


def body(state, tile_lists, tile_counts, ghost_counts, cell_index, fluid_vel, fluid_frac):
    particles = state.shape[3]
    cell_count = fluid_vel.shape[3]
    slab = cell_count // LANES
    tiles = state.reshape(7, NT, TILE)
    cells = cell_index.reshape(NT, TILE)
    lists = tile_lists.reshape(NT, K).T
    counts = tile_counts.reshape(NT)
    ghosts = ghost_counts.reshape(4)

    def shape(*dims):
        return jax.ShapeDtypeStruct(dims, f32)

    def held(*values):
        return [pltpu.with_memory_space_constraint(value, pltpu.HBM) for value in values]

    face = shape(8, FACE, TILE)
    paired = lax.axis_size("gz") == 4
    parts, xa, xb, ya, yb, state_vmem, cells_vmem = pl.pallas_call(
        deposit_kernel,
        out_shape=(
            shape(12, slab, LANES), face, face, face, face,
            shape(7, NT, TILE), jax.ShapeDtypeStruct((NT, TILE), jnp.int32),
        ),
        in_specs=[hbm] * 5,
        out_specs=(vmem,) * 7,
        scratch_shapes=[
            pltpu.VMEM((3, slab, LANES), f32),
            pltpu.VMEM((slab, LANES), f32),
            pltpu.VMEM((8 * NT, TILE), f32),
            pltpu.VMEM((2, 12 * slab, LANES), f32),
            pltpu.VMEM((3 * slab, LANES), f32),
            pltpu.SMEM((4,), jnp.int32),
            pltpu.SemaphoreType.DMA((5,)),
        ],
        compiler_params=roomy,
        name="deposit",
    )(*held(tiles, cells, fluid_vel.reshape(3, slab, LANES), fluid_frac.reshape(slab, LANES), ghosts))

    if paired:
        beside = lax.ppermute(parts, "gz", [(i, i ^ 1) for i in range(4)])
        slabs = (beside,)
    else:
        slabs = (
            shifted(parts[0:8], "gz", 1), shifted(parts[4:12], "gz", -1),
            shifted(parts[0:4], "gz", 2), shifted(parts[8:12], "gz", -2),
        )
    if lax.axis_size("gy") == 2:
        ya = yb = lax.ppermute(ya, "gy", [(0, 1), (1, 0)])
    else:
        ya, yb = rung(ya, yb, "gy")
    xa, xb = swapped(xa, xb, "gx", "gy")

    near, turned, value, sums, *across = pl.pallas_call(
        functools.partial(feature_kernel, paired),
        out_shape=(
            jax.ShapeDtypeStruct((NT * 128 + 128, TILE), bf16),
            jax.ShapeDtypeStruct((GHOST * NROW, TILE), bf16),
            jax.ShapeDtypeStruct((GHOST * VROW, TILE), bf16),
            shape((NT + 1) * VROW, TILE),
        ) + ((shape(8, slab, LANES),) if paired else ()),
        in_specs=[hbm] * 2 + [vmem] * (3 if paired else 1),
        out_specs=(vmem,) * (5 if paired else 4),
        scratch_shapes=[
            pltpu.VMEM((NT * NROW, TILE), f32),
            pltpu.VMEM((NT * NROW, TILE), f32),
            pltpu.VMEM((NT * VROW, TILE), f32),
            pltpu.SMEM((K, NT), jnp.int32),
            pltpu.SMEM((NT,), jnp.int32),
            pltpu.SMEM((16,), jnp.int32),
            pltpu.SemaphoreType.DMA((2,)),
        ],
        compiler_params=roomy,
        name="feature",
    )(*held(lists, counts), state_vmem, *((parts, beside) if paired else ()))
    if paired:
        slabs += (lax.ppermute(across[0], "gz", [(i, i ^ 2) for i in range(4)]),)

    sums = pl.pallas_call(
        interior_kernel,
        out_shape=shape((NT + 1) * VROW, TILE),
        in_specs=[hbm] * 3 + [vmem] * 8,
        out_specs=vmem,
        scratch_shapes=[
            pltpu.VMEM((NFAR * NROW, TILE), bf16),
            pltpu.VMEM((NFAR * VROW, TILE), bf16),
            pltpu.VMEM((4 * FACE * NROW, TILE), f32),
            pltpu.VMEM((4 * FACE * VROW, TILE), f32),
            pltpu.SMEM((K, NT), jnp.int32),
            pltpu.SMEM((NT,), jnp.int32),
            pltpu.SMEM((4,), jnp.int32),
            pltpu.SMEM((16,), jnp.int32),
            pltpu.SemaphoreType.DMA((3,)),
        ],
        compiler_params=roomy,
        name="interior",
    )(*held(lists, counts, ghosts), near, turned, value, sums, xa, xb, ya, yb)

    velocity_new, fluid_new = pl.pallas_call(
        functools.partial(update_kernel, paired),
        out_shape=(shape(3, NT, TILE), shape(3, slab, LANES)),
        in_specs=[vmem] * (4 + len(slabs)),
        out_specs=(vmem, vmem),
        scratch_shapes=[pltpu.VMEM((9 * slab, LANES), f32)],
        compiler_params=roomy,
        name="update",
    )(state_vmem, cells_vmem, sums, parts, *slabs)
    return velocity_new.reshape(3, 1, 1, particles), fluid_new.reshape(3, 1, 1, cell_count)


def solution(mesh):
    return jax.shard_map(
        body,
        mesh=mesh,
        in_specs=(
            P(None, "gx", "gy", "gz"),
            P("gx", "gy", "gz", None),
            P("gx", "gy", "gz"),
            P("gx", "gy", "gz", None),
            P("gx", "gy", "gz"),
            P(None, "gx", "gy", "gz"),
            P("gx", "gy", "gz"),
        ),
        out_specs=(P(None, "gx", "gy", "gz"), P(None, "gx", "gy", "gz")),
        check_vma=False,
    )
```
